256 devices in a mesh: wide: 64 (over y, z_hi, x), narrow: 4 (over z_lo, core).
Axes of the slice: x: 4, y: 4, z: 8 (z_hi: 4, z_lo: 2; z = z_hi * 2 + z_lo), core: 2. Of those that a mesh axis runs over, the one named last changes fastest.
Arguments:
- charges: float32 [2, 64, 65536], P(None, None, ('wide', 'narrow')), may hold values from -6 to 6
- projection: float32 [64, 64], replicated, may hold values from -0.75 to 0.75
- green_hat: float32 [2, 256, 512, 512], P(None, ('wide', 'narrow')), may hold values from -6 to 6
- near_table: float32 [27, 2, 64, 64], replicated, may hold values from -0.109375 to 0.109375
- block_site: int32 [65536], P(('wide', 'narrow')), may hold values from 0 to 511, as said below
- block_count: int32 [256], P(('wide', 'narrow')), may hold values from 128 to 256, as said below
- near_source: int32 [27, 65536], P(None, ('wide', 'narrow')), may hold values from 0 to 2303
Outputs:
- result: float32 [2, 64, 65536], P(None, None, ('wide', 'narrow'))
The draws below stay inside these ranges and needn't reach their ends.
Inputs may be any that keep to these rules, and one draw needn't show every extreme that they name: `block_count`: slots at or beyond a device's count hold no block; at least one device has all 256 slots occupied. `block_site`: distinct among the slots of one device.
All inputs are finite; a program needn't handle non-finite values.
Results may differ from the reference program's by a relative error of at most 0.0003.
Values sent between devices are 32-bit elements; how exact they have to be, the bound alone decides.
No kernel may reach another device: no remote copies, remote signals or barrier semaphores. Data moves between devices by JAX's collectives and lax.ppermute only.
A program may use at most 128 MiB of HBM per device.

```python
import jax
import jax.numpy as jnp
from jax import lax

PX = 4
PY = 64
PZ = 128
CELLS = 64
CLASSES = 27
BLOCK_SLOTS = 256
RANKS = 256
BLOCKS = 65536
GX = 512
GY = 512
GZ = 256
N_WIDE = 64
N_NARROW = 4


def draw_block_site(key, part):
    key = jax.random.fold_in(key, 11)
    device_keys = jax.random.split(key, RANKS)
    lattice = PX // 4 * (PY // 4) * (PZ // 4)

    def choose_sites(single):
        return jax.random.permutation(single, lattice)[:BLOCK_SLOTS]
    chosen = jax.vmap(choose_sites)(device_keys)
    return chosen.reshape(RANKS * BLOCK_SLOTS).astype(jnp.int32)


def draw_block_count(key, part):
    key = jax.random.fold_in(key, 23)
    count_key, full_key = jax.random.split(key)
    counts = jax.random.randint(count_key, (RANKS,), BLOCK_SLOTS // 2, BLOCK_SLOTS + 1)
    fullest = jax.random.randint(full_key, (), 0, RANKS)
    return jnp.where(jnp.arange(RANKS) == fullest, BLOCK_SLOTS, counts).astype(jnp.int32)


def set_ends(drawn, own_key, smallest, largest):
    shape = drawn.shape
    place = [jax.random.randint(jax.random.fold_in(own_key, axis), (), 0, shape[axis]) for axis in range(len(shape))]
    drawn = drawn.at[tuple(place)].set(smallest)
    longest = shape.index(max(shape))
    place[longest] = (place[longest] + 1) % shape[longest]
    return drawn.at[tuple(place)].set(largest)


def block_scale(own_key, shape, shards, least, high):
    factor_of, own = 1.0, jax.random.fold_in(own_key, 6)
    for dim, parts in shards:
        draws = jnp.exp(jax.random.uniform(jax.random.fold_in(own, dim), (parts,), jnp.float32, least / len(shards), high / len(shards)))
        factor_of = factor_of * jnp.repeat(draws, shape[dim] // parts).reshape([-1 if axis == dim else 1 for axis in range(len(shape))])
    return factor_of


def gaussian(stream_key, extent, scale, most, pieces=(), kind=jnp.bfloat16):
    drawn = jax.random.normal(stream_key, extent, jnp.float32) * scale
    if len(pieces) > 0:
        drawn = block_scale(stream_key, extent, pieces, -0.22, 0.18) * drawn
    return jnp.clip(drawn, min=-most, max=most).astype(kind)


def setup_inputs(seed: int = 0) -> dict:
    seeds = jax.random.split(jax.random.key(seed), 8)
    return {
        "charges": gaussian(seeds[0], (2, CELLS, BLOCKS), 1.0, 6.0, ((2, 256),), jnp.float32),
        "projection": gaussian(seeds[1], (CELLS, CELLS), CELLS ** -0.5, 0.75, (), jnp.float32),
        "green_hat": gaussian(seeds[2], (2, GZ, GX, GY), 1.0, 6.0, ((1, 256),), jnp.float32),
        "near_table": gaussian(seeds[3], (CLASSES, 2, CELLS, CELLS), (2 * CLASSES * CELLS) ** -0.5, 0.109375, (), jnp.float32),
        "block_site": draw_block_site(jax.random.fold_in(seeds[7], 71), 0),
        "block_count": draw_block_count(jax.random.fold_in(seeds[7], 71), 0),
        "near_source": set_ends(jax.random.randint(seeds[6], (CLASSES, BLOCKS), 0, 9 * BLOCK_SLOTS), jax.random.fold_in(seeds[6], 1), 0, (9 * BLOCK_SLOTS) - 1).astype(jnp.int32),
    }


EXACT = lax.Precision.HIGHEST


def reference(charges, projection, green_hat, near_table, block_site, block_count, near_source):
    span_x = PX // 4
    span_y = PY // 4
    span_z = PZ // 4
    lattice = span_x * span_y * span_z
    owners = jnp.arange(BLOCKS, dtype=jnp.int32) // BLOCK_SLOTS
    slot_index = jnp.arange(BLOCKS, dtype=jnp.int32) % BLOCK_SLOTS
    occupied = (slot_index < block_count[owners]).astype(jnp.float32)
    masked = charges * occupied
    stencil = jnp.einsum('gc,rcb->rgb', projection, masked, precision=EXACT, preferred_element_type=jnp.float32)
    position = owners * lattice + block_site
    placed = jnp.zeros((2, CELLS, RANKS * lattice), jnp.float32).at[:, :, position].add(stencil)
    grid_field = placed.reshape(2, 4, 4, 4, N_WIDE, N_NARROW, span_x, span_y, span_z)
    grid_field = grid_field.transpose(0, 4, 6, 1, 5, 7, 2, 8, 3).reshape(2, GX // 2, GY // 2, PZ)
    widths = ((0, GX // 2), (0, GY // 2), (0, GZ - PZ))
    complex_grid = jnp.pad(grid_field[0], widths) + 1j * jnp.pad(grid_field[1], widths)
    spectrum = jnp.fft.fftn(complex_grid)
    kernel = (green_hat[0] + 1j * green_hat[1]).transpose(1, 2, 0)
    potential = jnp.fft.ifftn(spectrum * kernel)[: GX // 2, : GY // 2, :PZ]
    values = jnp.stack([jnp.real(potential), jnp.imag(potential)])
    blocks = values.reshape(2, N_WIDE, span_x, 4, N_NARROW, span_y, 4, span_z, 4)
    blocks = blocks.transpose(0, 3, 6, 8, 1, 4, 2, 5, 7).reshape(2, CELLS, RANKS * lattice)
    gathered = blocks[:, :, position] * occupied
    far_field = jnp.einsum('gc,rgb->rcb', projection, gathered, precision=EXACT, preferred_element_type=jnp.float32)
    padded_cube = jnp.pad(masked.reshape(2, CELLS, N_WIDE, N_NARROW, BLOCK_SLOTS), ((0, 0), (0, 0), (1, 1), (1, 1), (0, 0)))
    padded_cube = padded_cube.reshape(2, CELLS, (N_WIDE + 2) * (N_NARROW + 2) * BLOCK_SLOTS)
    wide_pos = owners // N_NARROW
    narrow_pos = owners % N_NARROW

    def one_class(running, inputs):
        matrix, source = inputs
        step_wide = source // (3 * BLOCK_SLOTS)
        step_narrow = (source // BLOCK_SLOTS) % 3
        slot_pick = source % BLOCK_SLOTS
        flat_index = ((wide_pos + step_wide) * (N_NARROW + 2) + narrow_pos + step_narrow) * BLOCK_SLOTS + slot_pick
        picked = padded_cube[:, :, flat_index]
        real_part = jnp.dot(matrix[0], picked[0], precision=EXACT, preferred_element_type=jnp.float32) - jnp.dot(matrix[1], picked[1], precision=EXACT, preferred_element_type=jnp.float32)
        imag_part = jnp.dot(matrix[0], picked[1], precision=EXACT, preferred_element_type=jnp.float32) + jnp.dot(matrix[1], picked[0], precision=EXACT, preferred_element_type=jnp.float32)
        return running + jnp.stack([real_part, imag_part]), None

    near_field, _ = lax.scan(one_class, jnp.zeros((2, CELLS, BLOCKS), jnp.float32), (near_table, near_source))
    return far_field + near_field * occupied
```

```python
import numpy as np

import jax
import jax.numpy as jnp
from jax import lax
from jax.experimental import pallas as pl
from jax.experimental.pallas import tpu as pltpu
from jax.sharding import PartitionSpec as P

W = 64
N = 4
F32 = jnp.float32
BF16 = jnp.bfloat16
VMEM = pltpu.VMEM
BOTH = ("wide", "narrow")


def halves(table):
    high = table.astype(jnp.bfloat16)
    low = (table - high.astype(np.float64)).astype(jnp.bfloat16)
    return high, low


def split(value):
    high = value.astype(BF16)
    return high, (value - high.astype(F32)).astype(BF16)


def dot(left, right):
    return lax.dot_general(left, right, (((1,), (0,)), ((), ())), preferred_element_type=F32)


def dot_t(left, right):
    return lax.dot_general(left, right, (((1,), (1,)), ((), ())), preferred_element_type=F32)


def dot3(lh, ll, rh, rl):
    return dot(lh, rh) + (dot(lh, rl) + dot(ll, rh))


def tables():
    z = np.arange(128)
    z_of = 4 * (z % 32) + z // 32
    kz = np.arange(256)
    ang = 2 * np.pi * ((kz[:, None] * z_of[None, :]) % 256) / 256
    forward_z = np.concatenate([np.cos(ang), np.sin(ang)], 1)
    inverse_z = np.concatenate([np.cos(ang).T, -np.sin(ang).T], 1) * 2.0**-26
    lane = np.arange(2048)
    group, inner = lane // 128, lane % 128
    ez, ex = group // 4, group % 4
    r, ey = inner // 64, inner // 16 % 4
    row = r * 64 + 16 * ex + 4 * ey + ez
    expand = (np.arange(128)[:, None] == row[None, :]).astype(np.float32)
    k = np.arange(512)
    col = np.arange(512)
    n, rr, q = col // 128, col // 64 % 2, col % 64
    y = 64 * n + 4 * (q % 16) + q // 16
    ang = 2 * np.pi * ((y[:, None] * k[None, :]) % 512) / 512
    c, s = np.cos(ang), np.sin(ang)
    real = rr[:, None] == 0
    along = np.concatenate([np.where(real, c, s), np.where(real, -s, c)], 1)
    xi = np.arange(256)
    x = 4 * (xi % 64) + xi // 64
    ang = 2 * np.pi * ((k[:, None] * x[None, :]) % 512) / 512
    c, s = np.cos(ang), np.sin(ang)
    across = np.block([[c, s], [-s, c]])
    return forward_z, inverse_z, expand, along, across


def swap(value):
    lanes = value.shape[1]
    rolled = jnp.concatenate(
        [pltpu.roll(value[:, i : i + 128], 64, 1) for i in range(0, lanes, 128)], axis=1
    )
    sign = jnp.where(lax.broadcasted_iota(jnp.int32, (1, lanes), 1) % 128 < 64, 1.0, -1.0)
    return rolled * sign


def site_masks(count, site):
    rows = lax.broadcasted_iota(jnp.int32, (32, 256), 0)
    line = jnp.where(rows == site % 32, 1.0, 0.0)
    lanes = lax.broadcasted_iota(jnp.int32, (128, 256), 0)
    slots = lax.broadcasted_iota(jnp.int32, (128, 256), 1)
    plane = jnp.where((lanes % 16 == site // 32) & (slots < count), 1.0, 0.0)
    return line, plane.T


def to_grid(count_ref, site_ref, charges_ref, proj_ref, expand_ref, fh_ref, fl_ref, masked_ref, out_ref):
    count = count_ref[0]
    line, plane = site_masks(count, site_ref[...])
    slots = lax.broadcasted_iota(jnp.int32, (128, 256), 1)
    masked = jnp.where(slots < count, charges_ref[...], 0.0)
    turned = masked.T
    masked_ref[...] = turned
    ph, plo = split(proj_ref[...])
    parts = []
    for r in range(2):
        mh, ml = split(turned[:, 64 * r : 64 * r + 64])
        parts.append(dot_t(mh, ph) + (dot_t(mh, plo) + dot_t(ml, ph)))
    stencil = jnp.concatenate(parts, axis=1)
    sh, sl = split(stencil)
    line = line.astype(BF16)
    rows = []
    for ez in range(4):
        cols = []
        for ex in range(4):
            lo = (ez * 4 + ex) * 128
            e = expand_ref[:, lo : lo + 128]
            high = (dot(sh, e) * plane).astype(BF16)
            low = (dot(sl, e) * plane).astype(BF16)
            cols.append(dot(line, high) + dot(line, low))
        rows.append(jnp.concatenate(cols, axis=1))
    grid = jnp.concatenate(rows, axis=0)
    gh, gl = split(jnp.concatenate([grid, swap(grid)], axis=0))
    for ex in range(4):
        c = slice(128 * ex, 128 * ex + 128)
        out_ref[pl.ds(ex, 256, stride=4), :] = dot3(fh_ref[...], fl_ref[...], gh[:, c], gl[:, c])


def convolve(in_ref, green_ref, yh_ref, yl_ref, xh_ref, xl_ref, ih_ref, il_ref, out_ref,
             dh, dl, sh, sl, ph, plo, uh, ul):
    for n in range(4):
        for ex in range(4):
            h, l = split(in_ref[pl.ds(n * 4 + ex, 64, stride=16), :])
            dh[64 * ex : 64 * ex + 64, 128 * n : 128 * n + 128] = h
            dl[64 * ex : 64 * ex + 64, 128 * n : 128 * n + 128] = l
    for j in range(4):
        c = slice(256 * j, 256 * j + 256)
        h, l = split(dot3(dh[...], dl[...], yh_ref[:, c], yl_ref[:, c]))
        r, o = j // 2, 256 * (j % 2)
        sh[256 * r : 256 * r + 256, o : o + 256] = h
        sl[256 * r : 256 * r + 256, o : o + 256] = l
    for j in range(2):
        c = slice(256 * j, 256 * j + 256)
        for i in range(2):
            a = slice(256 * i, 256 * i + 256)
            b = slice(512 + 256 * i, 768 + 256 * i)
            re = dot3(xh_ref[a, :], xl_ref[a, :], sh[:, c], sl[:, c])
            im = dot3(xh_ref[b, :], xl_ref[b, :], sh[:, c], sl[:, c])
            gr, gi = green_ref[0, a, c], green_ref[1, a, c]
            h, l = split(gr * re - gi * im)
            ph[a, c] = h
            plo[a, c] = l
            h, l = split(gr * im + gi * re)
            ph[b, c] = h
            plo[b, c] = l
        for r in range(2):
            a = slice(256 * r, 256 * r + 256)
            h, l = split(dot3(ih_ref[a, :], il_ref[a, :], ph[:, c], plo[:, c]))
            o = slice(512 * r + 256 * j, 512 * r + 256 * j + 256)
            uh[:, o] = h
            ul[:, o] = l
    for j in range(2):
        a = slice(256 * j, 256 * j + 256)
        v = dot_t(uh[...], yh_ref[a, :]) + (dot_t(uh[...], yl_ref[a, :]) + dot_t(ul[...], yh_ref[a, :]))
        for m in range(2):
            n = 2 * j + m
            for ex in range(4):
                out_ref[pl.ds(n * 4 + ex, 64, stride=16), :] = v[64 * ex : 64 * ex + 64, 128 * m : 128 * m + 128]


def from_grid(count_ref, site_ref, in_ref, proj_ref, expand_ref, fh_ref, fl_ref, near_ref, out_ref):
    count = count_ref[0]
    line, plane = site_masks(count, site_ref[...])
    field = jnp.concatenate([in_ref[pl.ds(ex, 256, stride=4), :] for ex in range(4)], axis=1)
    vh, vl = split(jnp.concatenate([field, swap(field)], axis=0))
    points = dot3(fh_ref[...], fl_ref[...], vh, vl)
    bh, bl = split(points)
    pick = line.T.astype(BF16)
    total = jnp.zeros((256, 128), F32)
    for ez in range(4):
        rows = slice(32 * ez, 32 * ez + 32)
        for ex in range(4):
            c = slice(128 * ex, 128 * ex + 128)
            high = (dot(pick, bh[rows, c]) * plane).astype(BF16)
            low = (dot(pick, bl[rows, c]) * plane).astype(BF16)
            lo = (ez * 4 + ex) * 128
            e = expand_ref[:, lo : lo + 128]
            total = total + (dot_t(high, e) + dot_t(low, e))
    th, tl = split(total)
    ph, plo = split(proj_ref[...])
    parts = []
    for r in range(2):
        c = slice(64 * r, 64 * r + 64)
        parts.append(dot3(th[:, c], tl[:, c], ph, plo))
    far = jnp.concatenate(parts, axis=1).T
    slots = lax.broadcasted_iota(jnp.int32, (128, 256), 1)
    out_ref[...] = far + jnp.where(slots < count, near_ref[...], 0.0)


CLASSES = 27


def near(index_ref, source_ref, table_ref, out_ref, picked):
    def one(k, carry):
        for b in range(256):
            i = index_ref[k * 256 + b]
            picked[k, pl.ds(b, 1), :] = source_ref[pl.ds(i, 1), :]
        return carry

    lax.fori_loop(0, CLASSES, one, 0)
    total = jnp.zeros((256, 128), F32)
    for k in range(CLASSES):
        gh, gl = split(picked[k])
        th, tl = split(table_ref[k])
        total = total + (dot(gh, th) + (dot(gh, tl) + dot(gl, th)))
    out_ref[...] = total.T


def call(kernel, outs, args, smem, scratch=(), flops=0, bytes_accessed=0, name=None):
    specs = [pl.BlockSpec(memory_space=pltpu.SMEM if i in smem else VMEM) for i in range(len(args))]
    single = not isinstance(outs, (tuple, list))
    return pl.pallas_call(
        kernel,
        out_shape=outs,
        in_specs=specs,
        out_specs=pl.BlockSpec(memory_space=VMEM) if single else tuple(pl.BlockSpec(memory_space=VMEM) for _ in outs),
        scratch_shapes=list(scratch),
        compiler_params=pltpu.CompilerParams(vmem_limit_bytes=40 << 20),
        cost_estimate=pl.CostEstimate(flops=flops, bytes_accessed=bytes_accessed, transcendentals=0),
        name=name,
    )(*args)


def neighbours(array, axis, size):
    up = [(i, i + 1) for i in range(size - 1)]
    down = [(i + 1, i) for i in range(size - 1)]
    return lax.ppermute(array, axis, up), lax.ppermute(array, axis, down)


def per_device(charges, projection, green_hat, near_table, block_site, block_count, near_source):
    forward_z, inverse_z, expand, along, across = tables()
    fzh, fzl = halves(forward_z)
    izh, izl = halves(inverse_z)
    yh, yl = halves(along)
    xh, xl = halves(across)
    ih, il = halves(np.ascontiguousarray(across.T))
    expand = expand.astype(jnp.bfloat16)
    site = block_site.reshape(1, 256)
    shape = lambda *s: jax.ShapeDtypeStruct(s, F32)

    masked, sent = call(
        to_grid, (shape(256, 128), shape(1024, 128)),
        (block_count, site, charges.reshape(128, 256), projection, expand, fzh, fzl), (0,),
        flops=2 * 10**9, bytes_accessed=2 << 20, name="to_grid",
    )
    before, after = neighbours(masked, "wide", W)
    own = jnp.concatenate([before, masked, after], axis=0)
    planes = lax.all_to_all(sent.reshape(256, 4, 128), BOTH, split_axis=0, concat_axis=0, tiled=True)
    left, right = neighbours(own, "narrow", N)
    back = call(
        convolve, shape(1024, 128),
        (planes.reshape(1024, 128), green_hat.reshape(2, 512, 512), yh, yl, xh, xl, ih, il), (),
        scratch=[VMEM((256, 512), BF16)] * 2 + [VMEM((512, 512), BF16)] * 2
        + [VMEM((1024, 512), BF16)] * 2 + [VMEM((256, 1024), BF16)] * 2,
        flops=5 * 10**9, bytes_accessed=9 << 20, name="convolve",
    )
    field = lax.all_to_all(back.reshape(256, 4, 128), BOTH, split_axis=0, concat_axis=0, tiled=True)
    source = jnp.stack([left.reshape(3, 256, 128), own.reshape(3, 256, 128), right.reshape(3, 256, 128)], axis=1)
    turned = near_table.transpose(0, 1, 3, 2)
    table = jnp.concatenate(
        [
            jnp.concatenate([turned[:, 0], turned[:, 1]], axis=2),
            jnp.concatenate([-turned[:, 1], turned[:, 0]], axis=2),
        ],
        axis=1,
    )
    beside = call(
        near, shape(128, 256),
        (near_source.reshape(CLASSES * 256), source.reshape(2304, 128), table), (0,),
        scratch=[VMEM((CLASSES, 256, 128), F32)],
        flops=10**10, bytes_accessed=40 << 20, name="near",
    )
    result = call(
        from_grid, shape(128, 256),
        (block_count, site, field.reshape(1024, 128), projection, expand, izh, izl, beside), (0,),
        flops=2 * 10**9, bytes_accessed=2 << 20, name="from_grid",
    )
    return result.reshape(2, 64, 256)


def solution(mesh):
    placed = (
        P(None, None, BOTH),
        P(),
        P(None, BOTH, None, None),
        P(),
        P(BOTH),
        P(BOTH),
        P(None, BOTH),
    )
    return jax.shard_map(
        per_device,
        mesh=mesh,
        in_specs=placed,
        out_specs=P(None, None, BOTH),
        check_vma=False,
    )
```

```python
import numpy as np

import jax
import jax.numpy as jnp
from jax import lax
from jax.experimental import pallas as pl
from jax.experimental.pallas import tpu as pltpu
from jax.sharding import PartitionSpec as P

W = 64
N = 4
F32 = jnp.float32
BF16 = jnp.bfloat16
VMEM = pltpu.VMEM
BOTH = ("wide", "narrow")


def halves(table):
    high = table.astype(jnp.bfloat16)
    low = (table - high.astype(np.float64)).astype(jnp.bfloat16)
    return high, low


def split(value):
    high = value.astype(BF16)
    return high, (value - high.astype(F32)).astype(BF16)


def dot(left, right):
    return lax.dot_general(left, right, (((1,), (0,)), ((), ())), preferred_element_type=F32)


def dot_t(left, right):
    return lax.dot_general(left, right, (((1,), (1,)), ((), ())), preferred_element_type=F32)


def dot3(lh, ll, rh, rl):
    return dot(lh, rh) + (dot(lh, rl) + dot(ll, rh))


def tables():
    z = np.arange(128)
    z_of = 4 * (z % 32) + z // 32
    kz = np.arange(256)
    ang = 2 * np.pi * ((kz[:, None] * z_of[None, :]) % 256) / 256
    forward_z = np.concatenate([np.cos(ang), np.sin(ang)], 1)
    inverse_z = np.concatenate([np.cos(ang).T, -np.sin(ang).T], 1) * 2.0**-26
    lane = np.arange(2048)
    group, inner = lane // 128, lane % 128
    ez, ex = group // 4, group % 4
    r, ey = inner // 64, inner // 16 % 2 * 2 + inner // 32 % 2
    row = r * 64 + 16 * ex + 4 * ey + ez
    expand = (np.arange(128)[:, None] == row[None, :]).astype(np.float32)
    k = np.arange(256)
    i = np.arange(256)
    real = (i // 64 % 2 == 0)[:, None]
    along = []
    for p in range(2):
        y = 64 * (i // 128 * 2 + i // 32 % 2) + 4 * (i % 16) + 2 * (i // 16 % 2) + p
        ang = 2 * np.pi * ((y[:, None] * k[None, :]) % 512) / 512
        c, s = np.cos(ang), np.sin(ang)
        along.append(np.concatenate([np.where(real, c, s), np.where(real, -s, c)], 1))
    across = []
    j = np.arange(128)
    for p in range(2):
        x = 4 * (j % 64) + 2 * (j // 64) + p
        ang = 2 * np.pi * ((k[:, None] * x[None, :]) % 512) / 512
        c, s = np.cos(ang), np.sin(ang)
        across.append(np.block([[c, s], [-s, c]]))
    return forward_z, inverse_z, expand, np.stack(along), np.stack(across)


def swap(value):
    lanes = value.shape[1]
    rolled = jnp.concatenate(
        [pltpu.roll(value[:, i : i + 128], 64, 1) for i in range(0, lanes, 128)], axis=1
    )
    sign = jnp.where(lax.broadcasted_iota(jnp.int32, (1, lanes), 1) % 128 < 64, 1.0, -1.0)
    return rolled * sign


def site_masks(count, site):
    rows = lax.broadcasted_iota(jnp.int32, (32, 256), 0)
    line = jnp.where(rows == site % 32, 1.0, 0.0)
    lanes = lax.broadcasted_iota(jnp.int32, (128, 256), 0)
    slots = lax.broadcasted_iota(jnp.int32, (128, 256), 1)
    plane = jnp.where((lanes % 16 == site // 32) & (slots < count), 1.0, 0.0)
    return line, plane.T


def fetch(pairs, sems):
    copies = [pltpu.make_async_copy(s, d, sems.at[i]) for i, (s, d) in enumerate(pairs)]
    for copy in copies:
        copy.start()
    return copies


def to_grid(count_ref, charges_any, site_any, proj_any, expand_any, fh_any, fl_any, out_ref,
            charges_ref, site_ref, proj_ref, expand_ref, fh_ref, fl_ref, sems):
    copies = fetch(
        [(charges_any, charges_ref), (proj_any, proj_ref), (site_any, site_ref),
         (expand_any, expand_ref), (fh_any, fh_ref), (fl_any, fl_ref)], sems)
    count = count_ref[0]
    slots = lax.broadcasted_iota(jnp.int32, (128, 256), 1)
    for copy in copies[:3]:
        copy.wait()
    line, plane = site_masks(count, site_ref[...])
    turned = jnp.where(slots < count, charges_ref[...], 0.0).T
    ph, plo = split(proj_ref[...])
    parts = []
    for r in range(2):
        mh, ml = split(turned[:, 64 * r : 64 * r + 64])
        parts.append(dot_t(mh, ph) + (dot_t(mh, plo) + dot_t(ml, ph)))
    both = jnp.concatenate(split(jnp.concatenate(parts, axis=1)), axis=0)
    plane = jnp.concatenate([plane, plane], axis=1)
    line = line.astype(BF16)
    line = jnp.concatenate([line, line], axis=1)
    copies[3].wait()
    rows = []
    for ez in range(4):
        cols = []
        for e in range(2):
            lo = (ez * 4 + 2 * e) * 128
            spread = dot(both, expand_ref[:, lo : lo + 256])
            high = (spread[:256] * plane).astype(BF16)
            low = (spread[256:] * plane).astype(BF16)
            cols.append(dot(line, jnp.concatenate([high, low], axis=0)))
        rows.append(jnp.concatenate(cols, axis=1))
    grid = jnp.concatenate(rows, axis=0)
    gh, gl = split(jnp.concatenate([grid, swap(grid)], axis=0))
    copies[4].wait()
    copies[5].wait()
    for e in range(2):
        c = slice(256 * e, 256 * e + 256)
        planes = dot3(fh_ref[...], fl_ref[...], gh[:, c], gl[:, c])
        out_ref[pl.ds(2 * e, 256, stride=4), :] = planes[:, :128]
        out_ref[pl.ds(2 * e + 1, 256, stride=4), :] = planes[:, 128:]


def turn(count_ref, charges_ref, after_any, out_ref):
    slots = lax.broadcasted_iota(jnp.int32, (128, 256), 1)
    out_ref[...] = jnp.where(slots < count_ref[0], charges_ref[...], 0.0).T


def join(a_any, b_any, c_any, out_any, sems):
    copies = fetch([(r, out_any.at[pl.ds(256 * i, 256), :]) for i, r in enumerate((a_any, b_any, c_any))], sems)
    for copy in copies:
        copy.wait()


def convolve(in_any, green_any, yh_any, yl_any, xh_any, xl_any, ih_any, il_any, after_any, out_ref,
             in_ref, green_ref, yh, yl, xh, xl, ih, il, ah, al, sh, sl, qh, ql, bh, bl, sems):
    (arrived,) = fetch([(in_any, in_ref)], sems)
    copies = fetch(
        [(yh_any, yh), (yl_any, yl), (xh_any, xh), (xl_any, xl), (green_any, green_ref), (ih_any, ih), (il_any, il)],
        sems.at[pl.ds(1, 7)])
    arrived.wait()
    first = lax.broadcasted_iota(jnp.int32, (64, 128), 1) % 64 < 32
    order = (0, 2, 1, 3)
    for i, ex in enumerate(order):
        a = slice(64 * i, 64 * i + 64)
        for m in range(2):
            c = slice(128 * m, 128 * m + 128)
            d0 = in_ref[pl.ds(8 * m + ex, 64, stride=16), :]
            d1 = in_ref[pl.ds(8 * m + 4 + ex, 64, stride=16), :]
            ah[0, a, c], al[0, a, c] = split(jnp.where(first, d0, pltpu.roll(d1, 32, 1)))
            ah[1, a, c], al[1, a, c] = split(jnp.where(first, pltpu.roll(d0, 96, 1), d1))
    copies[0].wait()
    copies[1].wait()
    for xp in range(2):
        a = slice(128 * xp, 128 * xp + 128)
        for r in range(2):
            c = slice(256 * r, 256 * r + 256)
            even = dot3(ah[0, a, :], al[0, a, :], yh[0, :, c], yl[0, :, c])
            odd = dot3(ah[1, a, :], al[1, a, :], yh[1, :, c], yl[1, :, c])
            o = slice(128 * r, 128 * r + 128)
            sh[xp, o, 0:256], sl[xp, o, 0:256] = split(even + odd)
            sh[xp, o, 256:512], sl[xp, o, 256:512] = split(even - odd)
    copies[2].wait()
    copies[3].wait()
    copies[4].wait()
    for j in range(2):
        c = slice(256 * j, 256 * j + 256)
        for i in range(2):
            lo = slice(128 * i, 128 * i + 128)
            hi = slice(256 + 128 * i, 384 + 128 * i)
            part = [[dot3(xh[xp, a, :], xl[xp, a, :], sh[xp, :, c], sl[xp, :, c]) for xp in range(2)] for a in (lo, hi)]
            (re0, re1), (im0, im1) = part
            re, im = re0 + re1, im0 + im1
            gr, gi = green_ref[0, lo, c], green_ref[1, lo, c]
            p_re, p_im = gr * re - gi * im, gr * im + gi * re
            re, im = re0 - re1, im0 - im1
            gr, gi = green_ref[0, hi, c], green_ref[1, hi, c]
            q_re, q_im = gr * re - gi * im, gr * im + gi * re
            qh[0, lo, c], ql[0, lo, c] = split(p_re + q_re)
            qh[1, lo, c], ql[1, lo, c] = split(p_re - q_re)
            qh[0, hi, c], ql[0, hi, c] = split(p_im + q_im)
            qh[1, hi, c], ql[1, hi, c] = split(p_im - q_im)
    copies[5].wait()
    copies[6].wait()
    for xp in range(2):
        for r in range(2):
            a = slice(128 * r, 128 * r + 128)
            u0, u1 = [
                dot3(ih[xp, a, :], il[xp, a, :], qh[xp, :, c], ql[xp, :, c]) for c in (slice(0, 256), slice(256, 512))
            ]
            rows, o = slice(128 * xp, 128 * xp + 128), slice(256 * r, 256 * r + 256)
            bh[0, rows, o], bl[0, rows, o] = split(u0 + u1)
            bh[1, rows, o], bl[1, rows, o] = split(u0 - u1)
    for xp in range(2):
        a = slice(128 * xp, 128 * xp + 128)
        even, odd = [
            dot_t(bh[p, a, :], yh[p]) + (dot_t(bh[p, a, :], yl[p]) + dot_t(bl[p, a, :], yh[p])) for p in range(2)
        ]
        for e in range(2):
            ex = order[2 * xp + e]
            rows = slice(64 * e, 64 * e + 64)
            for m in range(2):
                c = slice(128 * m, 128 * m + 128)
                ve, vo = even[rows, c], odd[rows, c]
                out_ref[pl.ds(8 * m + ex, 64, stride=16), :] = jnp.where(first, ve, pltpu.roll(vo, 32, 1))
                out_ref[pl.ds(8 * m + 4 + ex, 64, stride=16), :] = jnp.where(first, pltpu.roll(ve, 96, 1), vo)


def from_grid(count_ref, site_ref, in_ref, proj_ref, expand_ref, fh_ref, fl_ref, near_ref, out_ref):
    count = count_ref[0]
    line, plane = site_masks(count, site_ref[...])
    field = jnp.concatenate([in_ref[pl.ds(ex, 256, stride=4), :] for ex in range(4)], axis=1)
    vh, vl = split(jnp.concatenate([field, swap(field)], axis=0))
    points = dot3(fh_ref[...], fl_ref[...], vh, vl)
    bh, bl = split(points)
    pick = line.T.astype(BF16)
    total = jnp.zeros((256, 128), F32)
    for ez in range(4):
        rows = slice(32 * ez, 32 * ez + 32)
        for ex in range(4):
            c = slice(128 * ex, 128 * ex + 128)
            high = (dot(pick, bh[rows, c]) * plane).astype(BF16)
            low = (dot(pick, bl[rows, c]) * plane).astype(BF16)
            lo = (ez * 4 + ex) * 128
            e = expand_ref[:, lo : lo + 128]
            total = total + (dot_t(high, e) + dot_t(low, e))
    th, tl = split(total)
    ph, plo = split(proj_ref[...])
    parts = []
    for r in range(2):
        c = slice(64 * r, 64 * r + 64)
        parts.append(dot3(th[:, c], tl[:, c], ph, plo))
    far = jnp.concatenate(parts, axis=1).T
    slots = lax.broadcasted_iota(jnp.int32, (128, 256), 1)
    out_ref[...] = far + jnp.where(slots < count, near_ref[...], 0.0)


CLASSES = 27


def near_tables(table_ref, after_any, high_ref, low_ref):
    for k in range(CLASSES):
        re, im = table_ref[k, 0], table_ref[k, 1]
        for r, (a, b) in enumerate(((re, -im), (im, re))):
            rows = slice(64 * r, 64 * r + 64)
            high_ref[k, rows, :], low_ref[k, rows, :] = split(jnp.concatenate([a, b], axis=1))


def near(index_ref, left_any, own_any, right_any, high_any, low_any, out_ref, source_ref, picked, high_ref, low_ref, sems):
    sources = [(r, source_ref.at[pl.ds(768 * i, 768), :]) for i, r in enumerate((left_any, own_any, right_any))]
    copies = fetch(sources + [(high_any, high_ref), (low_any, low_ref)], sems)
    for copy in copies[:3]:
        copy.wait()

    def one(k, carry):
        for b in range(256):
            i = index_ref[k * 256 + b]
            picked[k, pl.ds(b, 1), :] = source_ref[pl.ds(i, 1), :]
        return carry

    lax.fori_loop(0, CLASSES, one, 0)
    for copy in copies[3:]:
        copy.wait()
    total = jnp.zeros((256, 128), F32)
    for k in range(CLASSES):
        gh, gl = split(picked[k])
        th, tl = high_ref[k], low_ref[k]
        total = total + (dot_t(gh, th) + (dot_t(gh, tl) + dot_t(gl, th)))
    out_ref[...] = total.T


def call(kernel, outs, args, kinds, scratch=(), copies=0, flops=0, bytes_accessed=0, name=None, out_kind="v", room=40):
    spaces = {"s": pltpu.SMEM, "v": VMEM, "h": pltpu.HBM}
    single = not isinstance(outs, (tuple, list))
    out_spec = pl.BlockSpec(memory_space=spaces[out_kind])
    scratch = list(scratch) + ([pltpu.SemaphoreType.DMA((copies,))] if copies else [])
    return pl.pallas_call(
        kernel,
        out_shape=outs,
        in_specs=[pl.BlockSpec(memory_space=spaces[k]) for k in kinds],
        out_specs=out_spec if single else tuple(out_spec for _ in outs),
        scratch_shapes=scratch,
        compiler_params=pltpu.CompilerParams(vmem_limit_bytes=room << 20),
        cost_estimate=pl.CostEstimate(flops=flops, bytes_accessed=bytes_accessed, transcendentals=0),
        name=name,
    )(*args)


def neighbours(array, axis, size):
    up = [(i, i + 1) for i in range(size - 1)]
    down = [(i + 1, i) for i in range(size - 1)]
    return lax.ppermute(array, axis, up), lax.ppermute(array, axis, down)


def per_device(charges, projection, green_hat, near_table, block_site, block_count, near_source):
    forward_z, inverse_z, expand, along, across = tables()
    fzh, fzl = halves(forward_z)
    izh, izl = halves(inverse_z)
    yh, yl = halves(along)
    xh, xl = halves(across)
    ih, il = halves(np.ascontiguousarray(across.transpose(0, 2, 1)))
    expand = expand.astype(jnp.bfloat16)
    site = block_site.reshape(1, 256)
    shape = lambda *s: jax.ShapeDtypeStruct(s, F32)

    cells = charges.reshape(128, 256)
    sent = call(
        to_grid, shape(1024, 128), (block_count, cells, site, projection, expand, fzh, fzl), "shhhhhh",
        scratch=[VMEM((128, 256), F32), VMEM((1, 256), jnp.int32), VMEM((64, 64), F32), VMEM((128, 2048), BF16)]
        + [VMEM((256, 256), BF16)] * 2,
        copies=6, flops=2 * 10**9, bytes_accessed=2 << 20, name="to_grid", room=63,
    )
    planes = lax.all_to_all(sent.reshape(256, 4, 128), BOTH, split_axis=0, concat_axis=0, tiled=True)
    masked = call(turn, shape(256, 128), (block_count, cells, sent), "svh", bytes_accessed=1 << 20, name="turn", room=63)
    before, after = neighbours(masked, "wide", W)
    own = call(join, shape(768, 128), (before, masked, after), "hhh", copies=3, bytes_accessed=2 << 20, name="join", out_kind="h", room=63)
    left, right = neighbours(own, "narrow", N)
    table = jax.ShapeDtypeStruct((CLASSES, 128, 128), BF16)
    table_high, table_low = call(near_tables, (table, table), (near_table, sent), "vh", bytes_accessed=4 << 20,
                                  name="near_tables", room=63)
    back = call(
        convolve, shape(1024, 128),
        (planes.reshape(1024, 128), green_hat.reshape(2, 512, 512), yh, yl, xh, xl, ih, il, table_high), "hhhhhhhhh",
        scratch=[VMEM((1024, 128), F32), VMEM((2, 512, 512), F32)] + [VMEM((2, 256, 512), BF16)] * 2 + [VMEM((2, 512, 256), BF16)] * 2
        + [VMEM((2, 256, 512), BF16)] * 2 + [VMEM((2, 256, 256), BF16)] * 2 + [VMEM((2, 256, 512), BF16)] * 2
        + [VMEM((2, 512, 512), BF16)] * 2 + [VMEM((2, 256, 512), BF16)] * 2,
        copies=8, flops=5 * 10**9, bytes_accessed=9 << 20, name="convolve", room=63,
    )
    field = lax.all_to_all(back.reshape(256, 4, 128), BOTH, split_axis=0, concat_axis=0, tiled=True)
    step_wide, step_narrow, slot = near_source // 768, near_source // 256 % 3, near_source % 256
    index = (step_narrow * 768 + step_wide * 256 + slot).reshape(CLASSES * 256)
    beside = call(
        near, shape(128, 256), (index, left, own, right, table_high, table_low), "shhhhh",
        scratch=[VMEM((2304, 128), F32), VMEM((CLASSES, 256, 128), F32)] + [VMEM((CLASSES, 128, 128), BF16)] * 2,
        copies=5, flops=10**10, bytes_accessed=40 << 20, name="near", room=63,
    )
    result = call(
        from_grid, shape(128, 256),
        (block_count, site, field.reshape(1024, 128), projection, expand, izh, izl, beside), "svvvvvvv",
        flops=2 * 10**9, bytes_accessed=2 << 20, name="from_grid", room=16,
    )
    return result.reshape(2, 64, 256)


def solution(mesh):
    placed = (
        P(None, None, BOTH),
        P(),
        P(None, BOTH, None, None),
        P(),
        P(BOTH),
        P(BOTH),
        P(None, BOTH),
    )
    return jax.shard_map(
        per_device,
        mesh=mesh,
        in_specs=placed,
        out_specs=P(None, None, BOTH),
        check_vma=False,
    )
```

```python
import numpy as np

import jax
import jax.numpy as jnp
from jax import lax
from jax.experimental import pallas as pl
from jax.experimental.pallas import tpu as pltpu
from jax.sharding import PartitionSpec as P

W = 64
N = 4
F32 = jnp.float32
BF16 = jnp.bfloat16
VMEM = pltpu.VMEM
BOTH = ("wide", "narrow")


def halves(table):
    high = table.astype(jnp.bfloat16)
    low = (table - high.astype(np.float64)).astype(jnp.bfloat16)
    return high, low


def split(value):
    high = value.astype(BF16)
    return high, (value - high.astype(F32)).astype(BF16)


def dot(left, right):
    return lax.dot_general(left, right, (((1,), (0,)), ((), ())), preferred_element_type=F32)


def dot_t(left, right):
    return lax.dot_general(left, right, (((1,), (1,)), ((), ())), preferred_element_type=F32)


def dot3(lh, ll, rh, rl):
    return dot(lh, rh) + (dot(lh, rl) + dot(ll, rh))


def tables():
    z = np.arange(128)
    z_of = 4 * (z % 32) + z // 32
    kz = np.arange(256)
    ang = 2 * np.pi * ((kz[:, None] * z_of[None, :]) % 256) / 256
    forward_z = np.concatenate([np.cos(ang), np.sin(ang)], 1)
    inverse_z = np.concatenate([np.cos(ang).T, -np.sin(ang).T], 1) * 2.0**-26
    lane = np.arange(2048)
    group, inner = lane // 128, lane % 128
    ez, ex = group // 4, group % 4
    r, ey = inner // 64, inner // 16 % 2 * 2 + inner // 32 % 2
    row = r * 64 + 16 * ex + 4 * ey + ez
    expand = (np.arange(128)[:, None] == row[None, :]).astype(np.float32)
    k = np.arange(256)
    i = np.arange(256)
    real = (i // 64 % 2 == 0)[:, None]
    along = []
    for p in range(2):
        y = 64 * (i // 128 * 2 + i // 32 % 2) + 4 * (i % 16) + 2 * (i // 16 % 2) + p
        ang = 2 * np.pi * ((y[:, None] * k[None, :]) % 512) / 512
        c, s = np.cos(ang), np.sin(ang)
        along.append(np.concatenate([np.where(real, c, s), np.where(real, -s, c)], 1))
    across = []
    j = np.arange(128)
    for p in range(2):
        x = 4 * (j % 64) + 2 * (j // 64) + p
        ang = 2 * np.pi * ((k[:, None] * x[None, :]) % 512) / 512
        c, s = np.cos(ang), np.sin(ang)
        across.append(np.block([[c, s], [-s, c]]))
    return forward_z, inverse_z, expand, np.stack(along), np.stack(across)


def swap(value):
    lanes = value.shape[1]
    rolled = jnp.concatenate(
        [pltpu.roll(value[:, i : i + 128], 64, 1) for i in range(0, lanes, 128)], axis=1
    )
    sign = jnp.where(lax.broadcasted_iota(jnp.int32, (1, lanes), 1) % 128 < 64, 1.0, -1.0)
    return rolled * sign


def site_masks(count, site):
    rows = lax.broadcasted_iota(jnp.int32, (32, 256), 0)
    line = jnp.where(rows == site % 32, 1.0, 0.0)
    lanes = lax.broadcasted_iota(jnp.int32, (128, 256), 0)
    slots = lax.broadcasted_iota(jnp.int32, (128, 256), 1)
    plane = jnp.where((lanes % 16 == site // 32) & (slots < count), 1.0, 0.0)
    return line, plane.T


def fetch(pairs, sems):
    copies = [pltpu.make_async_copy(s, d, sems.at[i]) for i, (s, d) in enumerate(pairs)]
    for copy in copies:
        copy.start()
    return copies


def to_grid(count_ref, charges_any, site_any, proj_any, expand_any, fh_any, fl_any, out_ref,
            charges_ref, site_ref, proj_ref, expand_ref, fh_ref, fl_ref, sems):
    copies = fetch(
        [(charges_any, charges_ref), (proj_any, proj_ref), (site_any, site_ref),
         (expand_any, expand_ref), (fh_any, fh_ref), (fl_any, fl_ref)], sems)
    count = count_ref[0]
    slots = lax.broadcasted_iota(jnp.int32, (128, 256), 1)
    for copy in copies[:3]:
        copy.wait()
    line, plane = site_masks(count, site_ref[...])
    turned = jnp.where(slots < count, charges_ref[...], 0.0).T
    ph, plo = split(proj_ref[...])
    parts = []
    for r in range(2):
        mh, ml = split(turned[:, 64 * r : 64 * r + 64])
        parts.append(dot_t(mh, ph) + (dot_t(mh, plo) + dot_t(ml, ph)))
    both = jnp.concatenate(split(jnp.concatenate(parts, axis=1)), axis=0)
    plane = jnp.concatenate([plane, plane], axis=1)
    line = line.astype(BF16)
    line = jnp.concatenate([line, line], axis=1)
    copies[3].wait()
    rows = []
    for ez in range(4):
        cols = []
        for e in range(2):
            lo = (ez * 4 + 2 * e) * 128
            spread = dot(both, expand_ref[:, lo : lo + 256])
            high = (spread[:256] * plane).astype(BF16)
            low = (spread[256:] * plane).astype(BF16)
            cols.append(dot(line, jnp.concatenate([high, low], axis=0)))
        rows.append(jnp.concatenate(cols, axis=1))
    grid = jnp.concatenate(rows, axis=0)
    gh, gl = split(jnp.concatenate([grid, swap(grid)], axis=0))
    copies[4].wait()
    copies[5].wait()
    for e in range(2):
        c = slice(256 * e, 256 * e + 256)
        planes = dot3(fh_ref[...], fl_ref[...], gh[:, c], gl[:, c])
        out_ref[pl.ds(2 * e, 256, stride=4), :] = planes[:, :128]
        out_ref[pl.ds(2 * e + 1, 256, stride=4), :] = planes[:, 128:]


def turn(count_ref, charges_ref, after_any, out_ref):
    slots = lax.broadcasted_iota(jnp.int32, (128, 256), 1)
    out_ref[...] = jnp.where(slots < count_ref[0], charges_ref[...], 0.0).T


def join(a_ref, b_ref, c_ref, out_ref):
    for i, ref in enumerate((a_ref, b_ref, c_ref)):
        out_ref[256 * i : 256 * i + 256, :] = ref[...]


def convolve(in_any, green_any, yh_any, yl_any, xh_any, xl_any, ih_any, il_any, out_ref,
             in_ref, green_ref, yh, yl, xh, xl, ih, il, ah, al, sh, sl, qh, ql, bh, bl, sems):
    (arrived,) = fetch([(in_any, in_ref)], sems)
    copies = fetch(
        [(yh_any, yh), (yl_any, yl), (xh_any, xh), (xl_any, xl), (green_any, green_ref), (ih_any, ih), (il_any, il)],
        sems.at[pl.ds(1, 7)])
    arrived.wait()
    first = lax.broadcasted_iota(jnp.int32, (64, 128), 1) % 64 < 32
    order = (0, 2, 1, 3)
    for i, ex in enumerate(order):
        a = slice(64 * i, 64 * i + 64)
        for m in range(2):
            c = slice(128 * m, 128 * m + 128)
            d0 = in_ref[pl.ds(8 * m + ex, 64, stride=16), :]
            d1 = in_ref[pl.ds(8 * m + 4 + ex, 64, stride=16), :]
            ah[0, a, c], al[0, a, c] = split(jnp.where(first, d0, pltpu.roll(d1, 32, 1)))
            ah[1, a, c], al[1, a, c] = split(jnp.where(first, pltpu.roll(d0, 96, 1), d1))
    copies[0].wait()
    copies[1].wait()
    for xp in range(2):
        a = slice(128 * xp, 128 * xp + 128)
        for r in range(2):
            c = slice(256 * r, 256 * r + 256)
            even = dot3(ah[0, a, :], al[0, a, :], yh[0, :, c], yl[0, :, c])
            odd = dot3(ah[1, a, :], al[1, a, :], yh[1, :, c], yl[1, :, c])
            o = slice(128 * r, 128 * r + 128)
            sh[xp, o, 0:256], sl[xp, o, 0:256] = split(even + odd)
            sh[xp, o, 256:512], sl[xp, o, 256:512] = split(even - odd)
    copies[2].wait()
    copies[3].wait()
    copies[4].wait()
    for j in range(2):
        c = slice(256 * j, 256 * j + 256)
        for i in range(2):
            lo = slice(128 * i, 128 * i + 128)
            hi = slice(256 + 128 * i, 384 + 128 * i)
            part = [[dot3(xh[xp, a, :], xl[xp, a, :], sh[xp, :, c], sl[xp, :, c]) for xp in range(2)] for a in (lo, hi)]
            (re0, re1), (im0, im1) = part
            re, im = re0 + re1, im0 + im1
            gr, gi = green_ref[0, lo, c], green_ref[1, lo, c]
            p_re, p_im = gr * re - gi * im, gr * im + gi * re
            re, im = re0 - re1, im0 - im1
            gr, gi = green_ref[0, hi, c], green_ref[1, hi, c]
            q_re, q_im = gr * re - gi * im, gr * im + gi * re
            qh[0, lo, c], ql[0, lo, c] = split(p_re + q_re)
            qh[1, lo, c], ql[1, lo, c] = split(p_re - q_re)
            qh[0, hi, c], ql[0, hi, c] = split(p_im + q_im)
            qh[1, hi, c], ql[1, hi, c] = split(p_im - q_im)
    copies[5].wait()
    copies[6].wait()
    for xp in range(2):
        for r in range(2):
            a = slice(128 * r, 128 * r + 128)
            u0, u1 = [
                dot3(ih[xp, a, :], il[xp, a, :], qh[xp, :, c], ql[xp, :, c]) for c in (slice(0, 256), slice(256, 512))
            ]
            rows, o = slice(128 * xp, 128 * xp + 128), slice(256 * r, 256 * r + 256)
            bh[0, rows, o], bl[0, rows, o] = split(u0 + u1)
            bh[1, rows, o], bl[1, rows, o] = split(u0 - u1)
    for xp in range(2):
        a = slice(128 * xp, 128 * xp + 128)
        even, odd = [
            dot_t(bh[p, a, :], yh[p]) + (dot_t(bh[p, a, :], yl[p]) + dot_t(bl[p, a, :], yh[p])) for p in range(2)
        ]
        for e in range(2):
            ex = order[2 * xp + e]
            rows = slice(64 * e, 64 * e + 64)
            for m in range(2):
                c = slice(128 * m, 128 * m + 128)
                ve, vo = even[rows, c], odd[rows, c]
                out_ref[pl.ds(8 * m + ex, 64, stride=16), :] = jnp.where(first, ve, pltpu.roll(vo, 32, 1))
                out_ref[pl.ds(8 * m + 4 + ex, 64, stride=16), :] = jnp.where(first, pltpu.roll(ve, 96, 1), vo)


def from_grid(count_ref, site_ref, in_ref, proj_ref, expand_ref, fh_ref, fl_ref, near_ref, out_ref):
    count = count_ref[0]
    line, plane = site_masks(count, site_ref[...])
    field = jnp.concatenate([in_ref[pl.ds(ex, 256, stride=4), :] for ex in range(4)], axis=1)
    vh, vl = split(jnp.concatenate([field, swap(field)], axis=0))
    points = dot3(fh_ref[...], fl_ref[...], vh, vl)
    bh, bl = split(points)
    pick = line.T.astype(BF16)
    total = jnp.zeros((256, 128), F32)
    for ez in range(4):
        rows = slice(32 * ez, 32 * ez + 32)
        for ex in range(4):
            c = slice(128 * ex, 128 * ex + 128)
            high = (dot(pick, bh[rows, c]) * plane).astype(BF16)
            low = (dot(pick, bl[rows, c]) * plane).astype(BF16)
            lo = (ez * 4 + ex) * 128
            e = expand_ref[:, lo : lo + 128]
            total = total + (dot_t(high, e) + dot_t(low, e))
    th, tl = split(total)
    ph, plo = split(proj_ref[...])
    parts = []
    for r in range(2):
        c = slice(64 * r, 64 * r + 64)
        parts.append(dot3(th[:, c], tl[:, c], ph, plo))
    far = jnp.concatenate(parts, axis=1).T
    slots = lax.broadcasted_iota(jnp.int32, (128, 256), 1)
    out_ref[...] = far + jnp.where(slots < count, near_ref[...], 0.0)


CLASSES = 27


def near(index_ref, left_ref, own_ref, right_ref, table_ref, out_ref, source_ref, picked):
    for i, ref in enumerate((left_ref, own_ref, right_ref)):
        source_ref[768 * i : 768 * i + 768, :] = ref[...]

    def one(k, carry):
        for b in range(256):
            i = index_ref[k * 256 + b]
            picked[k, pl.ds(b, 1), :] = source_ref[pl.ds(i, 1), :]
        return carry

    lax.fori_loop(0, CLASSES, one, 0)
    total = jnp.zeros((256, 128), F32)
    for k in range(CLASSES):
        gh, gl = split(picked[k])
        re, im = table_ref[k, 0], table_ref[k, 1]
        rows = [jnp.concatenate([re, -im], axis=1), jnp.concatenate([im, re], axis=1)]
        th, tl = split(jnp.concatenate(rows, axis=0))
        total = total + (dot_t(gh, th) + (dot_t(gh, tl) + dot_t(gl, th)))
    out_ref[...] = total.T


def call(kernel, outs, args, kinds, scratch=(), copies=0, flops=0, bytes_accessed=0, name=None, out_kind="v", room=40):
    spaces = {"s": pltpu.SMEM, "v": VMEM, "h": pltpu.HBM}
    single = not isinstance(outs, (tuple, list))
    out_spec = pl.BlockSpec(memory_space=spaces[out_kind])
    scratch = list(scratch) + ([pltpu.SemaphoreType.DMA((copies,))] if copies else [])
    return pl.pallas_call(
        kernel,
        out_shape=outs,
        in_specs=[pl.BlockSpec(memory_space=spaces[k]) for k in kinds],
        out_specs=out_spec if single else tuple(out_spec for _ in outs),
        scratch_shapes=scratch,
        compiler_params=pltpu.CompilerParams(vmem_limit_bytes=room << 20),
        cost_estimate=pl.CostEstimate(flops=flops, bytes_accessed=bytes_accessed, transcendentals=0),
        name=name,
    )(*args)


def neighbours(array, axis, size):
    up = [(i, i + 1) for i in range(size - 1)]
    down = [(i + 1, i) for i in range(size - 1)]
    return lax.ppermute(array, axis, up), lax.ppermute(array, axis, down)


def per_device(charges, projection, green_hat, near_table, block_site, block_count, near_source):
    forward_z, inverse_z, expand, along, across = tables()
    fzh, fzl = halves(forward_z)
    izh, izl = halves(inverse_z)
    yh, yl = halves(along)
    xh, xl = halves(across)
    ih, il = halves(np.ascontiguousarray(across.transpose(0, 2, 1)))
    expand = expand.astype(jnp.bfloat16)
    site = block_site.reshape(1, 256)
    shape = lambda *s: jax.ShapeDtypeStruct(s, F32)

    cells = charges.reshape(128, 256)
    sent = call(
        to_grid, shape(1024, 128), (block_count, cells, site, projection, expand, fzh, fzl), "shhhhhh",
        scratch=[VMEM((128, 256), F32), VMEM((1, 256), jnp.int32), VMEM((64, 64), F32), VMEM((128, 2048), BF16)]
        + [VMEM((256, 256), BF16)] * 2,
        copies=6, flops=2 * 10**9, bytes_accessed=2 << 20, name="to_grid", room=63,
    )
    planes = lax.all_to_all(sent.reshape(256, 4, 128), BOTH, split_axis=0, concat_axis=0, tiled=True)
    masked = call(turn, shape(256, 128), (block_count, cells, sent), "svh", bytes_accessed=1 << 20, name="turn", room=16)
    before, after = neighbours(masked, "wide", W)
    own = call(join, shape(768, 128), (before, masked, after), "vvv", bytes_accessed=2 << 20, name="join", room=16)
    left, right = neighbours(own, "narrow", N)
    back = call(
        convolve, shape(1024, 128),
        (planes.reshape(1024, 128), green_hat.reshape(2, 512, 512), yh, yl, xh, xl, ih, il), "hhhhhhhh",
        scratch=[VMEM((1024, 128), F32), VMEM((2, 512, 512), F32)] + [VMEM((2, 256, 512), BF16)] * 2 + [VMEM((2, 512, 256), BF16)] * 2
        + [VMEM((2, 256, 512), BF16)] * 2 + [VMEM((2, 256, 256), BF16)] * 2 + [VMEM((2, 256, 512), BF16)] * 2
        + [VMEM((2, 512, 512), BF16)] * 2 + [VMEM((2, 256, 512), BF16)] * 2,
        copies=8, flops=5 * 10**9, bytes_accessed=9 << 20, name="convolve", room=63,
    )
    field = lax.all_to_all(back.reshape(256, 4, 128), BOTH, split_axis=0, concat_axis=0, tiled=True)
    step_wide, step_narrow, slot = near_source // 768, near_source // 256 % 3, near_source % 256
    index = (step_narrow * 768 + step_wide * 256 + slot).reshape(CLASSES * 256)
    beside = call(
        near, shape(128, 256), (index, left, own, right, near_table), "svvvv",
        scratch=[VMEM((2304, 128), F32), VMEM((CLASSES, 256, 128), F32)],
        flops=10**10, bytes_accessed=40 << 20, name="near",
    )
    result = call(
        from_grid, shape(128, 256),
        (block_count, site, field.reshape(1024, 128), projection, expand, izh, izl, beside), "svvvvvvv",
        flops=2 * 10**9, bytes_accessed=2 << 20, name="from_grid", room=16,
    )
    return result.reshape(2, 64, 256)


def solution(mesh):
    placed = (
        P(None, None, BOTH),
        P(),
        P(None, BOTH, None, None),
        P(),
        P(BOTH),
        P(BOTH),
        P(None, BOTH),
    )
    return jax.shard_map(
        per_device,
        mesh=mesh,
        in_specs=placed,
        out_specs=P(None, None, BOTH),
        check_vma=False,
    )
```

```python
import numpy as np

import jax
import jax.numpy as jnp
from jax import lax
from jax.experimental import pallas as pl
from jax.experimental.pallas import tpu as pltpu
from jax.sharding import PartitionSpec as P

W = 64
N = 4
F32 = jnp.float32
BF16 = jnp.bfloat16
VMEM = pltpu.VMEM
BOTH = ("wide", "narrow")


def halves(table):
    high = table.astype(jnp.bfloat16)
    low = (table - high.astype(np.float64)).astype(jnp.bfloat16)
    return high, low


def split(value):
    high = value.astype(BF16)
    return high, (value - high.astype(F32)).astype(BF16)


def dot(left, right):
    return lax.dot_general(left, right, (((1,), (0,)), ((), ())), preferred_element_type=F32)


def dot_t(left, right):
    return lax.dot_general(left, right, (((1,), (1,)), ((), ())), preferred_element_type=F32)


def dot3(lh, ll, rh, rl):
    return dot(lh, rh) + (dot(lh, rl) + dot(ll, rh))


def tables():
    z = np.arange(128)
    z_of = 4 * (z % 32) + z // 32
    kz = np.arange(256)
    ang = 2 * np.pi * ((kz[:, None] * z_of[None, :]) % 256) / 256
    forward_z = np.concatenate([np.cos(ang), np.sin(ang)], 1)
    inverse_z = np.concatenate([np.cos(ang).T, -np.sin(ang).T], 1) * 2.0**-26
    lane = np.arange(2048)
    group, inner = lane // 128, lane % 128
    ez, ex = group // 4, group % 4
    r, ey = inner // 64, inner // 16 % 2 * 2 + inner // 32 % 2
    row = r * 64 + 16 * ex + 4 * ey + ez
    expand = (np.arange(128)[:, None] == row[None, :]).astype(np.float32)
    k = np.arange(256)
    i = np.arange(256)
    real = (i // 64 % 2 == 0)[:, None]
    along = []
    for p in range(2):
        y = 64 * (i // 128 * 2 + i // 32 % 2) + 4 * (i % 16) + 2 * (i // 16 % 2) + p
        ang = 2 * np.pi * ((y[:, None] * k[None, :]) % 512) / 512
        c, s = np.cos(ang), np.sin(ang)
        along.append(np.concatenate([np.where(real, c, s), np.where(real, -s, c)], 1))
    across = []
    j = np.arange(128)
    for p in range(2):
        x = 4 * (j % 64) + 2 * (j // 64) + p
        ang = 2 * np.pi * ((k[:, None] * x[None, :]) % 512) / 512
        c, s = np.cos(ang), np.sin(ang)
        across.append(np.block([[c, s], [-s, c]]))
    return forward_z, inverse_z, expand, np.stack(along), np.stack(across)


def swap(value):
    lanes = value.shape[1]
    rolled = jnp.concatenate(
        [pltpu.roll(value[:, i : i + 128], 64, 1) for i in range(0, lanes, 128)], axis=1
    )
    sign = jnp.where(lax.broadcasted_iota(jnp.int32, (1, lanes), 1) % 128 < 64, 1.0, -1.0)
    return rolled * sign


def site_masks(count, site):
    rows = lax.broadcasted_iota(jnp.int32, (32, 256), 0)
    line = jnp.where(rows == site % 32, 1.0, 0.0)
    lanes = lax.broadcasted_iota(jnp.int32, (128, 256), 0)
    slots = lax.broadcasted_iota(jnp.int32, (128, 256), 1)
    plane = jnp.where((lanes % 16 == site // 32) & (slots < count), 1.0, 0.0)
    return line, plane.T


def fetch(pairs, sems):
    copies = [pltpu.make_async_copy(s, d, sems.at[i]) for i, (s, d) in enumerate(pairs)]
    for copy in copies:
        copy.start()
    return copies


def to_grid(count_ref, charges_any, site_any, proj_any, expand_any, fh_any, fl_any, out_ref, token_ref,
            charges_ref, site_ref, proj_ref, expand_ref, fh_ref, fl_ref, sems):
    copies = fetch(
        [(charges_any, charges_ref), (proj_any, proj_ref), (site_any, site_ref),
         (expand_any, expand_ref), (fh_any, fh_ref), (fl_any, fl_ref)], sems)
    token_ref[...] = jnp.zeros((8, 128), F32)
    count = count_ref[0]
    slots = lax.broadcasted_iota(jnp.int32, (128, 256), 1)
    for copy in copies[:3]:
        copy.wait()
    line, plane = site_masks(count, site_ref[...])
    turned = jnp.where(slots < count, charges_ref[...], 0.0).T
    ph, plo = split(proj_ref[...])
    parts = []
    for r in range(2):
        mh, ml = split(turned[:, 64 * r : 64 * r + 64])
        parts.append(dot_t(mh, ph) + (dot_t(mh, plo) + dot_t(ml, ph)))
    both = jnp.concatenate(split(jnp.concatenate(parts, axis=1)), axis=0)
    plane = jnp.concatenate([plane, plane], axis=1)
    line = line.astype(BF16)
    line = jnp.concatenate([line, line], axis=1)
    copies[3].wait()
    rows = []
    for ez in range(4):
        cols = []
        for e in range(2):
            lo = (ez * 4 + 2 * e) * 128
            spread = dot(both, expand_ref[:, lo : lo + 256])
            high = (spread[:256] * plane).astype(BF16)
            low = (spread[256:] * plane).astype(BF16)
            cols.append(dot(line, jnp.concatenate([high, low], axis=0)))
        rows.append(jnp.concatenate(cols, axis=1))
    grid = jnp.concatenate(rows, axis=0)
    gh, gl = split(jnp.concatenate([grid, swap(grid)], axis=0))
    copies[4].wait()
    copies[5].wait()
    for e in range(2):
        c = slice(256 * e, 256 * e + 256)
        planes = dot3(fh_ref[...], fl_ref[...], gh[:, c], gl[:, c])
        out_ref[pl.ds(2 * e, 256, stride=4), :] = planes[:, :128]
        out_ref[pl.ds(2 * e + 1, 256, stride=4), :] = planes[:, 128:]


def turn(count_ref, charges_ref, after_ref, out_ref):
    slots = lax.broadcasted_iota(jnp.int32, (128, 256), 1)
    out_ref[...] = jnp.where(slots < count_ref[0], charges_ref[...], 0.0).T


def join(a_ref, b_ref, c_ref, out_ref):
    for i, ref in enumerate((a_ref, b_ref, c_ref)):
        out_ref[256 * i : 256 * i + 256, :] = ref[...]


def convolve(in_any, green_any, yh_any, yl_any, xh_any, xl_any, ih_any, il_any, out_ref,
             in_ref, green_ref, yh, yl, xh, xl, ih, il, ah, al, sh, sl, qh, ql, bh, bl, sems):
    (arrived,) = fetch([(in_any, in_ref)], sems)
    copies = fetch(
        [(yh_any, yh), (yl_any, yl), (xh_any, xh), (xl_any, xl), (green_any, green_ref), (ih_any, ih), (il_any, il)],
        sems.at[pl.ds(1, 7)])
    arrived.wait()
    first = lax.broadcasted_iota(jnp.int32, (64, 128), 1) % 64 < 32
    order = (0, 2, 1, 3)
    for i, ex in enumerate(order):
        a = slice(64 * i, 64 * i + 64)
        for m in range(2):
            c = slice(128 * m, 128 * m + 128)
            d0 = in_ref[pl.ds(8 * m + ex, 64, stride=16), :]
            d1 = in_ref[pl.ds(8 * m + 4 + ex, 64, stride=16), :]
            ah[0, a, c], al[0, a, c] = split(jnp.where(first, d0, pltpu.roll(d1, 32, 1)))
            ah[1, a, c], al[1, a, c] = split(jnp.where(first, pltpu.roll(d0, 96, 1), d1))
    copies[0].wait()
    copies[1].wait()
    for xp in range(2):
        a = slice(128 * xp, 128 * xp + 128)
        for r in range(2):
            c = slice(256 * r, 256 * r + 256)
            even = dot3(ah[0, a, :], al[0, a, :], yh[0, :, c], yl[0, :, c])
            odd = dot3(ah[1, a, :], al[1, a, :], yh[1, :, c], yl[1, :, c])
            o = slice(128 * r, 128 * r + 128)
            sh[xp, o, 0:256], sl[xp, o, 0:256] = split(even + odd)
            sh[xp, o, 256:512], sl[xp, o, 256:512] = split(even - odd)
    copies[2].wait()
    copies[3].wait()
    copies[4].wait()
    for j in range(2):
        c = slice(256 * j, 256 * j + 256)
        for i in range(2):
            lo = slice(128 * i, 128 * i + 128)
            hi = slice(256 + 128 * i, 384 + 128 * i)
            part = [[dot3(xh[xp, a, :], xl[xp, a, :], sh[xp, :, c], sl[xp, :, c]) for xp in range(2)] for a in (lo, hi)]
            (re0, re1), (im0, im1) = part
            re, im = re0 + re1, im0 + im1
            gr, gi = green_ref[0, lo, c], green_ref[1, lo, c]
            p_re, p_im = gr * re - gi * im, gr * im + gi * re
            re, im = re0 - re1, im0 - im1
            gr, gi = green_ref[0, hi, c], green_ref[1, hi, c]
            q_re, q_im = gr * re - gi * im, gr * im + gi * re
            qh[0, lo, c], ql[0, lo, c] = split(p_re + q_re)
            qh[1, lo, c], ql[1, lo, c] = split(p_re - q_re)
            qh[0, hi, c], ql[0, hi, c] = split(p_im + q_im)
            qh[1, hi, c], ql[1, hi, c] = split(p_im - q_im)
    copies[5].wait()
    copies[6].wait()
    for xp in range(2):
        for r in range(2):
            a = slice(128 * r, 128 * r + 128)
            u0, u1 = [
                dot3(ih[xp, a, :], il[xp, a, :], qh[xp, :, c], ql[xp, :, c]) for c in (slice(0, 256), slice(256, 512))
            ]
            rows, o = slice(128 * xp, 128 * xp + 128), slice(256 * r, 256 * r + 256)
            bh[0, rows, o], bl[0, rows, o] = split(u0 + u1)
            bh[1, rows, o], bl[1, rows, o] = split(u0 - u1)
    for xp in range(2):
        a = slice(128 * xp, 128 * xp + 128)
        even, odd = [
            dot_t(bh[p, a, :], yh[p]) + (dot_t(bh[p, a, :], yl[p]) + dot_t(bl[p, a, :], yh[p])) for p in range(2)
        ]
        for e in range(2):
            ex = order[2 * xp + e]
            rows = slice(64 * e, 64 * e + 64)
            for m in range(2):
                c = slice(128 * m, 128 * m + 128)
                ve, vo = even[rows, c], odd[rows, c]
                out_ref[pl.ds(8 * m + ex, 64, stride=16), :] = jnp.where(first, ve, pltpu.roll(vo, 32, 1))
                out_ref[pl.ds(8 * m + 4 + ex, 64, stride=16), :] = jnp.where(first, pltpu.roll(ve, 96, 1), vo)


def from_grid(count_ref, site_ref, in_ref, proj_ref, expand_ref, fh_ref, fl_ref, near_ref, out_ref):
    count = count_ref[0]
    line, plane = site_masks(count, site_ref[...])
    field = jnp.concatenate([in_ref[pl.ds(ex, 256, stride=4), :] for ex in range(4)], axis=1)
    vh, vl = split(jnp.concatenate([field, swap(field)], axis=0))
    points = dot3(fh_ref[...], fl_ref[...], vh, vl)
    bh, bl = split(points)
    pick = line.T.astype(BF16)
    total = jnp.zeros((256, 128), F32)
    for ez in range(4):
        rows = slice(32 * ez, 32 * ez + 32)
        for ex in range(4):
            c = slice(128 * ex, 128 * ex + 128)
            high = (dot(pick, bh[rows, c]) * plane).astype(BF16)
            low = (dot(pick, bl[rows, c]) * plane).astype(BF16)
            lo = (ez * 4 + ex) * 128
            e = expand_ref[:, lo : lo + 128]
            total = total + (dot_t(high, e) + dot_t(low, e))
    th, tl = split(total)
    ph, plo = split(proj_ref[...])
    parts = []
    for r in range(2):
        c = slice(64 * r, 64 * r + 64)
        parts.append(dot3(th[:, c], tl[:, c], ph, plo))
    far = jnp.concatenate(parts, axis=1).T
    slots = lax.broadcasted_iota(jnp.int32, (128, 256), 1)
    out_ref[...] = far + jnp.where(slots < count, near_ref[...], 0.0)


CLASSES = 27


def near(index_ref, left_ref, own_ref, right_ref, table_ref, out_ref, source_ref, picked):
    for i, ref in enumerate((left_ref, own_ref, right_ref)):
        source_ref[768 * i : 768 * i + 768, :] = ref[...]

    def one(k, carry):
        for b in range(256):
            i = index_ref[k * 256 + b]
            picked[k, pl.ds(b, 1), :] = source_ref[pl.ds(i, 1), :]
        return carry

    lax.fori_loop(0, CLASSES, one, 0)
    total = jnp.zeros((256, 128), F32)
    for k in range(CLASSES):
        gh, gl = split(picked[k])
        re, im = table_ref[k, 0], table_ref[k, 1]
        rows = [jnp.concatenate([re, -im], axis=1), jnp.concatenate([im, re], axis=1)]
        th, tl = split(jnp.concatenate(rows, axis=0))
        total = total + (dot_t(gh, th) + (dot_t(gh, tl) + dot_t(gl, th)))
    out_ref[...] = total.T


def call(kernel, outs, args, kinds, scratch=(), copies=0, flops=0, bytes_accessed=0, name=None, out_kind="v", room=40):
    spaces = {"s": pltpu.SMEM, "v": VMEM, "h": pltpu.HBM}
    single = not isinstance(outs, (tuple, list))
    out_spec = pl.BlockSpec(memory_space=spaces[out_kind])
    scratch = list(scratch) + ([pltpu.SemaphoreType.DMA((copies,))] if copies else [])
    return pl.pallas_call(
        kernel,
        out_shape=outs,
        in_specs=[pl.BlockSpec(memory_space=spaces[k]) for k in kinds],
        out_specs=out_spec if single else tuple(out_spec for _ in outs),
        scratch_shapes=scratch,
        compiler_params=pltpu.CompilerParams(vmem_limit_bytes=room << 20),
        cost_estimate=pl.CostEstimate(flops=flops, bytes_accessed=bytes_accessed, transcendentals=0),
        name=name,
    )(*args)


def neighbours(array, axis, size):
    up = [(i, i + 1) for i in range(size - 1)]
    down = [(i + 1, i) for i in range(size - 1)]
    return lax.ppermute(array, axis, up), lax.ppermute(array, axis, down)


def per_device(charges, projection, green_hat, near_table, block_site, block_count, near_source):
    forward_z, inverse_z, expand, along, across = tables()
    fzh, fzl = halves(forward_z)
    izh, izl = halves(inverse_z)
    yh, yl = halves(along)
    xh, xl = halves(across)
    ih, il = halves(np.ascontiguousarray(across.transpose(0, 2, 1)))
    expand = expand.astype(jnp.bfloat16)
    site = block_site.reshape(1, 256)
    shape = lambda *s: jax.ShapeDtypeStruct(s, F32)

    cells = charges.reshape(128, 256)
    sent, token = call(
        to_grid, (shape(1024, 128), shape(8, 128)), (block_count, cells, site, projection, expand, fzh, fzl), "shhhhhh",
        scratch=[VMEM((128, 256), F32), VMEM((1, 256), jnp.int32), VMEM((64, 64), F32), VMEM((128, 2048), BF16)]
        + [VMEM((256, 256), BF16)] * 2,
        copies=6, flops=2 * 10**9, bytes_accessed=2 << 20, name="to_grid", room=63,
    )
    planes = lax.all_to_all(sent.reshape(256, 4, 128), BOTH, split_axis=0, concat_axis=0, tiled=True)
    masked = call(turn, shape(256, 128), (block_count, cells, token), "svv", bytes_accessed=1 << 20, name="turn", room=16)
    before, after = neighbours(masked, "wide", W)
    own = call(join, shape(768, 128), (before, masked, after), "vvv", bytes_accessed=2 << 20, name="join", room=16)
    left, right = neighbours(own, "narrow", N)
    back = call(
        convolve, shape(1024, 128),
        (planes.reshape(1024, 128), green_hat.reshape(2, 512, 512), yh, yl, xh, xl, ih, il), "hhhhhhhh",
        scratch=[VMEM((1024, 128), F32), VMEM((2, 512, 512), F32)] + [VMEM((2, 256, 512), BF16)] * 2 + [VMEM((2, 512, 256), BF16)] * 2
        + [VMEM((2, 256, 512), BF16)] * 2 + [VMEM((2, 256, 256), BF16)] * 2 + [VMEM((2, 256, 512), BF16)] * 2
        + [VMEM((2, 512, 512), BF16)] * 2 + [VMEM((2, 256, 512), BF16)] * 2,
        copies=8, flops=5 * 10**9, bytes_accessed=9 << 20, name="convolve", room=63,
    )
    back, left, right = lax.optimization_barrier((back, left, right))
    field = lax.all_to_all(back.reshape(256, 4, 128), BOTH, split_axis=0, concat_axis=0, tiled=True)
    step_wide, step_narrow, slot = near_source // 768, near_source // 256 % 3, near_source % 256
    index = (step_narrow * 768 + step_wide * 256 + slot).reshape(CLASSES * 256)
    beside = call(
        near, shape(128, 256), (index, left, own, right, near_table), "svvvv",
        scratch=[VMEM((2304, 128), F32), VMEM((CLASSES, 256, 128), F32)],
        flops=10**10, bytes_accessed=40 << 20, name="near", room=16,
    )
    result = call(
        from_grid, shape(128, 256),
        (block_count, site, field.reshape(1024, 128), projection, expand, izh, izl, beside), "svvvvvvv",
        flops=2 * 10**9, bytes_accessed=2 << 20, name="from_grid", room=12,
    )
    return result.reshape(2, 64, 256)


def solution(mesh):
    placed = (
        P(None, None, BOTH),
        P(),
        P(None, BOTH, None, None),
        P(),
        P(BOTH),
        P(BOTH),
        P(None, BOTH),
    )
    return jax.shard_map(
        per_device,
        mesh=mesh,
        in_specs=placed,
        out_specs=P(None, None, BOTH),
        check_vma=False,
    )
```

```python
import numpy as np

import jax
import jax.numpy as jnp
from jax import lax
from jax.experimental import pallas as pl
from jax.experimental.pallas import tpu as pltpu
from jax.sharding import PartitionSpec as P

W = 64
N = 4
F32 = jnp.float32
BF16 = jnp.bfloat16
VMEM = pltpu.VMEM
BOTH = ("wide", "narrow")


def halves(table):
    high = table.astype(jnp.bfloat16)
    low = (table - high.astype(np.float64)).astype(jnp.bfloat16)
    return high, low


def split(value):
    high = value.astype(BF16)
    return high, (value - high.astype(F32)).astype(BF16)


def dot(left, right):
    return lax.dot_general(left, right, (((1,), (0,)), ((), ())), preferred_element_type=F32)


def dot_t(left, right):
    return lax.dot_general(left, right, (((1,), (1,)), ((), ())), preferred_element_type=F32)


def dot3(lh, ll, rh, rl):
    return dot(lh, rh) + (dot(lh, rl) + dot(ll, rh))


def tables():
    z = np.arange(128)
    z_of = 4 * (z % 32) + z // 32
    kz = np.arange(256)
    ang = 2 * np.pi * ((kz[:, None] * z_of[None, :]) % 256) / 256
    forward_z = np.concatenate([np.cos(ang), np.sin(ang)], 1)
    inverse_z = np.concatenate([np.cos(ang).T, -np.sin(ang).T], 1) * 2.0**-26
    lane = np.arange(2048)
    group, inner = lane // 128, lane % 128
    ez, ex = group // 4, group % 4
    r, ey = inner // 64, inner // 16 % 2 * 2 + inner // 32 % 2
    row = r * 64 + 16 * ex + 4 * ey + ez
    expand = (np.arange(128)[:, None] == row[None, :]).astype(np.float32)
    k = np.arange(256)
    i = np.arange(256)
    real = (i // 64 % 2 == 0)[:, None]
    along = []
    for p in range(2):
        y = 64 * (i // 128 * 2 + i // 32 % 2) + 4 * (i % 16) + 2 * (i // 16 % 2) + p
        ang = 2 * np.pi * ((y[:, None] * k[None, :]) % 512) / 512
        c, s = np.cos(ang), np.sin(ang)
        along.append(np.concatenate([np.where(real, c, s), np.where(real, -s, c)], 1))
    across = []
    j = np.arange(128)
    for p in range(2):
        x = 4 * (j % 64) + 2 * (j // 64) + p
        ang = 2 * np.pi * ((k[:, None] * x[None, :]) % 512) / 512
        c, s = np.cos(ang), np.sin(ang)
        across.append(np.block([[c, s], [-s, c]]))
    return forward_z, inverse_z, expand, np.stack(along), np.stack(across)


def swap(value):
    lanes = value.shape[1]
    rolled = jnp.concatenate(
        [pltpu.roll(value[:, i : i + 128], 64, 1) for i in range(0, lanes, 128)], axis=1
    )
    sign = jnp.where(lax.broadcasted_iota(jnp.int32, (1, lanes), 1) % 128 < 64, 1.0, -1.0)
    return rolled * sign


def site_masks(count, site):
    rows = lax.broadcasted_iota(jnp.int32, (32, 256), 0)
    line = jnp.where(rows == site % 32, 1.0, 0.0)
    lanes = lax.broadcasted_iota(jnp.int32, (128, 256), 0)
    slots = lax.broadcasted_iota(jnp.int32, (128, 256), 1)
    plane = jnp.where((lanes % 16 == site // 32) & (slots < count), 1.0, 0.0)
    return line, plane.T


def fetch(pairs, sems):
    copies = [pltpu.make_async_copy(s, d, sems.at[i]) for i, (s, d) in enumerate(pairs)]
    for copy in copies:
        copy.start()
    return copies


def to_grid(count_ref, charges_any, site_any, proj_any, expand_any, fh_any, fl_any, out_ref, token_ref,
            charges_ref, site_ref, proj_ref, expand_ref, fh_ref, fl_ref, sems):
    copies = fetch(
        [(charges_any, charges_ref), (proj_any, proj_ref), (site_any, site_ref),
         (expand_any, expand_ref), (fh_any, fh_ref), (fl_any, fl_ref)], sems)
    token_ref[...] = jnp.zeros((8, 128), F32)
    count = count_ref[0]
    slots = lax.broadcasted_iota(jnp.int32, (128, 256), 1)
    for copy in copies[:3]:
        copy.wait()
    line, plane = site_masks(count, site_ref[...])
    turned = jnp.where(slots < count, charges_ref[...], 0.0).T
    ph, plo = split(proj_ref[...])
    parts = []
    for r in range(2):
        mh, ml = split(turned[:, 64 * r : 64 * r + 64])
        parts.append(dot_t(mh, ph) + (dot_t(mh, plo) + dot_t(ml, ph)))
    both = jnp.concatenate(split(jnp.concatenate(parts, axis=1)), axis=0)
    plane = jnp.concatenate([plane, plane], axis=1)
    line = line.astype(BF16)
    line = jnp.concatenate([line, line], axis=1)
    copies[3].wait()
    rows = []
    for ez in range(4):
        cols = []
        for e in range(2):
            lo = (ez * 4 + 2 * e) * 128
            spread = dot(both, expand_ref[:, lo : lo + 256])
            high = (spread[:256] * plane).astype(BF16)
            low = (spread[256:] * plane).astype(BF16)
            cols.append(dot(line, jnp.concatenate([high, low], axis=0)))
        rows.append(jnp.concatenate(cols, axis=1))
    grid = jnp.concatenate(rows, axis=0)
    gh, gl = split(jnp.concatenate([grid, swap(grid)], axis=0))
    copies[4].wait()
    copies[5].wait()
    for e in range(2):
        c = slice(256 * e, 256 * e + 256)
        planes = dot3(fh_ref[...], fl_ref[...], gh[:, c], gl[:, c])
        out_ref[pl.ds(2 * e, 256, stride=4), :] = planes[:, :128]
        out_ref[pl.ds(2 * e + 1, 256, stride=4), :] = planes[:, 128:]


def turn(count_ref, charges_ref, after_ref, out_ref):
    slots = lax.broadcasted_iota(jnp.int32, (128, 256), 1)
    out_ref[...] = jnp.where(slots < count_ref[0], charges_ref[...], 0.0).T


def join(a_ref, b_ref, c_ref, out_ref):
    for i, ref in enumerate((a_ref, b_ref, c_ref)):
        out_ref[256 * i : 256 * i + 256, :] = ref[...]


def convolve(in_any, green_any, yh_any, yl_any, xh_any, xl_any, ih_any, il_any, out_ref,
             in_ref, green_ref, yh, yl, xh, xl, ih, il, ah, al, sh, sl, qh, ql, bh, bl, sems):
    (arrived,) = fetch([(in_any, in_ref)], sems)
    copies = fetch(
        [(yh_any, yh), (yl_any, yl), (xh_any, xh), (xl_any, xl), (green_any, green_ref), (ih_any, ih), (il_any, il)],
        sems.at[pl.ds(1, 7)])
    arrived.wait()
    first = lax.broadcasted_iota(jnp.int32, (64, 128), 1) % 64 < 32
    order = (0, 2, 1, 3)
    for i, ex in enumerate(order):
        a = slice(64 * i, 64 * i + 64)
        for m in range(2):
            c = slice(128 * m, 128 * m + 128)
            d0 = in_ref[pl.ds(8 * m + ex, 64, stride=16), :]
            d1 = in_ref[pl.ds(8 * m + 4 + ex, 64, stride=16), :]
            ah[0, a, c], al[0, a, c] = split(jnp.where(first, d0, pltpu.roll(d1, 32, 1)))
            ah[1, a, c], al[1, a, c] = split(jnp.where(first, pltpu.roll(d0, 96, 1), d1))
    copies[0].wait()
    copies[1].wait()
    for xp in range(2):
        a = slice(128 * xp, 128 * xp + 128)
        for r in range(2):
            c = slice(256 * r, 256 * r + 256)
            even = dot3(ah[0, a, :], al[0, a, :], yh[0, :, c], yl[0, :, c])
            odd = dot3(ah[1, a, :], al[1, a, :], yh[1, :, c], yl[1, :, c])
            o = slice(128 * r, 128 * r + 128)
            sh[xp, o, 0:256], sl[xp, o, 0:256] = split(even + odd)
            sh[xp, o, 256:512], sl[xp, o, 256:512] = split(even - odd)
    copies[2].wait()
    copies[3].wait()
    copies[4].wait()
    for j in range(2):
        c = slice(256 * j, 256 * j + 256)
        for i in range(2):
            lo = slice(128 * i, 128 * i + 128)
            hi = slice(256 + 128 * i, 384 + 128 * i)
            part = [[dot3(xh[xp, a, :], xl[xp, a, :], sh[xp, :, c], sl[xp, :, c]) for xp in range(2)] for a in (lo, hi)]
            (re0, re1), (im0, im1) = part
            re, im = re0 + re1, im0 + im1
            gr, gi = green_ref[0, lo, c], green_ref[1, lo, c]
            p_re, p_im = gr * re - gi * im, gr * im + gi * re
            re, im = re0 - re1, im0 - im1
            gr, gi = green_ref[0, hi, c], green_ref[1, hi, c]
            q_re, q_im = gr * re - gi * im, gr * im + gi * re
            qh[0, lo, c], ql[0, lo, c] = split(p_re + q_re)
            qh[1, lo, c], ql[1, lo, c] = split(p_re - q_re)
            qh[0, hi, c], ql[0, hi, c] = split(p_im + q_im)
            qh[1, hi, c], ql[1, hi, c] = split(p_im - q_im)
    copies[5].wait()
    copies[6].wait()
    for xp in range(2):
        for r in range(2):
            a = slice(128 * r, 128 * r + 128)
            u0, u1 = [
                dot3(ih[xp, a, :], il[xp, a, :], qh[xp, :, c], ql[xp, :, c]) for c in (slice(0, 256), slice(256, 512))
            ]
            rows, o = slice(128 * xp, 128 * xp + 128), slice(256 * r, 256 * r + 256)
            bh[0, rows, o], bl[0, rows, o] = split(u0 + u1)
            bh[1, rows, o], bl[1, rows, o] = split(u0 - u1)
    for xp in range(2):
        a = slice(128 * xp, 128 * xp + 128)
        even, odd = [
            dot_t(bh[p, a, :], yh[p]) + (dot_t(bh[p, a, :], yl[p]) + dot_t(bl[p, a, :], yh[p])) for p in range(2)
        ]
        for e in range(2):
            ex = order[2 * xp + e]
            rows = slice(64 * e, 64 * e + 64)
            for m in range(2):
                c = slice(128 * m, 128 * m + 128)
                ve, vo = even[rows, c], odd[rows, c]
                out_ref[pl.ds(8 * m + ex, 64, stride=16), :] = jnp.where(first, ve, pltpu.roll(vo, 32, 1))
                out_ref[pl.ds(8 * m + 4 + ex, 64, stride=16), :] = jnp.where(first, pltpu.roll(ve, 96, 1), vo)


def from_grid(count_ref, site_ref, in_ref, proj_ref, expand_ref, fh_ref, fl_ref, near_ref, out_ref):
    count = count_ref[0]
    line, plane = site_masks(count, site_ref[...])
    field = jnp.concatenate([in_ref[pl.ds(ex, 256, stride=4), :] for ex in range(4)], axis=1)
    vh, vl = split(jnp.concatenate([field, swap(field)], axis=0))
    points = dot3(fh_ref[...], fl_ref[...], vh, vl)
    bh, bl = split(points)
    pick = line.T.astype(BF16)
    total = jnp.zeros((256, 128), F32)
    for ez in range(4):
        rows = slice(32 * ez, 32 * ez + 32)
        for ex in range(4):
            c = slice(128 * ex, 128 * ex + 128)
            high = (dot(pick, bh[rows, c]) * plane).astype(BF16)
            low = (dot(pick, bl[rows, c]) * plane).astype(BF16)
            lo = (ez * 4 + ex) * 128
            e = expand_ref[:, lo : lo + 128]
            total = total + (dot_t(high, e) + dot_t(low, e))
    th, tl = split(total)
    ph, plo = split(proj_ref[...])
    parts = []
    for r in range(2):
        c = slice(64 * r, 64 * r + 64)
        parts.append(dot3(th[:, c], tl[:, c], ph, plo))
    far = jnp.concatenate(parts, axis=1).T
    slots = lax.broadcasted_iota(jnp.int32, (128, 256), 1)
    out_ref[...] = far + jnp.where(slots < count, near_ref[...], 0.0)


CLASSES = 27


def near(index_ref, left_ref, own_ref, right_ref, table_ref, out_ref, source_ref, picked):
    for i, ref in enumerate((left_ref, own_ref, right_ref)):
        source_ref[768 * i : 768 * i + 768, :] = ref[...]

    def one(k, carry):
        for b in range(256):
            i = index_ref[k * 256 + b]
            picked[k, pl.ds(b, 1), :] = source_ref[pl.ds(i, 1), :]
        return carry

    lax.fori_loop(0, CLASSES, one, 0)
    total = jnp.zeros((256, 128), F32)
    for k in range(CLASSES):
        gh, gl = split(picked[k])
        re, im = table_ref[k, 0], table_ref[k, 1]
        rows = [jnp.concatenate([re, -im], axis=1), jnp.concatenate([im, re], axis=1)]
        th, tl = split(jnp.concatenate(rows, axis=0))
        total = total + (dot_t(gh, th) + (dot_t(gh, tl) + dot_t(gl, th)))
    out_ref[...] = total.T


def call(kernel, outs, args, kinds, scratch=(), copies=0, flops=0, bytes_accessed=0, name=None, out_kind="v", room=40):
    spaces = {"s": pltpu.SMEM, "v": VMEM, "h": pltpu.HBM}
    single = not isinstance(outs, (tuple, list))
    out_spec = pl.BlockSpec(memory_space=spaces[out_kind])
    scratch = list(scratch) + ([pltpu.SemaphoreType.DMA((copies,))] if copies else [])
    return pl.pallas_call(
        kernel,
        out_shape=outs,
        in_specs=[pl.BlockSpec(memory_space=spaces[k]) for k in kinds],
        out_specs=out_spec if single else tuple(out_spec for _ in outs),
        scratch_shapes=scratch,
        compiler_params=pltpu.CompilerParams(vmem_limit_bytes=room << 20),
        cost_estimate=pl.CostEstimate(flops=flops, bytes_accessed=bytes_accessed, transcendentals=0),
        name=name,
    )(*args)


def neighbours(array, axis, size):
    up = [(i, i + 1) for i in range(size - 1)]
    down = [(i + 1, i) for i in range(size - 1)]
    return lax.ppermute(array, axis, up), lax.ppermute(array, axis, down)


def per_device(charges, projection, green_hat, near_table, block_site, block_count, near_source):
    forward_z, inverse_z, expand, along, across = tables()
    fzh, fzl = halves(forward_z)
    izh, izl = halves(inverse_z)
    yh, yl = halves(along)
    xh, xl = halves(across)
    ih, il = halves(np.ascontiguousarray(across.transpose(0, 2, 1)))
    expand = expand.astype(jnp.bfloat16)
    site = block_site.reshape(1, 256)
    shape = lambda *s: jax.ShapeDtypeStruct(s, F32)

    cells = charges.reshape(128, 256)
    sent, token = call(
        to_grid, (shape(1024, 128), shape(8, 128)), (block_count, cells, site, projection, expand, fzh, fzl), "shhhhhh",
        scratch=[VMEM((128, 256), F32), VMEM((1, 256), jnp.int32), VMEM((64, 64), F32), VMEM((128, 2048), BF16)]
        + [VMEM((256, 256), BF16)] * 2,
        copies=6, flops=2 * 10**9, bytes_accessed=2 << 20, name="to_grid", room=63,
    )
    planes = lax.all_to_all(sent.reshape(256, 4, 128), BOTH, split_axis=0, concat_axis=0, tiled=True)
    masked = call(turn, shape(256, 128), (block_count, cells, token), "svv", bytes_accessed=1 << 20, name="turn", room=16)
    before, after = neighbours(masked, "narrow", N)
    own = call(join, shape(768, 128), (before, masked, after), "vvv", bytes_accessed=2 << 20, name="join", room=16)
    left, right = neighbours(own, "wide", W)
    back = call(
        convolve, shape(1024, 128),
        (planes.reshape(1024, 128), green_hat.reshape(2, 512, 512), yh, yl, xh, xl, ih, il), "hhhhhhhh",
        scratch=[VMEM((1024, 128), F32), VMEM((2, 512, 512), F32)] + [VMEM((2, 256, 512), BF16)] * 2 + [VMEM((2, 512, 256), BF16)] * 2
        + [VMEM((2, 256, 512), BF16)] * 2 + [VMEM((2, 256, 256), BF16)] * 2 + [VMEM((2, 256, 512), BF16)] * 2
        + [VMEM((2, 512, 512), BF16)] * 2 + [VMEM((2, 256, 512), BF16)] * 2,
        copies=8, flops=5 * 10**9, bytes_accessed=9 << 20, name="convolve", room=63,
    )
    field = lax.all_to_all(back.reshape(256, 4, 128), BOTH, split_axis=0, concat_axis=0, tiled=True)
    index = near_source.reshape(CLASSES * 256)
    beside = call(
        near, shape(128, 256), (index, left, own, right, near_table), "svvvv",
        scratch=[VMEM((2304, 128), F32), VMEM((CLASSES, 256, 128), F32)],
        flops=10**10, bytes_accessed=40 << 20, name="near", room=16,
    )
    result = call(
        from_grid, shape(128, 256),
        (block_count, site, field.reshape(1024, 128), projection, expand, izh, izl, beside), "svvvvvvv",
        flops=2 * 10**9, bytes_accessed=2 << 20, name="from_grid", room=12,
    )
    return result.reshape(2, 64, 256)


def solution(mesh):
    placed = (
        P(None, None, BOTH),
        P(),
        P(None, BOTH, None, None),
        P(),
        P(BOTH),
        P(BOTH),
        P(None, BOTH),
    )
    return jax.shard_map(
        per_device,
        mesh=mesh,
        in_specs=placed,
        out_specs=P(None, None, BOTH),
        check_vma=False,
    )
```

```python
import numpy as np

import jax
import jax.numpy as jnp
from jax import lax
from jax.experimental import pallas as pl
from jax.experimental.pallas import tpu as pltpu
from jax.sharding import PartitionSpec as P

W = 64
N = 4
F32 = jnp.float32
BF16 = jnp.bfloat16
VMEM = pltpu.VMEM
BOTH = ("wide", "narrow")


def halves(table):
    high = table.astype(jnp.bfloat16)
    low = (table - high.astype(np.float64)).astype(jnp.bfloat16)
    return high, low


def split(value):
    high = value.astype(BF16)
    return high, (value - high.astype(F32)).astype(BF16)


def dot(left, right):
    return lax.dot_general(left, right, (((1,), (0,)), ((), ())), preferred_element_type=F32)


def dot_t(left, right):
    return lax.dot_general(left, right, (((1,), (1,)), ((), ())), preferred_element_type=F32)


def dot3(lh, ll, rh, rl):
    return dot(lh, rh) + (dot(lh, rl) + dot(ll, rh))


def tables():
    z = np.arange(128)
    z_of = 4 * (z % 32) + z // 32
    kz = np.arange(256)
    ang = 2 * np.pi * ((kz[:, None] * z_of[None, :]) % 256) / 256
    forward_z = np.concatenate([np.cos(ang), np.sin(ang)], 1)
    inverse_z = np.concatenate([np.cos(ang).T, -np.sin(ang).T], 1) * 2.0**-26
    lane = np.arange(2048)
    group, inner = lane // 128, lane % 128
    ez, ex = group // 4, group % 4
    r, ey = inner // 64, inner // 16 % 2 * 2 + inner // 32 % 2
    row = r * 64 + 16 * ex + 4 * ey + ez
    expand = (np.arange(128)[:, None] == row[None, :]).astype(np.float32)
    k = np.arange(256)
    i = np.arange(256)
    real = (i // 64 % 2 == 0)[:, None]
    along = []
    for p in range(2):
        y = 64 * (i // 128 * 2 + i // 32 % 2) + 4 * (i % 16) + 2 * (i // 16 % 2) + p
        ang = 2 * np.pi * ((y[:, None] * k[None, :]) % 512) / 512
        c, s = np.cos(ang), np.sin(ang)
        along.append(np.concatenate([np.where(real, c, s), np.where(real, -s, c)], 1))
    across = []
    j = np.arange(128)
    for p in range(2):
        x = 4 * (j % 64) + 2 * (j // 64) + p
        ang = 2 * np.pi * ((k[:, None] * x[None, :]) % 512) / 512
        c, s = np.cos(ang), np.sin(ang)
        across.append(np.block([[c, s], [-s, c]]))
    return forward_z, inverse_z, expand, np.stack(along), np.stack(across)


def swap(value):
    lanes = value.shape[1]
    rolled = jnp.concatenate(
        [pltpu.roll(value[:, i : i + 128], 64, 1) for i in range(0, lanes, 128)], axis=1
    )
    sign = jnp.where(lax.broadcasted_iota(jnp.int32, (1, lanes), 1) % 128 < 64, 1.0, -1.0)
    return rolled * sign


def site_masks(count, site):
    rows = lax.broadcasted_iota(jnp.int32, (32, 256), 0)
    line = jnp.where(rows == site % 32, 1.0, 0.0)
    lanes = lax.broadcasted_iota(jnp.int32, (128, 256), 0)
    slots = lax.broadcasted_iota(jnp.int32, (128, 256), 1)
    plane = jnp.where((lanes % 16 == site // 32) & (slots < count), 1.0, 0.0)
    return line, plane.T


def fetch(pairs, sems):
    copies = [pltpu.make_async_copy(s, d, sems.at[i]) for i, (s, d) in enumerate(pairs)]
    for copy in copies:
        copy.start()
    return copies


def to_grid(count_ref, charges_any, site_any, proj_any, expand_any, fh_any, fl_any, out_ref, token_ref,
            charges_ref, site_ref, proj_ref, expand_ref, fh_ref, fl_ref, sems):
    copies = fetch(
        [(charges_any, charges_ref), (proj_any, proj_ref), (site_any, site_ref),
         (expand_any, expand_ref), (fh_any, fh_ref), (fl_any, fl_ref)], sems)
    token_ref[...] = jnp.zeros((8, 128), F32)
    count = count_ref[0]
    slots = lax.broadcasted_iota(jnp.int32, (128, 256), 1)
    for copy in copies[:3]:
        copy.wait()
    line, plane = site_masks(count, site_ref[...])
    turned = jnp.where(slots < count, charges_ref[...], 0.0).T
    ph, plo = split(proj_ref[...])
    parts = []
    for r in range(2):
        mh, ml = split(turned[:, 64 * r : 64 * r + 64])
        parts.append(dot_t(mh, ph) + (dot_t(mh, plo) + dot_t(ml, ph)))
    both = jnp.concatenate(split(jnp.concatenate(parts, axis=1)), axis=0)
    plane = jnp.concatenate([plane, plane], axis=1)
    line = line.astype(BF16)
    line = jnp.concatenate([line, line], axis=1)
    copies[3].wait()
    rows = []
    for ez in range(4):
        cols = []
        for e in range(2):
            lo = (ez * 4 + 2 * e) * 128
            spread = dot(both, expand_ref[:, lo : lo + 256])
            high = (spread[:256] * plane).astype(BF16)
            low = (spread[256:] * plane).astype(BF16)
            cols.append(dot(line, jnp.concatenate([high, low], axis=0)))
        rows.append(jnp.concatenate(cols, axis=1))
    grid = jnp.concatenate(rows, axis=0)
    gh, gl = split(jnp.concatenate([grid, swap(grid)], axis=0))
    copies[4].wait()
    copies[5].wait()
    for e in range(2):
        c = slice(256 * e, 256 * e + 256)
        planes = dot3(fh_ref[...], fl_ref[...], gh[:, c], gl[:, c])
        out_ref[pl.ds(2 * e, 256, stride=4), :] = planes[:, :128]
        out_ref[pl.ds(2 * e + 1, 256, stride=4), :] = planes[:, 128:]


def turn(count_ref, charges_ref, after_ref, out_ref):
    slots = lax.broadcasted_iota(jnp.int32, (128, 256), 1)
    out_ref[...] = jnp.where(slots < count_ref[0], charges_ref[...], 0.0).T


def join(a_ref, b_ref, c_ref, out_ref):
    for i, ref in enumerate((a_ref, b_ref, c_ref)):
        out_ref[256 * i : 256 * i + 256, :] = ref[...]


def convolve(in_any, green_any, yh_any, yl_any, xh_any, xl_any, ih_any, il_any, out_ref,
             in_ref, green_ref, yh, yl, xh, xl, ih, il, ah, al, sh, sl, qh, ql, bh, bl, sems):
    (arrived,) = fetch([(in_any, in_ref)], sems)
    copies = fetch(
        [(yh_any, yh), (yl_any, yl), (xh_any, xh), (xl_any, xl), (green_any, green_ref), (ih_any, ih), (il_any, il)],
        sems.at[pl.ds(1, 7)])
    arrived.wait()
    first = lax.broadcasted_iota(jnp.int32, (64, 128), 1) % 64 < 32
    order = (0, 2, 1, 3)
    for i, ex in enumerate(order):
        a = slice(64 * i, 64 * i + 64)
        for m in range(2):
            c = slice(128 * m, 128 * m + 128)
            d0 = in_ref[pl.ds(8 * m + ex, 64, stride=16), :]
            d1 = in_ref[pl.ds(8 * m + 4 + ex, 64, stride=16), :]
            ah[0, a, c], al[0, a, c] = split(jnp.where(first, d0, pltpu.roll(d1, 32, 1)))
            ah[1, a, c], al[1, a, c] = split(jnp.where(first, pltpu.roll(d0, 96, 1), d1))
    copies[0].wait()
    copies[1].wait()
    for r in range(2):
        c = slice(256 * r, 256 * r + 256)
        o = slice(128 * r, 128 * r + 128)
        even = dot3(ah[0], al[0], yh[0, :, c], yl[0, :, c])
        odd = dot3(ah[1], al[1], yh[1, :, c], yl[1, :, c])
        for half, (h, l) in enumerate((split(even + odd), split(even - odd))):
            k = slice(256 * half, 256 * half + 256)
            for xp in range(2):
                sh[xp, o, k] = h[128 * xp : 128 * xp + 128]
                sl[xp, o, k] = l[128 * xp : 128 * xp + 128]
    copies[2].wait()
    copies[3].wait()
    copies[4].wait()
    for j in range(2):
        c = slice(256 * j, 256 * j + 256)
        part = [dot3(xh[xp], xl[xp], sh[xp, :, c], sl[xp, :, c]) for xp in range(2)]
        sums, diffs = part[0] + part[1], part[0] - part[1]
        gr, gi = green_ref[0, 0:256, c], green_ref[1, 0:256, c]
        p_re, p_im = gr * sums[:256] - gi * sums[256:], gr * sums[256:] + gi * sums[:256]
        gr, gi = green_ref[0, 256:512, c], green_ref[1, 256:512, c]
        q_re, q_im = gr * diffs[:256] - gi * diffs[256:], gr * diffs[256:] + gi * diffs[:256]
        qh[0, 0:256, c], ql[0, 0:256, c] = split(p_re + q_re)
        qh[1, 0:256, c], ql[1, 0:256, c] = split(p_re - q_re)
        qh[0, 256:512, c], ql[0, 256:512, c] = split(p_im + q_im)
        qh[1, 256:512, c], ql[1, 256:512, c] = split(p_im - q_im)
    copies[5].wait()
    copies[6].wait()
    for xp in range(2):
        u0, u1 = [dot3(ih[xp], il[xp], qh[xp, :, c], ql[xp, :, c]) for c in (slice(0, 256), slice(256, 512))]
        rows = slice(128 * xp, 128 * xp + 128)
        for p, (h, l) in enumerate((split(u0 + u1), split(u0 - u1))):
            for r in range(2):
                bh[p, rows, 256 * r : 256 * r + 256] = h[128 * r : 128 * r + 128]
                bl[p, rows, 256 * r : 256 * r + 256] = l[128 * r : 128 * r + 128]
    even, odd = [dot_t(bh[p], yh[p]) + (dot_t(bh[p], yl[p]) + dot_t(bl[p], yh[p])) for p in range(2)]
    for e, ex in enumerate(order):
        rows = slice(64 * e, 64 * e + 64)
        for m in range(2):
            c = slice(128 * m, 128 * m + 128)
            ve, vo = even[rows, c], odd[rows, c]
            out_ref[pl.ds(8 * m + ex, 64, stride=16), :] = jnp.where(first, ve, pltpu.roll(vo, 32, 1))
            out_ref[pl.ds(8 * m + 4 + ex, 64, stride=16), :] = jnp.where(first, pltpu.roll(ve, 96, 1), vo)


def from_grid(count_ref, site_ref, in_ref, proj_ref, expand_ref, fh_ref, fl_ref, near_ref, out_ref):
    count = count_ref[0]
    line, plane = site_masks(count, site_ref[...])
    field = jnp.concatenate([in_ref[pl.ds(ex, 256, stride=4), :] for ex in range(4)], axis=1)
    vh, vl = split(jnp.concatenate([field, swap(field)], axis=0))
    points = dot3(fh_ref[...], fl_ref[...], vh, vl)
    bh, bl = split(points)
    pick = line.T.astype(BF16)
    total = jnp.zeros((256, 128), F32)
    for ez in range(4):
        rows = slice(32 * ez, 32 * ez + 32)
        for ex in range(4):
            c = slice(128 * ex, 128 * ex + 128)
            high = (dot(pick, bh[rows, c]) * plane).astype(BF16)
            low = (dot(pick, bl[rows, c]) * plane).astype(BF16)
            lo = (ez * 4 + ex) * 128
            e = expand_ref[:, lo : lo + 128]
            total = total + (dot_t(high, e) + dot_t(low, e))
    th, tl = split(total)
    ph, plo = split(proj_ref[...])
    parts = []
    for r in range(2):
        c = slice(64 * r, 64 * r + 64)
        parts.append(dot3(th[:, c], tl[:, c], ph, plo))
    far = jnp.concatenate(parts, axis=1).T
    slots = lax.broadcasted_iota(jnp.int32, (128, 256), 1)
    out_ref[...] = far + jnp.where(slots < count, near_ref[...], 0.0)


CLASSES = 27


def near(index_ref, left_ref, own_ref, right_ref, table_ref, out_ref, source_ref, picked):
    for i, ref in enumerate((left_ref, own_ref, right_ref)):
        source_ref[768 * i : 768 * i + 768, :] = ref[...]

    def one(k, carry):
        for b in range(256):
            i = index_ref[k * 256 + b]
            picked[k, pl.ds(b, 1), :] = source_ref[pl.ds(i, 1), :]
        return carry

    lax.fori_loop(0, CLASSES, one, 0)
    total = jnp.zeros((256, 128), F32)
    for k in range(CLASSES):
        gh, gl = split(picked[k])
        re, im = table_ref[k, 0], table_ref[k, 1]
        rows = [jnp.concatenate([re, -im], axis=1), jnp.concatenate([im, re], axis=1)]
        th, tl = split(jnp.concatenate(rows, axis=0))
        total = total + (dot_t(gh, th) + (dot_t(gh, tl) + dot_t(gl, th)))
    out_ref[...] = total.T


def call(kernel, outs, args, kinds, scratch=(), copies=0, flops=0, bytes_accessed=0, name=None, out_kind="v", room=40):
    spaces = {"s": pltpu.SMEM, "v": VMEM, "h": pltpu.HBM}
    single = not isinstance(outs, (tuple, list))
    out_spec = pl.BlockSpec(memory_space=spaces[out_kind])
    scratch = list(scratch) + ([pltpu.SemaphoreType.DMA((copies,))] if copies else [])
    return pl.pallas_call(
        kernel,
        out_shape=outs,
        in_specs=[pl.BlockSpec(memory_space=spaces[k]) for k in kinds],
        out_specs=out_spec if single else tuple(out_spec for _ in outs),
        scratch_shapes=scratch,
        compiler_params=pltpu.CompilerParams(vmem_limit_bytes=room << 20),
        cost_estimate=pl.CostEstimate(flops=flops, bytes_accessed=bytes_accessed, transcendentals=0),
        name=name,
    )(*args)


def neighbours(array, axis, size):
    up = [(i, i + 1) for i in range(size - 1)]
    down = [(i + 1, i) for i in range(size - 1)]
    return lax.ppermute(array, axis, up), lax.ppermute(array, axis, down)


def per_device(charges, projection, green_hat, near_table, block_site, block_count, near_source):
    forward_z, inverse_z, expand, along, across = tables()
    fzh, fzl = halves(forward_z)
    izh, izl = halves(inverse_z)
    yh, yl = halves(along)
    xh, xl = halves(across)
    ih, il = halves(np.ascontiguousarray(across.transpose(0, 2, 1)))
    expand = expand.astype(jnp.bfloat16)
    site = block_site.reshape(1, 256)
    shape = lambda *s: jax.ShapeDtypeStruct(s, F32)

    cells = charges.reshape(128, 256)
    sent, token = call(
        to_grid, (shape(1024, 128), shape(8, 128)), (block_count, cells, site, projection, expand, fzh, fzl), "shhhhhh",
        scratch=[VMEM((128, 256), F32), VMEM((1, 256), jnp.int32), VMEM((64, 64), F32), VMEM((128, 2048), BF16)]
        + [VMEM((256, 256), BF16)] * 2,
        copies=6, flops=2 * 10**9, bytes_accessed=2 << 20, name="to_grid", room=63,
    )
    planes = lax.all_to_all(sent.reshape(256, 4, 128), BOTH, split_axis=0, concat_axis=0, tiled=True)
    masked = call(turn, shape(256, 128), (block_count, cells, token), "svv", bytes_accessed=1 << 20, name="turn", room=16)
    before, after = neighbours(masked, "narrow", N)
    own = call(join, shape(768, 128), (before, masked, after), "vvv", bytes_accessed=2 << 20, name="join", room=16)
    left, _ = neighbours(own, "wide", W)
    later, planes = lax.optimization_barrier((own, planes))
    _, right = neighbours(later, "wide", W)
    back = call(
        convolve, shape(1024, 128),
        (planes.reshape(1024, 128), green_hat.reshape(2, 512, 512), yh, yl, xh, xl, ih, il), "hhhhhhhh",
        scratch=[VMEM((1024, 128), F32), VMEM((2, 512, 512), F32)] + [VMEM((2, 256, 512), BF16)] * 2 + [VMEM((2, 512, 256), BF16)] * 2
        + [VMEM((2, 256, 512), BF16)] * 2 + [VMEM((2, 256, 256), BF16)] * 2 + [VMEM((2, 256, 512), BF16)] * 2
        + [VMEM((2, 512, 512), BF16)] * 2 + [VMEM((2, 256, 512), BF16)] * 2,
        copies=8, flops=5 * 10**9, bytes_accessed=9 << 20, name="convolve", room=63,
    )
    field = lax.all_to_all(back.reshape(256, 4, 128), BOTH, split_axis=0, concat_axis=0, tiled=True)
    index = near_source.reshape(CLASSES * 256)
    beside = call(
        near, shape(128, 256), (index, left, own, right, near_table), "svvvv",
        scratch=[VMEM((2304, 128), F32), VMEM((CLASSES, 256, 128), F32)],
        flops=10**10, bytes_accessed=40 << 20, name="near", room=16,
    )
    result = call(
        from_grid, shape(128, 256),
        (block_count, site, field.reshape(1024, 128), projection, expand, izh, izl, beside), "svvvvvvv",
        flops=2 * 10**9, bytes_accessed=2 << 20, name="from_grid", room=12,
    )
    return result.reshape(2, 64, 256)


def solution(mesh):
    placed = (
        P(None, None, BOTH),
        P(),
        P(None, BOTH, None, None),
        P(),
        P(BOTH),
        P(BOTH),
        P(None, BOTH),
    )
    return jax.shard_map(
        per_device,
        mesh=mesh,
        in_specs=placed,
        out_specs=P(None, None, BOTH),
        check_vma=False,
    )
```

```python
import numpy as np

import jax
import jax.numpy as jnp
from jax import lax
from jax.experimental import pallas as pl
from jax.experimental.pallas import tpu as pltpu
from jax.sharding import PartitionSpec as P

W = 64
N = 4
F32 = jnp.float32
BF16 = jnp.bfloat16
VMEM = pltpu.VMEM
BOTH = ("wide", "narrow")


def halves(table):
    high = table.astype(jnp.bfloat16)
    low = (table - high.astype(np.float64)).astype(jnp.bfloat16)
    return high, low


def split(value):
    high = value.astype(BF16)
    return high, (value - high.astype(F32)).astype(BF16)


def dot(left, right):
    return lax.dot_general(left, right, (((1,), (0,)), ((), ())), preferred_element_type=F32)


def dot_t(left, right):
    return lax.dot_general(left, right, (((1,), (1,)), ((), ())), preferred_element_type=F32)


def dot3(lh, ll, rh, rl):
    return dot(lh, rh) + (dot(lh, rl) + dot(ll, rh))


def tables():
    z = np.arange(128)
    z_of = 4 * (z % 32) + z // 32
    kz = np.arange(256)
    ang = 2 * np.pi * ((kz[:, None] * z_of[None, :]) % 256) / 256
    forward_z = np.concatenate([np.cos(ang), np.sin(ang)], 1)
    inverse_z = np.concatenate([np.cos(ang).T, -np.sin(ang).T], 1) * 2.0**-26
    lane = np.arange(2048)
    group, inner = lane // 128, lane % 128
    ez, ex = group // 4, group % 4
    r, ey = inner // 64, inner // 16 % 2 * 2 + inner // 32 % 2
    row = r * 64 + 16 * ex + 4 * ey + ez
    expand = (np.arange(128)[:, None] == row[None, :]).astype(np.float32)
    k = np.arange(256)
    i = np.arange(256)
    real = (i // 64 % 2 == 0)[:, None]
    along = []
    for p in range(2):
        y = 64 * (i // 128 * 2 + i // 32 % 2) + 4 * (i % 16) + 2 * (i // 16 % 2) + p
        ang = 2 * np.pi * ((y[:, None] * k[None, :]) % 512) / 512
        c, s = np.cos(ang), np.sin(ang)
        along.append(np.concatenate([np.where(real, c, s), np.where(real, -s, c)], 1))
    across = []
    j = np.arange(128)
    for p in range(2):
        x = 4 * (j % 64) + 2 * (j // 64) + p
        ang = 2 * np.pi * ((k[:, None] * x[None, :]) % 512) / 512
        c, s = np.cos(ang), np.sin(ang)
        across.append(np.block([[c, s], [-s, c]]))
    return forward_z, inverse_z, expand, np.stack(along), np.stack(across)


def swap(value):
    lanes = value.shape[1]
    rolled = jnp.concatenate(
        [pltpu.roll(value[:, i : i + 128], 64, 1) for i in range(0, lanes, 128)], axis=1
    )
    sign = jnp.where(lax.broadcasted_iota(jnp.int32, (1, lanes), 1) % 128 < 64, 1.0, -1.0)
    return rolled * sign


def site_masks(count, site):
    rows = lax.broadcasted_iota(jnp.int32, (32, 256), 0)
    line = jnp.where(rows == site % 32, 1.0, 0.0)
    lanes = lax.broadcasted_iota(jnp.int32, (128, 256), 0)
    slots = lax.broadcasted_iota(jnp.int32, (128, 256), 1)
    plane = jnp.where((lanes % 16 == site // 32) & (slots < count), 1.0, 0.0)
    return line, plane.T


def fetch(pairs, sems):
    copies = [pltpu.make_async_copy(s, d, sems.at[i]) for i, (s, d) in enumerate(pairs)]
    for copy in copies:
        copy.start()
    return copies


def to_grid(count_ref, charges_any, site_any, proj_any, expand_any, fh_any, fl_any, out_ref, masked_ref,
            charges_ref, site_ref, proj_ref, expand_ref, fh_ref, fl_ref, sems):
    copies = fetch(
        [(charges_any, charges_ref), (proj_any, proj_ref), (site_any, site_ref),
         (expand_any, expand_ref), (fh_any, fh_ref), (fl_any, fl_ref)], sems)
    count = count_ref[0]
    slots = lax.broadcasted_iota(jnp.int32, (128, 256), 1)
    for copy in copies[:3]:
        copy.wait()
    line, plane = site_masks(count, site_ref[...])
    turned = jnp.where(slots < count, charges_ref[...], 0.0).T
    masked_ref[...] = turned
    ph, plo = split(proj_ref[...])
    parts = []
    for r in range(2):
        mh, ml = split(turned[:, 64 * r : 64 * r + 64])
        parts.append(dot_t(mh, ph) + (dot_t(mh, plo) + dot_t(ml, ph)))
    both = jnp.concatenate(split(jnp.concatenate(parts, axis=1)), axis=0)
    plane = jnp.concatenate([plane, plane], axis=1)
    line = line.astype(BF16)
    line = jnp.concatenate([line, line], axis=1)
    copies[3].wait()
    rows = []
    for ez in range(4):
        cols = []
        for e in range(2):
            lo = (ez * 4 + 2 * e) * 128
            spread = dot(both, expand_ref[:, lo : lo + 256])
            high = (spread[:256] * plane).astype(BF16)
            low = (spread[256:] * plane).astype(BF16)
            cols.append(dot(line, jnp.concatenate([high, low], axis=0)))
        rows.append(jnp.concatenate(cols, axis=1))
    grid = jnp.concatenate(rows, axis=0)
    gh, gl = split(jnp.concatenate([grid, swap(grid)], axis=0))
    copies[4].wait()
    copies[5].wait()
    for e in range(2):
        c = slice(256 * e, 256 * e + 256)
        planes = dot3(fh_ref[...], fl_ref[...], gh[:, c], gl[:, c])
        out_ref[pl.ds(2 * e, 256, stride=4), :] = planes[:, :128]
        out_ref[pl.ds(2 * e + 1, 256, stride=4), :] = planes[:, 128:]


def join(a_ref, b_ref, c_ref, out_ref):
    for i, ref in enumerate((a_ref, b_ref, c_ref)):
        out_ref[256 * i : 256 * i + 256, :] = ref[...]


def convolve(in_any, green_any, yh_any, yl_any, xh_any, xl_any, ih_any, il_any, out_ref,
             in_ref, green_ref, yh, yl, xh, xl, ih, il, ah, al, sh, sl, qh, ql, bh, bl, sems):
    (arrived,) = fetch([(in_any, in_ref)], sems)
    copies = fetch(
        [(yh_any, yh), (yl_any, yl), (xh_any, xh), (xl_any, xl), (green_any, green_ref), (ih_any, ih), (il_any, il)],
        sems.at[pl.ds(1, 7)])
    arrived.wait()
    first = lax.broadcasted_iota(jnp.int32, (64, 128), 1) % 64 < 32
    order = (0, 2, 1, 3)
    for i, ex in enumerate(order):
        a = slice(64 * i, 64 * i + 64)
        for m in range(2):
            c = slice(128 * m, 128 * m + 128)
            d0 = in_ref[pl.ds(8 * m + ex, 64, stride=16), :]
            d1 = in_ref[pl.ds(8 * m + 4 + ex, 64, stride=16), :]
            ah[0, a, c], al[0, a, c] = split(jnp.where(first, d0, pltpu.roll(d1, 32, 1)))
            ah[1, a, c], al[1, a, c] = split(jnp.where(first, pltpu.roll(d0, 96, 1), d1))
    copies[0].wait()
    copies[1].wait()
    for r in range(2):
        c = slice(256 * r, 256 * r + 256)
        o = slice(128 * r, 128 * r + 128)
        even = dot3(ah[0], al[0], yh[0, :, c], yl[0, :, c])
        odd = dot3(ah[1], al[1], yh[1, :, c], yl[1, :, c])
        for half, (h, l) in enumerate((split(even + odd), split(even - odd))):
            k = slice(256 * half, 256 * half + 256)
            for xp in range(2):
                sh[xp, o, k] = h[128 * xp : 128 * xp + 128]
                sl[xp, o, k] = l[128 * xp : 128 * xp + 128]
    copies[2].wait()
    copies[3].wait()
    copies[4].wait()
    for j in range(2):
        c = slice(256 * j, 256 * j + 256)
        part = [dot3(xh[xp], xl[xp], sh[xp, :, c], sl[xp, :, c]) for xp in range(2)]
        sums, diffs = part[0] + part[1], part[0] - part[1]
        gr, gi = green_ref[0, 0:256, c], green_ref[1, 0:256, c]
        p_re, p_im = gr * sums[:256] - gi * sums[256:], gr * sums[256:] + gi * sums[:256]
        gr, gi = green_ref[0, 256:512, c], green_ref[1, 256:512, c]
        q_re, q_im = gr * diffs[:256] - gi * diffs[256:], gr * diffs[256:] + gi * diffs[:256]
        qh[0, 0:256, c], ql[0, 0:256, c] = split(p_re + q_re)
        qh[1, 0:256, c], ql[1, 0:256, c] = split(p_re - q_re)
        qh[0, 256:512, c], ql[0, 256:512, c] = split(p_im + q_im)
        qh[1, 256:512, c], ql[1, 256:512, c] = split(p_im - q_im)
    copies[5].wait()
    copies[6].wait()
    for xp in range(2):
        u0, u1 = [dot3(ih[xp], il[xp], qh[xp, :, c], ql[xp, :, c]) for c in (slice(0, 256), slice(256, 512))]
        rows = slice(128 * xp, 128 * xp + 128)
        for p, (h, l) in enumerate((split(u0 + u1), split(u0 - u1))):
            for r in range(2):
                bh[p, rows, 256 * r : 256 * r + 256] = h[128 * r : 128 * r + 128]
                bl[p, rows, 256 * r : 256 * r + 256] = l[128 * r : 128 * r + 128]
    even, odd = [dot_t(bh[p], yh[p]) + (dot_t(bh[p], yl[p]) + dot_t(bl[p], yh[p])) for p in range(2)]
    for e, ex in enumerate(order):
        rows = slice(64 * e, 64 * e + 64)
        for m in range(2):
            c = slice(128 * m, 128 * m + 128)
            ve, vo = even[rows, c], odd[rows, c]
            out_ref[pl.ds(8 * m + ex, 64, stride=16), :] = jnp.where(first, ve, pltpu.roll(vo, 32, 1))
            out_ref[pl.ds(8 * m + 4 + ex, 64, stride=16), :] = jnp.where(first, pltpu.roll(ve, 96, 1), vo)


def from_grid(count_ref, site_ref, in_ref, proj_ref, expand_ref, fh_ref, fl_ref, near_ref, out_ref):
    count = count_ref[0]
    line, plane = site_masks(count, site_ref[...])
    field = jnp.concatenate([in_ref[pl.ds(ex, 256, stride=4), :] for ex in range(4)], axis=1)
    vh, vl = split(jnp.concatenate([field, swap(field)], axis=0))
    points = dot3(fh_ref[...], fl_ref[...], vh, vl)
    bh, bl = split(points)
    pick = line.T.astype(BF16)
    total = jnp.zeros((256, 128), F32)
    for ez in range(4):
        rows = slice(32 * ez, 32 * ez + 32)
        for ex in range(4):
            c = slice(128 * ex, 128 * ex + 128)
            high = (dot(pick, bh[rows, c]) * plane).astype(BF16)
            low = (dot(pick, bl[rows, c]) * plane).astype(BF16)
            lo = (ez * 4 + ex) * 128
            e = expand_ref[:, lo : lo + 128]
            total = total + (dot_t(high, e) + dot_t(low, e))
    th, tl = split(total)
    ph, plo = split(proj_ref[...])
    parts = []
    for r in range(2):
        c = slice(64 * r, 64 * r + 64)
        parts.append(dot3(th[:, c], tl[:, c], ph, plo))
    far = jnp.concatenate(parts, axis=1).T
    slots = lax.broadcasted_iota(jnp.int32, (128, 256), 1)
    out_ref[...] = far + jnp.where(slots < count, near_ref[...], 0.0)


CLASSES = 27


def near(index_ref, left_ref, own_ref, right_ref, table_ref, out_ref, source_ref, picked):
    for i, ref in enumerate((left_ref, own_ref, right_ref)):
        source_ref[768 * i : 768 * i + 768, :] = ref[...]

    def one(k, carry):
        for b in range(256):
            i = index_ref[k * 256 + b]
            picked[k, pl.ds(b, 1), :] = source_ref[pl.ds(i, 1), :]
        return carry

    lax.fori_loop(0, CLASSES, one, 0)
    total = jnp.zeros((256, 128), F32)
    for k in range(CLASSES):
        gh, gl = split(picked[k])
        re, im = table_ref[k, 0], table_ref[k, 1]
        rows = [jnp.concatenate([re, -im], axis=1), jnp.concatenate([im, re], axis=1)]
        th, tl = split(jnp.concatenate(rows, axis=0))
        total = total + (dot_t(gh, th) + (dot_t(gh, tl) + dot_t(gl, th)))
    out_ref[...] = total.T


def call(kernel, outs, args, kinds, scratch=(), copies=0, flops=0, bytes_accessed=0, name=None, out_kind="v", room=40):
    spaces = {"s": pltpu.SMEM, "v": VMEM, "h": pltpu.HBM}
    single = not isinstance(outs, (tuple, list))
    out_spec = pl.BlockSpec(memory_space=spaces[out_kind])
    scratch = list(scratch) + ([pltpu.SemaphoreType.DMA((copies,))] if copies else [])
    return pl.pallas_call(
        kernel,
        out_shape=outs,
        in_specs=[pl.BlockSpec(memory_space=spaces[k]) for k in kinds],
        out_specs=out_spec if single else tuple(out_spec for _ in outs),
        scratch_shapes=scratch,
        compiler_params=pltpu.CompilerParams(vmem_limit_bytes=room << 20),
        cost_estimate=pl.CostEstimate(flops=flops, bytes_accessed=bytes_accessed, transcendentals=0),
        name=name,
    )(*args)


def neighbours(array, axis, size):
    up = [(i, i + 1) for i in range(size - 1)]
    down = [(i + 1, i) for i in range(size - 1)]
    return lax.ppermute(array, axis, up), lax.ppermute(array, axis, down)


def per_device(charges, projection, green_hat, near_table, block_site, block_count, near_source):
    forward_z, inverse_z, expand, along, across = tables()
    fzh, fzl = halves(forward_z)
    izh, izl = halves(inverse_z)
    yh, yl = halves(along)
    xh, xl = halves(across)
    ih, il = halves(np.ascontiguousarray(across.transpose(0, 2, 1)))
    expand = expand.astype(jnp.bfloat16)
    site = block_site.reshape(1, 256)
    shape = lambda *s: jax.ShapeDtypeStruct(s, F32)

    cells = charges.reshape(128, 256)
    sent, masked = call(
        to_grid, (shape(1024, 128), shape(256, 128)), (block_count, cells, site, projection, expand, fzh, fzl), "shhhhhh",
        scratch=[VMEM((128, 256), F32), VMEM((1, 256), jnp.int32), VMEM((64, 64), F32), VMEM((128, 2048), BF16)]
        + [VMEM((256, 256), BF16)] * 2,
        copies=6, flops=2 * 10**9, bytes_accessed=2 << 20, name="to_grid", room=63,
    )
    planes = lax.all_to_all(sent.reshape(256, 4, 128), BOTH, split_axis=0, concat_axis=0, tiled=True)
    before, after = neighbours(masked, "narrow", N)
    own = call(join, shape(768, 128), (before, masked, after), "vvv", bytes_accessed=2 << 20, name="join", room=16)
    left, right = neighbours(own, "wide", W)
    back = call(
        convolve, shape(1024, 128),
        (planes.reshape(1024, 128), green_hat.reshape(2, 512, 512), yh, yl, xh, xl, ih, il), "hhhhhhhh",
        scratch=[VMEM((1024, 128), F32), VMEM((2, 512, 512), F32)] + [VMEM((2, 256, 512), BF16)] * 2 + [VMEM((2, 512, 256), BF16)] * 2
        + [VMEM((2, 256, 512), BF16)] * 2 + [VMEM((2, 256, 256), BF16)] * 2 + [VMEM((2, 256, 512), BF16)] * 2
        + [VMEM((2, 512, 512), BF16)] * 2 + [VMEM((2, 256, 512), BF16)] * 2,
        copies=8, flops=5 * 10**9, bytes_accessed=9 << 20, name="convolve", room=63,
    )
    field = lax.all_to_all(back.reshape(256, 4, 128), BOTH, split_axis=0, concat_axis=0, tiled=True)
    index = near_source.reshape(CLASSES * 256)
    beside = call(
        near, shape(128, 256), (index, left, own, right, near_table), "svvvv",
        scratch=[VMEM((2304, 128), F32), VMEM((CLASSES, 256, 128), F32)],
        flops=10**10, bytes_accessed=40 << 20, name="near", room=16,
    )
    result = call(
        from_grid, shape(128, 256),
        (block_count, site, field.reshape(1024, 128), projection, expand, izh, izl, beside), "svvvvvvv",
        flops=2 * 10**9, bytes_accessed=2 << 20, name="from_grid", room=12,
    )
    return result.reshape(2, 64, 256)


def solution(mesh):
    placed = (
        P(None, None, BOTH),
        P(),
        P(None, BOTH, None, None),
        P(),
        P(BOTH),
        P(BOTH),
        P(None, BOTH),
    )
    return jax.shard_map(
        per_device,
        mesh=mesh,
        in_specs=placed,
        out_specs=P(None, None, BOTH),
        check_vma=False,
    )
```

```python
import numpy as np

import jax
import jax.numpy as jnp
from jax import lax
from jax.experimental import pallas as pl
from jax.experimental.pallas import tpu as pltpu
from jax.sharding import PartitionSpec as P

W = 64
N = 4
F32 = jnp.float32
BF16 = jnp.bfloat16
VMEM = pltpu.VMEM
BOTH = ("wide", "narrow")


def halves(table):
    high = table.astype(jnp.bfloat16)
    low = (table - high.astype(np.float64)).astype(jnp.bfloat16)
    return high, low


def split(value):
    high = value.astype(BF16)
    return high, (value - high.astype(F32)).astype(BF16)


def dot(left, right):
    return lax.dot_general(left, right, (((1,), (0,)), ((), ())), preferred_element_type=F32)


def dot_t(left, right):
    return lax.dot_general(left, right, (((1,), (1,)), ((), ())), preferred_element_type=F32)


def dot3(lh, ll, rh, rl):
    return dot(lh, rh) + (dot(lh, rl) + dot(ll, rh))


def tables():
    z = np.arange(128)
    z_of = 4 * (z % 32) + z // 32
    kz = np.arange(256)
    ang = 2 * np.pi * ((kz[:, None] * z_of[None, :]) % 256) / 256
    forward_z = np.concatenate([np.cos(ang), np.sin(ang)], 1)
    inverse_z = np.concatenate([np.cos(ang).T, -np.sin(ang).T], 1) * 2.0**-26
    lane = np.arange(2048)
    group, inner = lane // 128, lane % 128
    ez, ex = group // 4, group % 4
    r, ey = inner // 64, inner // 16 % 2 * 2 + inner // 32 % 2
    row = r * 64 + 16 * ex + 4 * ey + ez
    expand = (np.arange(128)[:, None] == row[None, :]).astype(np.float32)
    k = np.arange(256)
    i = np.arange(256)
    real = (i // 64 % 2 == 0)[:, None]
    along = []
    for p in range(2):
        y = 64 * (i // 128 * 2 + i // 32 % 2) + 4 * (i % 16) + 2 * (i // 16 % 2) + p
        ang = 2 * np.pi * ((y[:, None] * k[None, :]) % 512) / 512
        c, s = np.cos(ang), np.sin(ang)
        along.append(np.concatenate([np.where(real, c, s), np.where(real, -s, c)], 1))
    across = []
    j = np.arange(128)
    for p in range(2):
        x = 4 * (j % 64) + 2 * (j // 64) + p
        ang = 2 * np.pi * ((k[:, None] * x[None, :]) % 512) / 512
        c, s = np.cos(ang), np.sin(ang)
        across.append(np.block([[c, s], [-s, c]]))
    return forward_z, inverse_z, expand, np.stack(along), np.stack(across)


def swap(value):
    lanes = value.shape[1]
    rolled = jnp.concatenate(
        [pltpu.roll(value[:, i : i + 128], 64, 1) for i in range(0, lanes, 128)], axis=1
    )
    sign = jnp.where(lax.broadcasted_iota(jnp.int32, (1, lanes), 1) % 128 < 64, 1.0, -1.0)
    return rolled * sign


def site_masks(count, site):
    rows = lax.broadcasted_iota(jnp.int32, (32, 256), 0)
    line = jnp.where(rows == site % 32, 1.0, 0.0)
    lanes = lax.broadcasted_iota(jnp.int32, (128, 256), 0)
    slots = lax.broadcasted_iota(jnp.int32, (128, 256), 1)
    plane = jnp.where((lanes % 16 == site // 32) & (slots < count), 1.0, 0.0)
    return line, plane.T


def fetch(pairs, sems):
    copies = [pltpu.make_async_copy(s, d, sems.at[i]) for i, (s, d) in enumerate(pairs)]
    for copy in copies:
        copy.start()
    return copies


def to_grid(count_ref, charges_any, site_any, proj_any, expand_any, fh_any, fl_any, out_ref, masked_ref,
            charges_ref, site_ref, proj_ref, expand_ref, fh_ref, fl_ref, sems):
    copies = fetch(
        [(charges_any, charges_ref), (proj_any, proj_ref), (site_any, site_ref),
         (expand_any, expand_ref), (fh_any, fh_ref), (fl_any, fl_ref)], sems)
    count = count_ref[0]
    slots = lax.broadcasted_iota(jnp.int32, (128, 256), 1)
    for copy in copies[:3]:
        copy.wait()
    line, plane = site_masks(count, site_ref[...])
    turned = jnp.where(slots < count, charges_ref[...], 0.0).T
    masked_ref[...] = turned
    ph, plo = split(proj_ref[...])
    parts = []
    for r in range(2):
        mh, ml = split(turned[:, 64 * r : 64 * r + 64])
        parts.append(dot_t(mh, ph) + (dot_t(mh, plo) + dot_t(ml, ph)))
    both = jnp.concatenate(split(jnp.concatenate(parts, axis=1)), axis=0)
    plane = jnp.concatenate([plane, plane], axis=1)
    line = line.astype(BF16)
    line = jnp.concatenate([line, line], axis=1)
    copies[3].wait()
    rows = []
    for ez in range(4):
        cols = []
        for e in range(2):
            lo = (ez * 4 + 2 * e) * 128
            spread = dot(both, expand_ref[:, lo : lo + 256])
            high = (spread[:256] * plane).astype(BF16)
            low = (spread[256:] * plane).astype(BF16)
            cols.append(dot(line, jnp.concatenate([high, low], axis=0)))
        rows.append(jnp.concatenate(cols, axis=1))
    grid = jnp.concatenate(rows, axis=0)
    gh, gl = split(jnp.concatenate([grid, swap(grid)], axis=0))
    copies[4].wait()
    copies[5].wait()
    for e in range(2):
        c = slice(256 * e, 256 * e + 256)
        planes = dot3(fh_ref[...], fl_ref[...], gh[:, c], gl[:, c])
        out_ref[pl.ds(2 * e, 256, stride=4), :] = planes[:, :128]
        out_ref[pl.ds(2 * e + 1, 256, stride=4), :] = planes[:, 128:]


def join(count_ref, before_ref, charges_ref, after_ref, out_ref):
    slots = lax.broadcasted_iota(jnp.int32, (128, 256), 1)
    out_ref[0:256, :] = before_ref[...]
    out_ref[256:512, :] = jnp.where(slots < count_ref[0], charges_ref[...], 0.0).T
    out_ref[512:768, :] = after_ref[...]


def convolve(in_ref, green_any, yh_any, yl_any, xh_any, xl_any, ih_any, il_any, out_ref,
             green_ref, yh, yl, xh, xl, ih, il, ah, al, sh, sl, qh, ql, bh, bl, sems):
    copies = fetch(
        [(yh_any, yh), (yl_any, yl), (xh_any, xh), (xl_any, xl), (green_any, green_ref), (ih_any, ih), (il_any, il)],
        sems)
    first = lax.broadcasted_iota(jnp.int32, (64, 128), 1) % 64 < 32
    order = (0, 2, 1, 3)
    for i, ex in enumerate(order):
        a = slice(64 * i, 64 * i + 64)
        for m in range(2):
            c = slice(128 * m, 128 * m + 128)
            d0 = in_ref[pl.ds(8 * m + ex, 64, stride=16), :]
            d1 = in_ref[pl.ds(8 * m + 4 + ex, 64, stride=16), :]
            ah[0, a, c], al[0, a, c] = split(jnp.where(first, d0, pltpu.roll(d1, 32, 1)))
            ah[1, a, c], al[1, a, c] = split(jnp.where(first, pltpu.roll(d0, 96, 1), d1))
    copies[0].wait()
    copies[1].wait()
    for r in range(2):
        c = slice(256 * r, 256 * r + 256)
        o = slice(128 * r, 128 * r + 128)
        even = dot3(ah[0], al[0], yh[0, :, c], yl[0, :, c])
        odd = dot3(ah[1], al[1], yh[1, :, c], yl[1, :, c])
        for half, (h, l) in enumerate((split(even + odd), split(even - odd))):
            k = slice(256 * half, 256 * half + 256)
            for xp in range(2):
                sh[xp, o, k] = h[128 * xp : 128 * xp + 128]
                sl[xp, o, k] = l[128 * xp : 128 * xp + 128]
    copies[2].wait()
    copies[3].wait()
    copies[4].wait()
    for j in range(2):
        c = slice(256 * j, 256 * j + 256)
        part = [dot3(xh[xp], xl[xp], sh[xp, :, c], sl[xp, :, c]) for xp in range(2)]
        sums, diffs = part[0] + part[1], part[0] - part[1]
        gr, gi = green_ref[0, 0:256, c], green_ref[1, 0:256, c]
        p_re, p_im = gr * sums[:256] - gi * sums[256:], gr * sums[256:] + gi * sums[:256]
        gr, gi = green_ref[0, 256:512, c], green_ref[1, 256:512, c]
        q_re, q_im = gr * diffs[:256] - gi * diffs[256:], gr * diffs[256:] + gi * diffs[:256]
        qh[0, 0:256, c], ql[0, 0:256, c] = split(p_re + q_re)
        qh[1, 0:256, c], ql[1, 0:256, c] = split(p_re - q_re)
        qh[0, 256:512, c], ql[0, 256:512, c] = split(p_im + q_im)
        qh[1, 256:512, c], ql[1, 256:512, c] = split(p_im - q_im)
    copies[5].wait()
    copies[6].wait()
    for xp in range(2):
        u0, u1 = [dot3(ih[xp], il[xp], qh[xp, :, c], ql[xp, :, c]) for c in (slice(0, 256), slice(256, 512))]
        rows = slice(128 * xp, 128 * xp + 128)
        for p, (h, l) in enumerate((split(u0 + u1), split(u0 - u1))):
            for r in range(2):
                bh[p, rows, 256 * r : 256 * r + 256] = h[128 * r : 128 * r + 128]
                bl[p, rows, 256 * r : 256 * r + 256] = l[128 * r : 128 * r + 128]
    even, odd = [dot_t(bh[p], yh[p]) + (dot_t(bh[p], yl[p]) + dot_t(bl[p], yh[p])) for p in range(2)]
    for e, ex in enumerate(order):
        rows = slice(64 * e, 64 * e + 64)
        for m in range(2):
            c = slice(128 * m, 128 * m + 128)
            ve, vo = even[rows, c], odd[rows, c]
            out_ref[pl.ds(8 * m + ex, 64, stride=16), :] = jnp.where(first, ve, pltpu.roll(vo, 32, 1))
            out_ref[pl.ds(8 * m + 4 + ex, 64, stride=16), :] = jnp.where(first, pltpu.roll(ve, 96, 1), vo)


def from_grid(count_ref, site_ref, in_ref, proj_ref, expand_ref, fh_ref, fl_ref, near_ref, out_ref):
    count = count_ref[0]
    line, plane = site_masks(count, site_ref[...])
    field = jnp.concatenate([in_ref[pl.ds(ex, 256, stride=4), :] for ex in range(4)], axis=1)
    vh, vl = split(jnp.concatenate([field, swap(field)], axis=0))
    points = dot3(fh_ref[...], fl_ref[...], vh, vl)
    bh, bl = split(points)
    pick = line.T.astype(BF16)
    total = jnp.zeros((256, 128), F32)
    for ez in range(4):
        rows = slice(32 * ez, 32 * ez + 32)
        for ex in range(4):
            c = slice(128 * ex, 128 * ex + 128)
            high = (dot(pick, bh[rows, c]) * plane).astype(BF16)
            low = (dot(pick, bl[rows, c]) * plane).astype(BF16)
            lo = (ez * 4 + ex) * 128
            e = expand_ref[:, lo : lo + 128]
            total = total + (dot_t(high, e) + dot_t(low, e))
    th, tl = split(total)
    ph, plo = split(proj_ref[...])
    parts = []
    for r in range(2):
        c = slice(64 * r, 64 * r + 64)
        parts.append(dot3(th[:, c], tl[:, c], ph, plo))
    far = jnp.concatenate(parts, axis=1).T
    slots = lax.broadcasted_iota(jnp.int32, (128, 256), 1)
    out_ref[...] = far + jnp.where(slots < count, near_ref[...], 0.0)


CLASSES = 27


def near(index_ref, left_ref, own_ref, right_ref, table_ref, out_ref, source_ref, picked):
    for i, ref in enumerate((left_ref, own_ref, right_ref)):
        source_ref[768 * i : 768 * i + 768, :] = ref[...]

    def one(k, carry):
        for b in range(256):
            i = index_ref[k * 256 + b]
            picked[k, pl.ds(b, 1), :] = source_ref[pl.ds(i, 1), :]
        return carry

    lax.fori_loop(0, CLASSES, one, 0)
    total = jnp.zeros((256, 128), F32)
    for k in range(CLASSES):
        gh, gl = split(picked[k])
        re, im = table_ref[k, 0], table_ref[k, 1]
        rows = [jnp.concatenate([re, -im], axis=1), jnp.concatenate([im, re], axis=1)]
        th, tl = split(jnp.concatenate(rows, axis=0))
        total = total + (dot_t(gh, th) + (dot_t(gh, tl) + dot_t(gl, th)))
    out_ref[...] = total.T


def call(kernel, outs, args, kinds, scratch=(), copies=0, flops=0, bytes_accessed=0, name=None, out_kind="v", room=40):
    spaces = {"s": pltpu.SMEM, "v": VMEM, "h": pltpu.HBM}
    single = not isinstance(outs, (tuple, list))
    out_spec = pl.BlockSpec(memory_space=spaces[out_kind])
    scratch = list(scratch) + ([pltpu.SemaphoreType.DMA((copies,))] if copies else [])
    return pl.pallas_call(
        kernel,
        out_shape=outs,
        in_specs=[pl.BlockSpec(memory_space=spaces[k]) for k in kinds],
        out_specs=out_spec if single else tuple(out_spec for _ in outs),
        scratch_shapes=scratch,
        compiler_params=pltpu.CompilerParams(vmem_limit_bytes=int(room * 2**20)),
        cost_estimate=pl.CostEstimate(flops=flops, bytes_accessed=bytes_accessed, transcendentals=0),
        name=name,
    )(*args)


def neighbours(array, axis, size):
    up = [(i, i + 1) for i in range(size - 1)]
    down = [(i + 1, i) for i in range(size - 1)]
    return lax.ppermute(array, axis, up), lax.ppermute(array, axis, down)


def per_device(charges, projection, green_hat, near_table, block_site, block_count, near_source):
    forward_z, inverse_z, expand, along, across = tables()
    fzh, fzl = halves(forward_z)
    izh, izl = halves(inverse_z)
    yh, yl = halves(along)
    xh, xl = halves(across)
    ih, il = halves(np.ascontiguousarray(across.transpose(0, 2, 1)))
    expand = expand.astype(jnp.bfloat16)
    site = block_site.reshape(1, 256)
    shape = lambda *s: jax.ShapeDtypeStruct(s, F32)

    cells = charges.reshape(128, 256)
    sent, masked = call(
        to_grid, (shape(1024, 128), shape(256, 128)), (block_count, cells, site, projection, expand, fzh, fzl), "shhhhhh",
        scratch=[VMEM((128, 256), F32), VMEM((1, 256), jnp.int32), VMEM((64, 64), F32), VMEM((128, 2048), BF16)]
        + [VMEM((256, 256), BF16)] * 2,
        copies=6, flops=2 * 10**9, bytes_accessed=2 << 20, name="to_grid", room=63,
    )
    planes = lax.all_to_all(sent.reshape(256, 4, 128), BOTH, split_axis=0, concat_axis=0, tiled=True)
    before, after = neighbours(masked, "narrow", N)
    own = call(join, shape(768, 128), (block_count, before, cells, after), "svvv", bytes_accessed=2 << 20, name="join", room=16)
    left, _ = neighbours(own, "wide", W)
    later, planes = lax.optimization_barrier((own, planes))
    _, right = neighbours(later, "wide", W)
    back = call(
        convolve, shape(1024, 128),
        (planes.reshape(1024, 128), green_hat.reshape(2, 512, 512), yh, yl, xh, xl, ih, il), "vhhhhhhh",
        scratch=[VMEM((2, 512, 512), F32)] + [VMEM((2, 256, 512), BF16)] * 2 + [VMEM((2, 512, 256), BF16)] * 2
        + [VMEM((2, 256, 512), BF16)] * 2 + [VMEM((2, 256, 256), BF16)] * 2 + [VMEM((2, 256, 512), BF16)] * 2
        + [VMEM((2, 512, 512), BF16)] * 2 + [VMEM((2, 256, 512), BF16)] * 2,
        copies=7, flops=5 * 10**9, bytes_accessed=9 << 20, name="convolve", room=52.5,
    )
    field = lax.all_to_all(back.reshape(256, 4, 128), BOTH, split_axis=0, concat_axis=0, tiled=True)
    index = near_source.reshape(CLASSES * 256)
    beside = call(
        near, shape(128, 256), (index, left, own, right, near_table), "svvvv",
        scratch=[VMEM((2304, 128), F32), VMEM((CLASSES, 256, 128), F32)],
        flops=10**10, bytes_accessed=40 << 20, name="near", room=52.5,
    )
    result = call(
        from_grid, shape(128, 256),
        (block_count, site, field.reshape(1024, 128), projection, expand, izh, izl, beside), "svvvvvvv",
        flops=2 * 10**9, bytes_accessed=2 << 20, name="from_grid", room=52.5,
    )
    return result.reshape(2, 64, 256)


def solution(mesh):
    placed = (
        P(None, None, BOTH),
        P(),
        P(None, BOTH, None, None),
        P(),
        P(BOTH),
        P(BOTH),
        P(None, BOTH),
    )
    return jax.shard_map(
        per_device,
        mesh=mesh,
        in_specs=placed,
        out_specs=P(None, None, BOTH),
        check_vma=False,
    )
```

```python
import numpy as np

import jax
import jax.numpy as jnp
from jax import lax
from jax.experimental import pallas as pl
from jax.experimental.pallas import tpu as pltpu
from jax.sharding import PartitionSpec as P

W = 64
N = 4
F32 = jnp.float32
BF16 = jnp.bfloat16
VMEM = pltpu.VMEM
BOTH = ("wide", "narrow")


def halves(table):
    high = table.astype(jnp.bfloat16)
    low = (table - high.astype(np.float64)).astype(jnp.bfloat16)
    return high, low


def split(value):
    high = value.astype(BF16)
    return high, (value - high.astype(F32)).astype(BF16)


def dot(left, right):
    return lax.dot_general(left, right, (((1,), (0,)), ((), ())), preferred_element_type=F32)


def dot_t(left, right):
    return lax.dot_general(left, right, (((1,), (1,)), ((), ())), preferred_element_type=F32)


def dot3(lh, ll, rh, rl):
    return dot(lh, rh) + (dot(lh, rl) + dot(ll, rh))


def tables():
    z = np.arange(128)
    z_of = 4 * (z % 32) + z // 32
    kz = np.arange(256)
    ang = 2 * np.pi * ((kz[:, None] * z_of[None, :]) % 256) / 256
    forward_z = np.concatenate([np.cos(ang), np.sin(ang)], 1)
    inverse_z = np.concatenate([np.cos(ang).T, -np.sin(ang).T], 1) * 2.0**-26
    lane = np.arange(2048)
    group, inner = lane // 128, lane % 128
    ez, ex = group // 4, group % 4
    r, ey = inner // 64, inner // 16 % 2 * 2 + inner // 32 % 2
    row = r * 64 + 16 * ex + 4 * ey + ez
    expand = (np.arange(128)[:, None] == row[None, :]).astype(np.float32)
    k = np.arange(256)
    i = np.arange(256)
    real = (i // 64 % 2 == 0)[:, None]
    along = []
    for p in range(2):
        y = 64 * (i // 128 * 2 + i // 32 % 2) + 4 * (i % 16) + 2 * (i // 16 % 2) + p
        ang = 2 * np.pi * ((y[:, None] * k[None, :]) % 512) / 512
        c, s = np.cos(ang), np.sin(ang)
        along.append(np.concatenate([np.where(real, c, s), np.where(real, -s, c)], 1))
    across = []
    j = np.arange(128)
    for p in range(2):
        x = 4 * (j % 64) + 2 * (j // 64) + p
        ang = 2 * np.pi * ((k[:, None] * x[None, :]) % 512) / 512
        c, s = np.cos(ang), np.sin(ang)
        across.append(np.block([[c, s], [-s, c]]))
    return forward_z, inverse_z, expand, np.stack(along), np.stack(across)


def swap(value):
    lanes = value.shape[1]
    rolled = jnp.concatenate(
        [pltpu.roll(value[:, i : i + 128], 64, 1) for i in range(0, lanes, 128)], axis=1
    )
    sign = jnp.where(lax.broadcasted_iota(jnp.int32, (1, lanes), 1) % 128 < 64, 1.0, -1.0)
    return rolled * sign


def site_masks(count, site):
    rows = lax.broadcasted_iota(jnp.int32, (32, 256), 0)
    line = jnp.where(rows == site % 32, 1.0, 0.0)
    lanes = lax.broadcasted_iota(jnp.int32, (128, 256), 0)
    slots = lax.broadcasted_iota(jnp.int32, (128, 256), 1)
    plane = jnp.where((lanes % 16 == site // 32) & (slots < count), 1.0, 0.0)
    return line, plane.T


def fetch(pairs, sems):
    copies = [pltpu.make_async_copy(s, d, sems.at[i]) for i, (s, d) in enumerate(pairs)]
    for copy in copies:
        copy.start()
    return copies


def to_grid(count_ref, charges_any, site_any, proj_any, expand_any, fh_any, fl_any, out_ref,
            charges_ref, site_ref, proj_ref, expand_ref, fh_ref, fl_ref, sems):
    copies = fetch(
        [(charges_any, charges_ref), (proj_any, proj_ref), (site_any, site_ref),
         (expand_any, expand_ref), (fh_any, fh_ref), (fl_any, fl_ref)], sems)
    count = count_ref[0]
    slots = lax.broadcasted_iota(jnp.int32, (128, 256), 1)
    for copy in copies[:3]:
        copy.wait()
    line, plane = site_masks(count, site_ref[...])
    turned = jnp.where(slots < count, charges_ref[...], 0.0).T
    ph, plo = split(proj_ref[...])
    parts = []
    for r in range(2):
        mh, ml = split(turned[:, 64 * r : 64 * r + 64])
        parts.append(dot_t(mh, ph) + (dot_t(mh, plo) + dot_t(ml, ph)))
    both = jnp.concatenate(split(jnp.concatenate(parts, axis=1)), axis=0)
    plane = jnp.concatenate([plane, plane], axis=1)
    line = line.astype(BF16)
    line = jnp.concatenate([line, line], axis=1)
    copies[3].wait()
    rows = []
    for ez in range(4):
        cols = []
        for e in range(2):
            lo = (ez * 4 + 2 * e) * 128
            spread = dot(both, expand_ref[:, lo : lo + 256])
            high = (spread[:256] * plane).astype(BF16)
            low = (spread[256:] * plane).astype(BF16)
            cols.append(dot(line, jnp.concatenate([high, low], axis=0)))
        rows.append(jnp.concatenate(cols, axis=1))
    grid = jnp.concatenate(rows, axis=0)
    gh, gl = split(jnp.concatenate([grid, swap(grid)], axis=0))
    copies[4].wait()
    copies[5].wait()
    for e in range(2):
        c = slice(256 * e, 256 * e + 256)
        planes = dot3(fh_ref[...], fl_ref[...], gh[:, c], gl[:, c])
        out_ref[pl.ds(2 * e, 256, stride=4), :] = planes[:, :128]
        out_ref[pl.ds(2 * e + 1, 256, stride=4), :] = planes[:, 128:]


def turn(count_ref, charges_ref, out_ref):
    slots = lax.broadcasted_iota(jnp.int32, (128, 256), 1)
    out_ref[...] = jnp.where(slots < count_ref[0], charges_ref[...], 0.0).T


def join(count_ref, before_ref, charges_ref, after_ref, out_ref):
    slots = lax.broadcasted_iota(jnp.int32, (128, 256), 1)
    out_ref[0:256, :] = before_ref[...]
    out_ref[256:512, :] = jnp.where(slots < count_ref[0], charges_ref[...], 0.0).T
    out_ref[512:768, :] = after_ref[...]


def convolve(in_ref, green_any, yh_any, yl_any, xh_any, xl_any, ih_any, il_any, out_ref,
             green_ref, yh, yl, xh, xl, ih, il, ah, al, sh, sl, qh, ql, bh, bl, sems):
    copies = fetch(
        [(yh_any, yh), (yl_any, yl), (xh_any, xh), (xl_any, xl), (green_any, green_ref), (ih_any, ih), (il_any, il)],
        sems)
    first = lax.broadcasted_iota(jnp.int32, (64, 128), 1) % 64 < 32
    order = (0, 2, 1, 3)
    for i, ex in enumerate(order):
        a = slice(64 * i, 64 * i + 64)
        for m in range(2):
            c = slice(128 * m, 128 * m + 128)
            d0 = in_ref[pl.ds(8 * m + ex, 64, stride=16), :]
            d1 = in_ref[pl.ds(8 * m + 4 + ex, 64, stride=16), :]
            ah[0, a, c], al[0, a, c] = split(jnp.where(first, d0, pltpu.roll(d1, 32, 1)))
            ah[1, a, c], al[1, a, c] = split(jnp.where(first, pltpu.roll(d0, 96, 1), d1))
    copies[0].wait()
    copies[1].wait()
    for r in range(2):
        c = slice(256 * r, 256 * r + 256)
        o = slice(128 * r, 128 * r + 128)
        even = dot3(ah[0], al[0], yh[0, :, c], yl[0, :, c])
        odd = dot3(ah[1], al[1], yh[1, :, c], yl[1, :, c])
        for half, (h, l) in enumerate((split(even + odd), split(even - odd))):
            k = slice(256 * half, 256 * half + 256)
            for xp in range(2):
                sh[xp, o, k] = h[128 * xp : 128 * xp + 128]
                sl[xp, o, k] = l[128 * xp : 128 * xp + 128]
    copies[2].wait()
    copies[3].wait()
    copies[4].wait()
    for j in range(2):
        c = slice(256 * j, 256 * j + 256)
        part = [dot3(xh[xp], xl[xp], sh[xp, :, c], sl[xp, :, c]) for xp in range(2)]
        sums, diffs = part[0] + part[1], part[0] - part[1]
        gr, gi = green_ref[0, 0:256, c], green_ref[1, 0:256, c]
        p_re, p_im = gr * sums[:256] - gi * sums[256:], gr * sums[256:] + gi * sums[:256]
        gr, gi = green_ref[0, 256:512, c], green_ref[1, 256:512, c]
        q_re, q_im = gr * diffs[:256] - gi * diffs[256:], gr * diffs[256:] + gi * diffs[:256]
        qh[0, 0:256, c], ql[0, 0:256, c] = split(p_re + q_re)
        qh[1, 0:256, c], ql[1, 0:256, c] = split(p_re - q_re)
        qh[0, 256:512, c], ql[0, 256:512, c] = split(p_im + q_im)
        qh[1, 256:512, c], ql[1, 256:512, c] = split(p_im - q_im)
    copies[5].wait()
    copies[6].wait()
    for xp in range(2):
        u0, u1 = [dot3(ih[xp], il[xp], qh[xp, :, c], ql[xp, :, c]) for c in (slice(0, 256), slice(256, 512))]
        rows = slice(128 * xp, 128 * xp + 128)
        for p, (h, l) in enumerate((split(u0 + u1), split(u0 - u1))):
            for r in range(2):
                bh[p, rows, 256 * r : 256 * r + 256] = h[128 * r : 128 * r + 128]
                bl[p, rows, 256 * r : 256 * r + 256] = l[128 * r : 128 * r + 128]
    even, odd = [dot_t(bh[p], yh[p]) + (dot_t(bh[p], yl[p]) + dot_t(bl[p], yh[p])) for p in range(2)]
    for e, ex in enumerate(order):
        rows = slice(64 * e, 64 * e + 64)
        for m in range(2):
            c = slice(128 * m, 128 * m + 128)
            ve, vo = even[rows, c], odd[rows, c]
            out_ref[pl.ds(8 * m + ex, 64, stride=16), :] = jnp.where(first, ve, pltpu.roll(vo, 32, 1))
            out_ref[pl.ds(8 * m + 4 + ex, 64, stride=16), :] = jnp.where(first, pltpu.roll(ve, 96, 1), vo)


def from_grid(count_ref, site_ref, in_ref, proj_ref, expand_ref, fh_ref, fl_ref, near_ref, out_ref):
    count = count_ref[0]
    line, plane = site_masks(count, site_ref[...])
    field = jnp.concatenate([in_ref[pl.ds(ex, 256, stride=4), :] for ex in range(4)], axis=1)
    vh, vl = split(jnp.concatenate([field, swap(field)], axis=0))
    points = dot3(fh_ref[...], fl_ref[...], vh, vl)
    bh, bl = split(points)
    pick = line.T.astype(BF16)
    total = jnp.zeros((256, 128), F32)
    for ez in range(4):
        rows = slice(32 * ez, 32 * ez + 32)
        for ex in range(4):
            c = slice(128 * ex, 128 * ex + 128)
            high = (dot(pick, bh[rows, c]) * plane).astype(BF16)
            low = (dot(pick, bl[rows, c]) * plane).astype(BF16)
            lo = (ez * 4 + ex) * 128
            e = expand_ref[:, lo : lo + 128]
            total = total + (dot_t(high, e) + dot_t(low, e))
    th, tl = split(total)
    ph, plo = split(proj_ref[...])
    parts = []
    for r in range(2):
        c = slice(64 * r, 64 * r + 64)
        parts.append(dot3(th[:, c], tl[:, c], ph, plo))
    far = jnp.concatenate(parts, axis=1).T
    slots = lax.broadcasted_iota(jnp.int32, (128, 256), 1)
    out_ref[...] = far + jnp.where(slots < count, near_ref[...], 0.0)


CLASSES = 27


def near(index_ref, left_ref, own_ref, right_ref, table_ref, out_ref, source_ref, picked):
    for i, ref in enumerate((left_ref, own_ref, right_ref)):
        source_ref[768 * i : 768 * i + 768, :] = ref[...]

    def one(k, carry):
        for b in range(256):
            i = index_ref[k * 256 + b]
            picked[k, pl.ds(b, 1), :] = source_ref[pl.ds(i, 1), :]
        return carry

    lax.fori_loop(0, CLASSES, one, 0)
    total = jnp.zeros((256, 128), F32)
    for k in range(CLASSES):
        gh, gl = split(picked[k])
        re, im = table_ref[k, 0], table_ref[k, 1]
        rows = [jnp.concatenate([re, -im], axis=1), jnp.concatenate([im, re], axis=1)]
        th, tl = split(jnp.concatenate(rows, axis=0))
        total = total + (dot_t(gh, th) + (dot_t(gh, tl) + dot_t(gl, th)))
    out_ref[...] = total.T


def call(kernel, outs, args, kinds, scratch=(), copies=0, flops=0, bytes_accessed=0, name=None, out_kind="v", room=40):
    spaces = {"s": pltpu.SMEM, "v": VMEM, "h": pltpu.HBM}
    single = not isinstance(outs, (tuple, list))
    out_spec = pl.BlockSpec(memory_space=spaces[out_kind])
    scratch = list(scratch) + ([pltpu.SemaphoreType.DMA((copies,))] if copies else [])
    return pl.pallas_call(
        kernel,
        out_shape=outs,
        in_specs=[pl.BlockSpec(memory_space=spaces[k]) for k in kinds],
        out_specs=out_spec if single else tuple(out_spec for _ in outs),
        scratch_shapes=scratch,
        compiler_params=pltpu.CompilerParams(vmem_limit_bytes=int(room * 2**20)),
        cost_estimate=pl.CostEstimate(flops=flops, bytes_accessed=bytes_accessed, transcendentals=0),
        name=name,
    )(*args)


def neighbours(array, axis, size):
    up = [(i, i + 1) for i in range(size - 1)]
    down = [(i + 1, i) for i in range(size - 1)]
    return lax.ppermute(array, axis, up), lax.ppermute(array, axis, down)


def per_device(charges, projection, green_hat, near_table, block_site, block_count, near_source):
    forward_z, inverse_z, expand, along, across = tables()
    fzh, fzl = halves(forward_z)
    izh, izl = halves(inverse_z)
    yh, yl = halves(along)
    xh, xl = halves(across)
    ih, il = halves(np.ascontiguousarray(across.transpose(0, 2, 1)))
    expand = expand.astype(jnp.bfloat16)
    site = block_site.reshape(1, 256)
    shape = lambda *s: jax.ShapeDtypeStruct(s, F32)

    cells = charges.reshape(128, 256)
    masked = call(turn, shape(256, 128), (block_count, cells), "sv", bytes_accessed=1 << 20, name="turn", room=16)
    before, after = neighbours(masked, "narrow", N)
    sent = call(
        to_grid, shape(1024, 128), (block_count, cells, site, projection, expand, fzh, fzl), "shhhhhh",
        scratch=[VMEM((128, 256), F32), VMEM((1, 256), jnp.int32), VMEM((64, 64), F32), VMEM((128, 2048), BF16)]
        + [VMEM((256, 256), BF16)] * 2,
        copies=6, flops=2 * 10**9, bytes_accessed=2 << 20, name="to_grid", room=63,
    )
    sent, before, after = lax.optimization_barrier((sent, before, after))
    planes = lax.all_to_all(sent.reshape(256, 4, 128), BOTH, split_axis=0, concat_axis=0, tiled=True)
    own = call(join, shape(768, 128), (block_count, before, cells, after), "svvv", bytes_accessed=2 << 20, name="join", room=16)
    left, right = neighbours(own, "wide", W)
    back = call(
        convolve, shape(1024, 128),
        (planes.reshape(1024, 128), green_hat.reshape(2, 512, 512), yh, yl, xh, xl, ih, il), "vhhhhhhh",
        scratch=[VMEM((2, 512, 512), F32)] + [VMEM((2, 256, 512), BF16)] * 2 + [VMEM((2, 512, 256), BF16)] * 2
        + [VMEM((2, 256, 512), BF16)] * 2 + [VMEM((2, 256, 256), BF16)] * 2 + [VMEM((2, 256, 512), BF16)] * 2
        + [VMEM((2, 512, 512), BF16)] * 2 + [VMEM((2, 256, 512), BF16)] * 2,
        copies=7, flops=5 * 10**9, bytes_accessed=9 << 20, name="convolve", room=52.5,
    )
    field = lax.all_to_all(back.reshape(256, 4, 128), BOTH, split_axis=0, concat_axis=0, tiled=True)
    index = near_source.reshape(CLASSES * 256)
    beside = call(
        near, shape(128, 256), (index, left, own, right, near_table), "svvvv",
        scratch=[VMEM((2304, 128), F32), VMEM((CLASSES, 256, 128), F32)],
        flops=10**10, bytes_accessed=40 << 20, name="near", room=52.5,
    )
    result = call(
        from_grid, shape(128, 256),
        (block_count, site, field.reshape(1024, 128), projection, expand, izh, izl, beside), "svvvvvvv",
        flops=2 * 10**9, bytes_accessed=2 << 20, name="from_grid", room=52.5,
    )
    return result.reshape(2, 64, 256)


def solution(mesh):
    placed = (
        P(None, None, BOTH),
        P(),
        P(None, BOTH, None, None),
        P(),
        P(BOTH),
        P(BOTH),
        P(None, BOTH),
    )
    return jax.shard_map(
        per_device,
        mesh=mesh,
        in_specs=placed,
        out_specs=P(None, None, BOTH),
        check_vma=False,
    )
```

```python
import numpy as np

import jax
import jax.numpy as jnp
from jax import lax
from jax.experimental import pallas as pl
from jax.experimental.pallas import tpu as pltpu
from jax.sharding import PartitionSpec as P

W = 64
N = 4
F32 = jnp.float32
BF16 = jnp.bfloat16
VMEM = pltpu.VMEM
BOTH = ("wide", "narrow")


def halves(table):
    high = table.astype(jnp.bfloat16)
    low = (table - high.astype(np.float64)).astype(jnp.bfloat16)
    return high, low


def split(value):
    high = value.astype(BF16)
    return high, (value - high.astype(F32)).astype(BF16)


def dot(left, right):
    return lax.dot_general(left, right, (((1,), (0,)), ((), ())), preferred_element_type=F32)


def dot_t(left, right):
    return lax.dot_general(left, right, (((1,), (1,)), ((), ())), preferred_element_type=F32)


def dot3(lh, ll, rh, rl):
    return dot(lh, rh) + (dot(lh, rl) + dot(ll, rh))


def tables():
    z = np.arange(128)
    z_of = 4 * (z % 32) + z // 32
    kz = np.arange(256)
    ang = 2 * np.pi * ((kz[:, None] * z_of[None, :]) % 256) / 256
    forward_z = np.concatenate([np.cos(ang), np.sin(ang)], 1)
    inverse_z = np.concatenate([np.cos(ang).T, -np.sin(ang).T], 1) * 2.0**-26
    lane = np.arange(2048)
    group, inner = lane // 128, lane % 128
    ez, ex = group // 4, group % 4
    r, ey = inner // 64, inner // 16 % 2 * 2 + inner // 32 % 2
    row = r * 64 + 16 * ex + 4 * ey + ez
    expand = (np.arange(128)[:, None] == row[None, :]).astype(np.float32)
    k = np.arange(256)
    i = np.arange(256)
    real = (i // 64 % 2 == 0)[:, None]
    along = []
    for p in range(2):
        y = 64 * (i // 128 * 2 + i // 32 % 2) + 4 * (i % 16) + 2 * (i // 16 % 2) + p
        ang = 2 * np.pi * ((y[:, None] * k[None, :]) % 512) / 512
        c, s = np.cos(ang), np.sin(ang)
        along.append(np.concatenate([np.where(real, c, s), np.where(real, -s, c)], 1))
    across = []
    j = np.arange(128)
    for p in range(2):
        x = 4 * (j % 64) + 2 * (j // 64) + p
        ang = 2 * np.pi * ((k[:, None] * x[None, :]) % 512) / 512
        c, s = np.cos(ang), np.sin(ang)
        across.append(np.block([[c, s], [-s, c]]))
    return forward_z, inverse_z, expand, np.stack(along), np.stack(across)


def swap(value):
    lanes = value.shape[1]
    rolled = jnp.concatenate(
        [pltpu.roll(value[:, i : i + 128], 64, 1) for i in range(0, lanes, 128)], axis=1
    )
    sign = jnp.where(lax.broadcasted_iota(jnp.int32, (1, lanes), 1) % 128 < 64, 1.0, -1.0)
    return rolled * sign


def site_masks(count, site):
    rows = lax.broadcasted_iota(jnp.int32, (32, 256), 0)
    line = jnp.where(rows == site % 32, 1.0, 0.0)
    lanes = lax.broadcasted_iota(jnp.int32, (128, 256), 0)
    slots = lax.broadcasted_iota(jnp.int32, (128, 256), 1)
    plane = jnp.where((lanes % 16 == site // 32) & (slots < count), 1.0, 0.0)
    return line, plane.T


def fetch(pairs, sems):
    copies = [pltpu.make_async_copy(s, d, sems.at[i]) for i, (s, d) in enumerate(pairs)]
    for copy in copies:
        copy.start()
    return copies


def to_grid(count_ref, charges_any, site_any, proj_any, expand_any, fh_any, fl_any, out_ref, token_ref,
            charges_ref, site_ref, proj_ref, expand_ref, fh_ref, fl_ref, sems):
    copies = fetch(
        [(charges_any, charges_ref), (proj_any, proj_ref), (site_any, site_ref),
         (expand_any, expand_ref), (fh_any, fh_ref), (fl_any, fl_ref)], sems)
    token_ref[...] = jnp.zeros((8, 128), F32)
    rows = lax.broadcasted_iota(jnp.int32, (128, 256), 0)
    slots = lax.broadcasted_iota(jnp.int32, (128, 256), 1)
    for copy in copies[:3]:
        copy.wait()
    occupied = slots < count_ref[0]
    site = site_ref[...]
    plane = jnp.where((rows % 16 == site // 32) & occupied, 1.0, 0.0).astype(BF16)
    plane = jnp.concatenate([plane] * 4, axis=0)
    masked = jnp.where(occupied, charges_ref[...], 0.0)
    ph, plo = split(proj_ref[...])
    parts = []
    for r in range(2):
        mh, ml = split(masked[64 * r : 64 * r + 64])
        parts.append(dot3(ph, plo, mh, ml))
    both = jnp.concatenate(split(jnp.concatenate(parts, axis=0)), axis=1)
    copies[3].wait()
    grid = jnp.zeros((512, 128), F32)
    for ez in range(4):
        line = jnp.where((rows % 32 == site % 32) & (rows // 32 == ez), 1.0, 0.0).astype(BF16)
        spread = dot(expand_ref[512 * ez : 512 * ez + 512, :], both)
        for h in range(2):
            grid = grid + dot_t(spread[:, 256 * h : 256 * h + 256].astype(BF16) * plane, line)
    turned = []
    for ex in range(4):
        turned += [grid[128 * ex + 64 : 128 * ex + 128], -grid[128 * ex : 128 * ex + 64]]
    gh, gl = split(jnp.concatenate([grid, jnp.concatenate(turned, axis=0)], axis=1))
    copies[4].wait()
    copies[5].wait()
    fh, fl = fh_ref[...], fl_ref[...]
    for e in range(2):
        c = slice(256 * e, 256 * e + 256)
        planes = dot_t(fh, gh[c]) + (dot_t(fh, gl[c]) + dot_t(fl, gh[c]))
        out_ref[pl.ds(2 * e, 256, stride=4), :] = planes[:, :128]
        out_ref[pl.ds(2 * e + 1, 256, stride=4), :] = planes[:, 128:]


def turn(count_ref, charges_ref, after_ref, out_ref):
    slots = lax.broadcasted_iota(jnp.int32, (128, 256), 1)
    out_ref[...] = jnp.where(slots < count_ref[0], charges_ref[...], 0.0).T


def join(a_ref, b_ref, c_ref, out_ref):
    for i, ref in enumerate((a_ref, b_ref, c_ref)):
        out_ref[256 * i : 256 * i + 256, :] = ref[...]


def convolve(in_any, green_any, yh_any, yl_any, xh_any, xl_any, ih_any, il_any, out_ref,
             in_ref, green_ref, yh, yl, xh, xl, ih, il, ah, al, sh, sl, qh, ql, bh, bl, sems):
    (arrived,) = fetch([(in_any, in_ref)], sems)
    copies = fetch(
        [(yh_any, yh), (yl_any, yl), (xh_any, xh), (xl_any, xl), (green_any, green_ref), (ih_any, ih), (il_any, il)],
        sems.at[pl.ds(1, 7)])
    arrived.wait()
    first = lax.broadcasted_iota(jnp.int32, (64, 128), 1) % 64 < 32
    order = (0, 2, 1, 3)
    for i, ex in enumerate(order):
        a = slice(64 * i, 64 * i + 64)
        for m in range(2):
            c = slice(128 * m, 128 * m + 128)
            d0 = in_ref[pl.ds(8 * m + ex, 64, stride=16), :]
            d1 = in_ref[pl.ds(8 * m + 4 + ex, 64, stride=16), :]
            ah[0, a, c], al[0, a, c] = split(jnp.where(first, d0, pltpu.roll(d1, 32, 1)))
            ah[1, a, c], al[1, a, c] = split(jnp.where(first, pltpu.roll(d0, 96, 1), d1))
    copies[0].wait()
    copies[1].wait()
    for r in range(2):
        c = slice(256 * r, 256 * r + 256)
        o = slice(128 * r, 128 * r + 128)
        even = dot3(ah[0], al[0], yh[0, :, c], yl[0, :, c])
        odd = dot3(ah[1], al[1], yh[1, :, c], yl[1, :, c])
        for half, (h, l) in enumerate((split(even + odd), split(even - odd))):
            k = slice(256 * half, 256 * half + 256)
            for xp in range(2):
                sh[xp, o, k] = h[128 * xp : 128 * xp + 128]
                sl[xp, o, k] = l[128 * xp : 128 * xp + 128]
    copies[2].wait()
    copies[3].wait()
    copies[4].wait()
    for j in range(2):
        c = slice(256 * j, 256 * j + 256)
        part = [dot3(xh[xp], xl[xp], sh[xp, :, c], sl[xp, :, c]) for xp in range(2)]
        sums, diffs = part[0] + part[1], part[0] - part[1]
        gr, gi = green_ref[0, 0:256, c], green_ref[1, 0:256, c]
        p_re, p_im = gr * sums[:256] - gi * sums[256:], gr * sums[256:] + gi * sums[:256]
        gr, gi = green_ref[0, 256:512, c], green_ref[1, 256:512, c]
        q_re, q_im = gr * diffs[:256] - gi * diffs[256:], gr * diffs[256:] + gi * diffs[:256]
        qh[0, 0:256, c], ql[0, 0:256, c] = split(p_re + q_re)
        qh[1, 0:256, c], ql[1, 0:256, c] = split(p_re - q_re)
        qh[0, 256:512, c], ql[0, 256:512, c] = split(p_im + q_im)
        qh[1, 256:512, c], ql[1, 256:512, c] = split(p_im - q_im)
    copies[5].wait()
    copies[6].wait()
    for xp in range(2):
        u0, u1 = [dot3(ih[xp], il[xp], qh[xp, :, c], ql[xp, :, c]) for c in (slice(0, 256), slice(256, 512))]
        rows = slice(128 * xp, 128 * xp + 128)
        for p, (h, l) in enumerate((split(u0 + u1), split(u0 - u1))):
            for r in range(2):
                bh[p, rows, 256 * r : 256 * r + 256] = h[128 * r : 128 * r + 128]
                bl[p, rows, 256 * r : 256 * r + 256] = l[128 * r : 128 * r + 128]
    even, odd = [dot_t(bh[p], yh[p]) + (dot_t(bh[p], yl[p]) + dot_t(bl[p], yh[p])) for p in range(2)]
    for e, ex in enumerate(order):
        rows = slice(64 * e, 64 * e + 64)
        for m in range(2):
            c = slice(128 * m, 128 * m + 128)
            ve, vo = even[rows, c], odd[rows, c]
            out_ref[pl.ds(8 * m + ex, 64, stride=16), :] = jnp.where(first, ve, pltpu.roll(vo, 32, 1))
            out_ref[pl.ds(8 * m + 4 + ex, 64, stride=16), :] = jnp.where(first, pltpu.roll(ve, 96, 1), vo)


def from_grid(count_ref, site_ref, in_ref, proj_ref, expand_ref, fh_ref, fl_ref, near_ref, out_ref):
    count = count_ref[0]
    line, plane = site_masks(count, site_ref[...])
    field = jnp.concatenate([in_ref[pl.ds(ex, 256, stride=4), :] for ex in range(4)], axis=1)
    vh, vl = split(jnp.concatenate([field, swap(field)], axis=0))
    points = dot3(fh_ref[...], fl_ref[...], vh, vl)
    bh, bl = split(points)
    pick = line.T.astype(BF16)
    total = jnp.zeros((256, 128), F32)
    for ez in range(4):
        rows = slice(32 * ez, 32 * ez + 32)
        for ex in range(4):
            c = slice(128 * ex, 128 * ex + 128)
            high = (dot(pick, bh[rows, c]) * plane).astype(BF16)
            low = (dot(pick, bl[rows, c]) * plane).astype(BF16)
            lo = (ez * 4 + ex) * 128
            e = expand_ref[:, lo : lo + 128]
            total = total + (dot_t(high, e) + dot_t(low, e))
    th, tl = split(total)
    ph, plo = split(proj_ref[...])
    parts = []
    for r in range(2):
        c = slice(64 * r, 64 * r + 64)
        parts.append(dot3(th[:, c], tl[:, c], ph, plo))
    far = jnp.concatenate(parts, axis=1).T
    slots = lax.broadcasted_iota(jnp.int32, (128, 256), 1)
    out_ref[...] = far + jnp.where(slots < count, near_ref[...], 0.0)


CLASSES = 27


def near(index_ref, left_ref, own_ref, right_ref, table_ref, out_ref, source_ref, picked):
    for i, ref in enumerate((left_ref, own_ref, right_ref)):
        source_ref[768 * i : 768 * i + 768, :] = ref[...]

    def one(k, carry):
        for b in range(256):
            i = index_ref[k * 256 + b]
            picked[k, pl.ds(b, 1), :] = source_ref[pl.ds(i, 1), :]
        return carry

    lax.fori_loop(0, CLASSES, one, 0)
    total = jnp.zeros((256, 128), F32)
    for k in range(CLASSES):
        gh, gl = split(picked[k])
        re, im = table_ref[k, 0], table_ref[k, 1]
        rows = [jnp.concatenate([re, -im], axis=1), jnp.concatenate([im, re], axis=1)]
        th, tl = split(jnp.concatenate(rows, axis=0))
        total = total + (dot_t(gh, th) + (dot_t(gh, tl) + dot_t(gl, th)))
    out_ref[...] = total.T


def call(kernel, outs, args, kinds, scratch=(), copies=0, flops=0, bytes_accessed=0, name=None, out_kind="v", room=40):
    spaces = {"s": pltpu.SMEM, "v": VMEM, "h": pltpu.HBM}
    single = not isinstance(outs, (tuple, list))
    out_spec = pl.BlockSpec(memory_space=spaces[out_kind])
    scratch = list(scratch) + ([pltpu.SemaphoreType.DMA((copies,))] if copies else [])
    return pl.pallas_call(
        kernel,
        out_shape=outs,
        in_specs=[pl.BlockSpec(memory_space=spaces[k]) for k in kinds],
        out_specs=out_spec if single else tuple(out_spec for _ in outs),
        scratch_shapes=scratch,
        compiler_params=pltpu.CompilerParams(vmem_limit_bytes=room << 20),
        cost_estimate=pl.CostEstimate(flops=flops, bytes_accessed=bytes_accessed, transcendentals=0),
        name=name,
    )(*args)


def neighbours(array, axis, size):
    up = [(i, i + 1) for i in range(size - 1)]
    down = [(i + 1, i) for i in range(size - 1)]
    return lax.ppermute(array, axis, up), lax.ppermute(array, axis, down)


def per_device(charges, projection, green_hat, near_table, block_site, block_count, near_source):
    forward_z, inverse_z, expand, along, across = tables()
    fzh, fzl = halves(forward_z)
    izh, izl = halves(inverse_z)
    yh, yl = halves(along)
    xh, xl = halves(across)
    ih, il = halves(np.ascontiguousarray(across.transpose(0, 2, 1)))
    expand = expand.astype(jnp.bfloat16)
    site = block_site.reshape(1, 256)
    shape = lambda *s: jax.ShapeDtypeStruct(s, F32)

    cells = charges.reshape(128, 256)
    sent, token = call(
        to_grid, (shape(1024, 128), shape(8, 128)), (block_count, cells, site, projection, np.ascontiguousarray(expand.T), fzh, fzl), "shhhhhh",
        scratch=[VMEM((128, 256), F32), VMEM((1, 256), jnp.int32), VMEM((64, 64), F32), VMEM((2048, 128), BF16)]
        + [VMEM((256, 256), BF16)] * 2,
        copies=6, flops=2 * 10**9, bytes_accessed=2 << 20, name="to_grid", room=63,
    )
    planes = lax.all_to_all(sent.reshape(256, 4, 128), BOTH, split_axis=0, concat_axis=0, tiled=True)
    masked = call(turn, shape(256, 128), (block_count, cells, token), "svv", bytes_accessed=1 << 20, name="turn", room=16)
    before, after = neighbours(masked, "narrow", N)
    own = call(join, shape(768, 128), (before, masked, after), "vvv", bytes_accessed=2 << 20, name="join", room=16)
    left, _ = neighbours(own, "wide", W)
    later, planes = lax.optimization_barrier((own, planes))
    _, right = neighbours(later, "wide", W)
    back = call(
        convolve, shape(1024, 128),
        (planes.reshape(1024, 128), green_hat.reshape(2, 512, 512), yh, yl, xh, xl, ih, il), "hhhhhhhh",
        scratch=[VMEM((1024, 128), F32), VMEM((2, 512, 512), F32)] + [VMEM((2, 256, 512), BF16)] * 2 + [VMEM((2, 512, 256), BF16)] * 2
        + [VMEM((2, 256, 512), BF16)] * 2 + [VMEM((2, 256, 256), BF16)] * 2 + [VMEM((2, 256, 512), BF16)] * 2
        + [VMEM((2, 512, 512), BF16)] * 2 + [VMEM((2, 256, 512), BF16)] * 2,
        copies=8, flops=5 * 10**9, bytes_accessed=9 << 20, name="convolve", room=63,
    )
    field = lax.all_to_all(back.reshape(256, 4, 128), BOTH, split_axis=0, concat_axis=0, tiled=True)
    index = near_source.reshape(CLASSES * 256)
    beside = call(
        near, shape(128, 256), (index, left, own, right, near_table), "svvvv",
        scratch=[VMEM((2304, 128), F32), VMEM((CLASSES, 256, 128), F32)],
        flops=10**10, bytes_accessed=40 << 20, name="near", room=16,
    )
    result = call(
        from_grid, shape(128, 256),
        (block_count, site, field.reshape(1024, 128), projection, expand, izh, izl, beside), "svvvvvvv",
        flops=2 * 10**9, bytes_accessed=2 << 20, name="from_grid", room=12,
    )
    return result.reshape(2, 64, 256)


def solution(mesh):
    placed = (
        P(None, None, BOTH),
        P(),
        P(None, BOTH, None, None),
        P(),
        P(BOTH),
        P(BOTH),
        P(None, BOTH),
    )
    return jax.shard_map(
        per_device,
        mesh=mesh,
        in_specs=placed,
        out_specs=P(None, None, BOTH),
        check_vma=False,
    )
```

```python
import numpy as np

import jax
import jax.numpy as jnp
from jax import lax
from jax.experimental import pallas as pl
from jax.experimental.pallas import tpu as pltpu
from jax.sharding import PartitionSpec as P

W = 64
N = 4
F32 = jnp.float32
BF16 = jnp.bfloat16
VMEM = pltpu.VMEM
BOTH = ("wide", "narrow")


def halves(table):
    high = table.astype(jnp.bfloat16)
    low = (table - high.astype(np.float64)).astype(jnp.bfloat16)
    return high, low


def split(value):
    high = value.astype(BF16)
    return high, (value - high.astype(F32)).astype(BF16)


def dot(left, right):
    return lax.dot_general(left, right, (((1,), (0,)), ((), ())), preferred_element_type=F32)


def dot_t(left, right):
    return lax.dot_general(left, right, (((1,), (1,)), ((), ())), preferred_element_type=F32)


def dot3(lh, ll, rh, rl):
    return dot(lh, rh) + (dot(lh, rl) + dot(ll, rh))


def dot_l(left, right):
    return lax.dot_general(left, right, (((0,), (0,)), ((), ())), preferred_element_type=F32)


def tables():
    z = np.arange(128)
    z_of = 4 * (z % 32) + z // 32
    kz = np.arange(256)
    ang = 2 * np.pi * ((kz[:, None] * z_of[None, :]) % 256) / 256
    forward_z = np.concatenate([np.cos(ang), np.sin(ang)], 1)
    inverse_z = np.concatenate([np.cos(ang).T, -np.sin(ang).T], 1) * 2.0**-26
    lane = np.arange(2048)
    group, inner = lane // 128, lane % 128
    ez, ex = group // 4, group % 4
    r, ey = inner // 64, inner // 16 % 2 * 2 + inner // 32 % 2
    row = r * 64 + 16 * ex + 4 * ey + ez
    expand = (np.arange(128)[:, None] == row[None, :]).astype(np.float32)
    k = np.arange(256)
    i = np.arange(256)
    real = (i // 64 % 2 == 0)[:, None]
    along = []
    for p in range(2):
        y = 64 * (i // 128 * 2 + i // 32 % 2) + 4 * (i % 16) + 2 * (i // 16 % 2) + p
        ang = 2 * np.pi * ((y[:, None] * k[None, :]) % 512) / 512
        c, s = np.cos(ang), np.sin(ang)
        along.append(np.concatenate([np.where(real, c, s), np.where(real, -s, c)], 1))
    return forward_z, inverse_z, expand, np.stack(along)


def swap(value):
    lanes = value.shape[1]
    rolled = jnp.concatenate(
        [pltpu.roll(value[:, i : i + 128], 64, 1) for i in range(0, lanes, 128)], axis=1
    )
    sign = jnp.where(lax.broadcasted_iota(jnp.int32, (1, lanes), 1) % 128 < 64, 1.0, -1.0)
    return rolled * sign


def site_masks(count, site):
    rows = lax.broadcasted_iota(jnp.int32, (32, 256), 0)
    line = jnp.where(rows == site % 32, 1.0, 0.0)
    lanes = lax.broadcasted_iota(jnp.int32, (128, 256), 0)
    slots = lax.broadcasted_iota(jnp.int32, (128, 256), 1)
    plane = jnp.where((lanes % 16 == site // 32) & (slots < count), 1.0, 0.0)
    return line, plane.T


def fetch(pairs, sems):
    copies = [pltpu.make_async_copy(s, d, sems.at[i]) for i, (s, d) in enumerate(pairs)]
    for copy in copies:
        copy.start()
    return copies


def to_grid(count_ref, charges_any, site_any, proj_any, expand_any, fh_any, fl_any, out_ref, token_ref,
            charges_ref, site_ref, proj_ref, expand_ref, fh_ref, fl_ref, sems):
    copies = fetch(
        [(charges_any, charges_ref), (proj_any, proj_ref), (site_any, site_ref),
         (expand_any, expand_ref), (fh_any, fh_ref), (fl_any, fl_ref)], sems)
    token_ref[...] = jnp.zeros((8, 128), F32)
    rows = lax.broadcasted_iota(jnp.int32, (128, 256), 0)
    slots = lax.broadcasted_iota(jnp.int32, (128, 256), 1)
    for copy in copies[:3]:
        copy.wait()
    occupied = slots < count_ref[0]
    site = site_ref[...]
    plane = jnp.where((rows % 16 == site // 32) & occupied, 1.0, 0.0).astype(BF16)
    plane = jnp.concatenate([plane] * 4, axis=0)
    masked = jnp.where(occupied, charges_ref[...], 0.0)
    ph, plo = split(proj_ref[...])
    parts = []
    for r in range(2):
        mh, ml = split(masked[64 * r : 64 * r + 64])
        parts.append(dot3(ph, plo, mh, ml))
    both = jnp.concatenate(split(jnp.concatenate(parts, axis=0)), axis=1)
    copies[3].wait()
    grid = jnp.zeros((512, 128), F32)
    for ez in range(4):
        line = jnp.where((rows % 32 == site % 32) & (rows // 32 == ez), 1.0, 0.0).astype(BF16)
        spread = dot(expand_ref[512 * ez : 512 * ez + 512, :], both)
        for h in range(2):
            grid = grid + dot_t(spread[:, 256 * h : 256 * h + 256].astype(BF16) * plane, line)
    turned = []
    for ex in range(4):
        turned += [grid[128 * ex + 64 : 128 * ex + 128], -grid[128 * ex : 128 * ex + 64]]
    gh, gl = split(jnp.concatenate([grid, jnp.concatenate(turned, axis=0)], axis=1))
    copies[4].wait()
    copies[5].wait()
    fh, fl = fh_ref[...], fl_ref[...]
    for e in range(2):
        c = slice(256 * e, 256 * e + 256)
        planes = dot_t(fh, gh[c]) + (dot_t(fh, gl[c]) + dot_t(fl, gh[c]))
        out_ref[pl.ds(2 * e, 256, stride=4), :] = planes[:, :128]
        out_ref[pl.ds(2 * e + 1, 256, stride=4), :] = planes[:, 128:]


def turn(count_ref, charges_ref, after_ref, out_ref):
    slots = lax.broadcasted_iota(jnp.int32, (128, 256), 1)
    out_ref[...] = jnp.where(slots < count_ref[0], charges_ref[...], 0.0).T


def join(even_ref, own_ref, odd_ref, out_ref):
    last = lax.axis_index("narrow") % 2
    out_ref[pl.ds(pl.multiple_of(512 - 512 * last, 512), 256), :] = even_ref[...]
    out_ref[256:512, :] = own_ref[...]
    out_ref[pl.ds(pl.multiple_of(512 * last, 512), 256), :] = odd_ref[...]


def convolve(in_any, th_any, tl_any, green_any, out_ref,
             in_ref, th, tl, green_ref, ah, al, sh, sl, qh, ql, bh, bl, sems):
    arrived, *copies = fetch([(in_any, in_ref), (th_any, th), (tl_any, tl), (green_any, green_ref)], sems)
    arrived.wait()
    first = lax.broadcasted_iota(jnp.int32, (64, 128), 1) % 64 < 32
    for ex in range(4):
        base = ex % 2 * 128 + ex // 2 * 16
        for m in range(2):
            c = slice(128 * m, 128 * m + 128)
            d0 = in_ref[pl.ds(8 * m + ex, 64, stride=16), :]
            d1 = in_ref[pl.ds(8 * m + 4 + ex, 64, stride=16), :]
            pieces = split(jnp.where(first, d0, pltpu.roll(d1, 32, 1))), split(jnp.where(first, pltpu.roll(d0, 96, 1), d1))
            for p, (h, l) in enumerate(pieces):
                for w in range(4):
                    a = slice(base + 32 * w, base + 32 * w + 16)
                    ah[p, a, c], al[p, a, c] = h[16 * w : 16 * w + 16], l[16 * w : 16 * w + 16]
    copies[0].wait()
    copies[1].wait()
    for r in range(2):
        c = slice(256 * r, 256 * r + 256)
        even = dot3(ah[0], al[0], th[0, :, c], tl[0, :, c])
        odd = dot3(ah[1], al[1], th[1, :, c], tl[1, :, c])
        for half, (h, l) in enumerate((split(even + odd), split(even - odd))):
            k = slice(256 * half, 256 * half + 256)
            for xp in range(2):
                for m in range(2):
                    o, a = slice(128 * m + 64 * r, 128 * m + 64 * r + 64), slice(128 * xp + 64 * m, 128 * xp + 64 * m + 64)
                    sh[xp, o, k], sl[xp, o, k] = h[a], l[a]
    copies[2].wait()
    for j in range(2):
        c = slice(256 * j, 256 * j + 256)
        part = []
        for xp in range(2):
            h, l = sh[xp, :, c], sl[xp, :, c]
            part.append(dot_l(th[xp], h) + (dot_l(th[xp], l) + dot_l(tl[xp], h)))
        sums, diffs = part[0] + part[1], part[0] - part[1]
        gr, gi = green_ref[0, 0:256, c], green_ref[1, 0:256, c]
        p_re, p_im = gr * sums[:256] - gi * sums[256:], gr * sums[256:] + gi * sums[:256]
        gr, gi = green_ref[0, 256:512, c], green_ref[1, 256:512, c]
        q_re, q_im = gr * diffs[:256] - gi * diffs[256:], gr * diffs[256:] + gi * diffs[:256]
        qh[0, 0:256, c], ql[0, 0:256, c] = split(p_re + q_re)
        qh[1, 0:256, c], ql[1, 0:256, c] = split(p_re - q_re)
        qh[0, 256:512, c], ql[0, 256:512, c] = split(p_im + q_im)
        qh[1, 256:512, c], ql[1, 256:512, c] = split(p_im - q_im)
    for xp in range(2):
        u0, u1 = [dot3(th[xp], tl[xp], qh[xp, :, c], ql[xp, :, c]) for c in (slice(0, 256), slice(256, 512))]
        for p, (h, l) in enumerate((split(u0 + u1), split(u0 - u1))):
            for r in range(2):
                for m in range(2):
                    o, a = slice(128 * m + 64 * r, 128 * m + 64 * r + 64), slice(128 * xp + 64 * m, 128 * xp + 64 * m + 64)
                    k = slice(256 * r, 256 * r + 256)
                    bh[p, a, k], bl[p, a, k] = h[o], l[o]
    even, odd = [dot_t(bh[p], th[p]) + (dot_t(bh[p], tl[p]) + dot_t(bl[p], th[p])) for p in range(2)]
    first = first[:16]
    for ex in range(4):
        base = ex % 2 * 128 + ex // 2 * 16
        for w in range(4):
            rows = slice(base + 32 * w, base + 32 * w + 16)
            for m in range(2):
                c = slice(128 * m, 128 * m + 128)
                ve, vo = even[rows, c], odd[rows, c]
                place = 256 * w + 8 * m + ex
                out_ref[pl.ds(place, 16, stride=16), :] = jnp.where(first, ve, pltpu.roll(vo, 32, 1))
                out_ref[pl.ds(place + 4, 16, stride=16), :] = jnp.where(first, pltpu.roll(ve, 96, 1), vo)


def from_grid(count_ref, site_ref, in_ref, proj_ref, expand_ref, fh_ref, fl_ref, near_ref, out_ref):
    count = count_ref[0]
    line, plane = site_masks(count, site_ref[...])
    field = jnp.concatenate([in_ref[pl.ds(ex, 256, stride=4), :] for ex in range(4)], axis=1)
    vh, vl = split(jnp.concatenate([field, swap(field)], axis=0))
    points = dot3(fh_ref[...], fl_ref[...], vh, vl)
    bh, bl = split(points)
    pick = line.T.astype(BF16)
    total = jnp.zeros((256, 128), F32)
    for ez in range(4):
        rows = slice(32 * ez, 32 * ez + 32)
        for ex in range(4):
            c = slice(128 * ex, 128 * ex + 128)
            high = (dot(pick, bh[rows, c]) * plane).astype(BF16)
            low = (dot(pick, bl[rows, c]) * plane).astype(BF16)
            lo = (ez * 4 + ex) * 128
            e = expand_ref[:, lo : lo + 128]
            total = total + (dot_t(high, e) + dot_t(low, e))
    th, tl = split(total)
    ph, plo = split(proj_ref[...])
    parts = []
    for r in range(2):
        c = slice(64 * r, 64 * r + 64)
        parts.append(dot3(th[:, c], tl[:, c], ph, plo))
    far = jnp.concatenate(parts, axis=1).T
    slots = lax.broadcasted_iota(jnp.int32, (128, 256), 1)
    out_ref[...] = far + jnp.where(slots < count, near_ref[...], 0.0)


CLASSES = 27


def near(index_ref, even_ref, own_ref, odd_ref, table_ref, out_ref, source_ref, picked):
    last = lax.axis_index("wide") % 2
    source_ref[pl.ds(pl.multiple_of(1536 - 1536 * last, 512), 768), :] = even_ref[...]
    source_ref[768:1536, :] = own_ref[...]
    source_ref[pl.ds(pl.multiple_of(1536 * last, 512), 768), :] = odd_ref[...]

    def one(k, carry):
        for b in range(256):
            i = index_ref[k * 256 + b]
            picked[k, pl.ds(b, 1), :] = source_ref[pl.ds(i, 1), :]
        return carry

    lax.fori_loop(0, CLASSES, one, 0)
    total = jnp.zeros((256, 128), F32)
    for k in range(CLASSES):
        gh, gl = split(picked[k])
        re, im = table_ref[k, 0], table_ref[k, 1]
        rows = [jnp.concatenate([re, -im], axis=1), jnp.concatenate([im, re], axis=1)]
        th, tl = split(jnp.concatenate(rows, axis=0))
        total = total + (dot_t(gh, th) + (dot_t(gh, tl) + dot_t(gl, th)))
    out_ref[...] = total.T


def call(kernel, outs, args, kinds, scratch=(), copies=0, flops=0, bytes_accessed=0, name=None, out_kind="v", room=40):
    spaces = {"s": pltpu.SMEM, "v": VMEM, "h": pltpu.HBM}
    single = not isinstance(outs, (tuple, list))
    out_spec = pl.BlockSpec(memory_space=spaces[out_kind])
    scratch = list(scratch) + ([pltpu.SemaphoreType.DMA((copies,))] if copies else [])
    return pl.pallas_call(
        kernel,
        out_shape=outs,
        in_specs=[pl.BlockSpec(memory_space=spaces[k]) for k in kinds],
        out_specs=out_spec if single else tuple(out_spec for _ in outs),
        scratch_shapes=scratch,
        compiler_params=pltpu.CompilerParams(vmem_limit_bytes=room << 20),
        cost_estimate=pl.CostEstimate(flops=flops, bytes_accessed=bytes_accessed, transcendentals=0),
        name=name,
    )(*args)


def swap_pairs(array, axis, size, first):
    pairs = [(i, i + 1) for i in range(first, size - 1, 2)]
    return lax.ppermute(array, axis, pairs + [(j, i) for i, j in pairs])


def per_device(charges, projection, green_hat, near_table, block_site, block_count, near_source):
    forward_z, inverse_z, expand, along = tables()
    fzh, fzl = halves(forward_z)
    izh, izl = halves(inverse_z)
    yh, yl = halves(along)
    expand = expand.astype(jnp.bfloat16)
    site = block_site.reshape(1, 256)
    shape = lambda *s: jax.ShapeDtypeStruct(s, F32)

    cells = charges.reshape(128, 256)
    sent, token = call(
        to_grid, (shape(1024, 128), shape(8, 128)), (block_count, cells, site, projection, np.ascontiguousarray(expand.T), fzh, fzl), "shhhhhh",
        scratch=[VMEM((128, 256), F32), VMEM((1, 256), jnp.int32), VMEM((64, 64), F32), VMEM((2048, 128), BF16)]
        + [VMEM((256, 256), BF16)] * 2,
        copies=6, flops=2 * 10**9, bytes_accessed=2 << 20, name="to_grid", room=63,
    )
    planes = lax.all_to_all(sent.reshape(256, 4, 128), BOTH, split_axis=0, concat_axis=0, tiled=True)
    masked = call(turn, shape(256, 128), (block_count, cells, token), "svv", bytes_accessed=1 << 20, name="turn", room=16)
    odd = swap_pairs(masked, "narrow", N, 1)
    even = swap_pairs(masked, "narrow", N, 0)
    own = call(join, shape(768, 128), (even, masked, odd), "vvv", bytes_accessed=2 << 20, name="join", room=16)
    odd = swap_pairs(own, "wide", W, 1)
    later, planes = lax.optimization_barrier((own, planes))
    even = swap_pairs(later, "wide", W, 0)
    back = call(
        convolve, shape(1024, 128),
        (planes.reshape(1024, 128), yh, yl, green_hat.reshape(2, 512, 512)), "hhhh",
        scratch=[VMEM((1024, 128), F32)] + [VMEM((2, 256, 512), BF16)] * 2 + [VMEM((2, 512, 512), F32)]
        + [VMEM((2, 256, 256), BF16)] * 2 + [VMEM((2, 256, 512), BF16)] * 2
        + [VMEM((2, 512, 512), BF16)] * 2 + [VMEM((2, 256, 512), BF16)] * 2,
        copies=4, flops=5 * 10**9, bytes_accessed=9 << 20, name="convolve", room=63,
    )
    field = lax.all_to_all(back.reshape(256, 4, 128), BOTH, split_axis=0, concat_axis=0, tiled=True)
    index = near_source.reshape(CLASSES * 256)
    beside = call(
        near, shape(128, 256), (index, even, own, odd, near_table), "svvvv",
        scratch=[VMEM((2304, 128), F32), VMEM((CLASSES, 256, 128), F32)],
        flops=10**10, bytes_accessed=40 << 20, name="near", room=16,
    )
    result = call(
        from_grid, shape(128, 256),
        (block_count, site, field.reshape(1024, 128), projection, expand, izh, izl, beside), "svvvvvvv",
        flops=2 * 10**9, bytes_accessed=2 << 20, name="from_grid", room=12,
    )
    return result.reshape(2, 64, 256)


def solution(mesh):
    placed = (
        P(None, None, BOTH),
        P(),
        P(None, BOTH, None, None),
        P(),
        P(BOTH),
        P(BOTH),
        P(None, BOTH),
    )
    return jax.shard_map(
        per_device,
        mesh=mesh,
        in_specs=placed,
        out_specs=P(None, None, BOTH),
        check_vma=False,
    )
```

```python
import numpy as np

import jax
import jax.numpy as jnp
from jax import lax
from jax.experimental import pallas as pl
from jax.experimental.pallas import tpu as pltpu
from jax.sharding import PartitionSpec as P

W = 64
N = 4
F32 = jnp.float32
BF16 = jnp.bfloat16
VMEM = pltpu.VMEM
BOTH = ("wide", "narrow")


def halves(table):
    high = table.astype(jnp.bfloat16)
    low = (table - high.astype(np.float64)).astype(jnp.bfloat16)
    return high, low


def split(value):
    high = value.astype(BF16)
    return high, (value - high.astype(F32)).astype(BF16)


def dot(left, right):
    return lax.dot_general(left, right, (((1,), (0,)), ((), ())), preferred_element_type=F32)


def dot_t(left, right):
    return lax.dot_general(left, right, (((1,), (1,)), ((), ())), preferred_element_type=F32)


def dot3(lh, ll, rh, rl):
    return dot(lh, rh) + (dot(lh, rl) + dot(ll, rh))


def dot_l(left, right):
    return lax.dot_general(left, right, (((0,), (0,)), ((), ())), preferred_element_type=F32)


def tables():
    z = np.arange(128)
    z_of = 4 * (z % 32) + z // 32
    kz = np.arange(256)
    ang = 2 * np.pi * ((kz[:, None] * z_of[None, :]) % 256) / 256
    forward_z = np.concatenate([np.cos(ang), np.sin(ang)], 1)
    inverse_z = np.concatenate([np.cos(ang).T, -np.sin(ang).T], 1) * 2.0**-26
    lane = np.arange(2048)
    group, inner = lane // 128, lane % 128
    ez, ex = group // 4, group % 4
    r, ey = inner // 64, inner // 16 % 2 * 2 + inner // 32 % 2
    row = r * 64 + 16 * ex + 4 * ey + ez
    expand = (np.arange(128)[:, None] == row[None, :]).astype(np.float32)
    k = np.arange(256)
    i = np.arange(256)
    real = (i // 64 % 2 == 0)[:, None]
    along = []
    for p in range(2):
        y = 64 * (i // 128 * 2 + i // 32 % 2) + 4 * (i % 16) + 2 * (i // 16 % 2) + p
        ang = 2 * np.pi * ((y[:, None] * k[None, :]) % 512) / 512
        c, s = np.cos(ang), np.sin(ang)
        along.append(np.concatenate([np.where(real, c, s), np.where(real, -s, c)], 1))
    return forward_z, inverse_z, expand, np.stack(along)


def swap(value):
    lanes = value.shape[1]
    rolled = jnp.concatenate(
        [pltpu.roll(value[:, i : i + 128], 64, 1) for i in range(0, lanes, 128)], axis=1
    )
    sign = jnp.where(lax.broadcasted_iota(jnp.int32, (1, lanes), 1) % 128 < 64, 1.0, -1.0)
    return rolled * sign


def site_masks(count, site):
    rows = lax.broadcasted_iota(jnp.int32, (32, 256), 0)
    line = jnp.where(rows == site % 32, 1.0, 0.0)
    lanes = lax.broadcasted_iota(jnp.int32, (128, 256), 0)
    slots = lax.broadcasted_iota(jnp.int32, (128, 256), 1)
    plane = jnp.where((lanes % 16 == site // 32) & (slots < count), 1.0, 0.0)
    return line, plane.T


def fetch(pairs, sems):
    copies = [pltpu.make_async_copy(s, d, sems.at[i]) for i, (s, d) in enumerate(pairs)]
    for copy in copies:
        copy.start()
    return copies


def to_grid(count_ref, charges_any, site_any, proj_any, expand_any, fh_any, fl_any, out_ref, token_ref,
            charges_ref, site_ref, proj_ref, expand_ref, fh_ref, fl_ref, sems):
    copies = fetch(
        [(charges_any, charges_ref), (proj_any, proj_ref), (site_any, site_ref),
         (expand_any, expand_ref), (fh_any, fh_ref), (fl_any, fl_ref)], sems)
    token_ref[...] = jnp.zeros((8, 128), F32)
    rows = lax.broadcasted_iota(jnp.int32, (128, 256), 0)
    slots = lax.broadcasted_iota(jnp.int32, (128, 256), 1)
    for copy in copies[:3]:
        copy.wait()
    occupied = slots < count_ref[0]
    site = site_ref[...]
    plane = jnp.where((rows % 16 == site // 32) & occupied, 1.0, 0.0).astype(BF16)
    plane = jnp.concatenate([plane] * 4, axis=0)
    masked = jnp.where(occupied, charges_ref[...], 0.0)
    ph, plo = split(proj_ref[...])
    parts = []
    for r in range(2):
        mh, ml = split(masked[64 * r : 64 * r + 64])
        parts.append(dot3(ph, plo, mh, ml))
    both = jnp.concatenate(split(jnp.concatenate(parts, axis=0)), axis=1)
    copies[3].wait()
    grid = jnp.zeros((512, 128), F32)
    for ez in range(4):
        line = jnp.where((rows % 32 == site % 32) & (rows // 32 == ez), 1.0, 0.0).astype(BF16)
        spread = dot(expand_ref[512 * ez : 512 * ez + 512, :], both)
        for h in range(2):
            grid = grid + dot_t(spread[:, 256 * h : 256 * h + 256].astype(BF16) * plane, line)
    turned = []
    for ex in range(4):
        turned += [grid[128 * ex + 64 : 128 * ex + 128], -grid[128 * ex : 128 * ex + 64]]
    gh, gl = split(jnp.concatenate([grid, jnp.concatenate(turned, axis=0)], axis=1))
    copies[4].wait()
    copies[5].wait()
    fh, fl = fh_ref[...], fl_ref[...]
    for e in range(2):
        c = slice(256 * e, 256 * e + 256)
        planes = dot_t(fh, gh[c]) + (dot_t(fh, gl[c]) + dot_t(fl, gh[c]))
        out_ref[pl.ds(2 * e, 256, stride=4), :] = planes[:, :128]
        out_ref[pl.ds(2 * e + 1, 256, stride=4), :] = planes[:, 128:]


def turn(count_ref, charges_ref, *refs):
    out_ref = refs[-1]
    slots = lax.broadcasted_iota(jnp.int32, (128, 256), 1)
    out_ref[...] = jnp.where(slots < count_ref[0], charges_ref[...], 0.0).T


def join(even_ref, own_ref, odd_ref, out_ref):
    last = lax.axis_index("narrow") % 2
    out_ref[pl.ds(pl.multiple_of(512 - 512 * last, 512), 256), :] = even_ref[...]
    out_ref[256:512, :] = own_ref[...]
    out_ref[pl.ds(pl.multiple_of(512 * last, 512), 256), :] = odd_ref[...]


def convolve(in_any, th_any, tl_any, green_any, out_ref,
             in_ref, th, tl, green_ref, ah, al, sh, sl, qh, ql, bh, bl, sems):
    arrived, *copies = fetch([(in_any, in_ref), (th_any, th), (tl_any, tl), (green_any, green_ref)], sems)
    arrived.wait()
    first = lax.broadcasted_iota(jnp.int32, (64, 128), 1) % 64 < 32
    for ex in range(4):
        base = ex % 2 * 128 + ex // 2 * 16
        for m in range(2):
            c = slice(128 * m, 128 * m + 128)
            d0 = in_ref[pl.ds(8 * m + ex, 64, stride=16), :]
            d1 = in_ref[pl.ds(8 * m + 4 + ex, 64, stride=16), :]
            pieces = split(jnp.where(first, d0, pltpu.roll(d1, 32, 1))), split(jnp.where(first, pltpu.roll(d0, 96, 1), d1))
            for p, (h, l) in enumerate(pieces):
                for w in range(4):
                    a = slice(base + 32 * w, base + 32 * w + 16)
                    ah[p, a, c], al[p, a, c] = h[16 * w : 16 * w + 16], l[16 * w : 16 * w + 16]
    copies[0].wait()
    copies[1].wait()
    for r in range(2):
        c = slice(256 * r, 256 * r + 256)
        even = dot3(ah[0], al[0], th[0, :, c], tl[0, :, c])
        odd = dot3(ah[1], al[1], th[1, :, c], tl[1, :, c])
        for half, (h, l) in enumerate((split(even + odd), split(even - odd))):
            k = slice(256 * half, 256 * half + 256)
            for xp in range(2):
                for m in range(2):
                    o, a = slice(128 * m + 64 * r, 128 * m + 64 * r + 64), slice(128 * xp + 64 * m, 128 * xp + 64 * m + 64)
                    sh[xp, o, k], sl[xp, o, k] = h[a], l[a]
    copies[2].wait()
    for j in range(2):
        c = slice(256 * j, 256 * j + 256)
        part = []
        for xp in range(2):
            h, l = sh[xp, :, c], sl[xp, :, c]
            part.append(dot_l(th[xp], h) + (dot_l(th[xp], l) + dot_l(tl[xp], h)))
        sums, diffs = part[0] + part[1], part[0] - part[1]
        gr, gi = green_ref[0, 0:256, c], green_ref[1, 0:256, c]
        p_re, p_im = gr * sums[:256] - gi * sums[256:], gr * sums[256:] + gi * sums[:256]
        gr, gi = green_ref[0, 256:512, c], green_ref[1, 256:512, c]
        q_re, q_im = gr * diffs[:256] - gi * diffs[256:], gr * diffs[256:] + gi * diffs[:256]
        qh[0, 0:256, c], ql[0, 0:256, c] = split(p_re + q_re)
        qh[1, 0:256, c], ql[1, 0:256, c] = split(p_re - q_re)
        qh[0, 256:512, c], ql[0, 256:512, c] = split(p_im + q_im)
        qh[1, 256:512, c], ql[1, 256:512, c] = split(p_im - q_im)
    for xp in range(2):
        u0, u1 = [dot3(th[xp], tl[xp], qh[xp, :, c], ql[xp, :, c]) for c in (slice(0, 256), slice(256, 512))]
        for p, (h, l) in enumerate((split(u0 + u1), split(u0 - u1))):
            for r in range(2):
                for m in range(2):
                    o, a = slice(128 * m + 64 * r, 128 * m + 64 * r + 64), slice(128 * xp + 64 * m, 128 * xp + 64 * m + 64)
                    k = slice(256 * r, 256 * r + 256)
                    bh[p, a, k], bl[p, a, k] = h[o], l[o]
    even, odd = [dot_t(bh[p], th[p]) + (dot_t(bh[p], tl[p]) + dot_t(bl[p], th[p])) for p in range(2)]
    first = first[:16]
    for ex in range(4):
        base = ex % 2 * 128 + ex // 2 * 16
        for w in range(4):
            rows = slice(base + 32 * w, base + 32 * w + 16)
            for m in range(2):
                c = slice(128 * m, 128 * m + 128)
                ve, vo = even[rows, c], odd[rows, c]
                place = 256 * w + 8 * m + ex
                out_ref[pl.ds(place, 16, stride=16), :] = jnp.where(first, ve, pltpu.roll(vo, 32, 1))
                out_ref[pl.ds(place + 4, 16, stride=16), :] = jnp.where(first, pltpu.roll(ve, 96, 1), vo)


def from_grid(count_ref, site_ref, in_ref, proj_ref, expand_ref, fh_ref, fl_ref, near_ref, out_ref):
    count = count_ref[0]
    line, plane = site_masks(count, site_ref[...])
    field = jnp.concatenate([in_ref[pl.ds(ex, 256, stride=4), :] for ex in range(4)], axis=1)
    vh, vl = split(jnp.concatenate([field, swap(field)], axis=0))
    points = dot3(fh_ref[...], fl_ref[...], vh, vl)
    bh, bl = split(points)
    pick = line.T.astype(BF16)
    total = jnp.zeros((256, 128), F32)
    for ez in range(4):
        rows = slice(32 * ez, 32 * ez + 32)
        for ex in range(4):
            c = slice(128 * ex, 128 * ex + 128)
            high = (dot(pick, bh[rows, c]) * plane).astype(BF16)
            low = (dot(pick, bl[rows, c]) * plane).astype(BF16)
            lo = (ez * 4 + ex) * 128
            e = expand_ref[:, lo : lo + 128]
            total = total + (dot_t(high, e) + dot_t(low, e))
    th, tl = split(total)
    ph, plo = split(proj_ref[...])
    parts = []
    for r in range(2):
        c = slice(64 * r, 64 * r + 64)
        parts.append(dot3(th[:, c], tl[:, c], ph, plo))
    far = jnp.concatenate(parts, axis=1).T
    slots = lax.broadcasted_iota(jnp.int32, (128, 256), 1)
    out_ref[...] = far + jnp.where(slots < count, near_ref[...], 0.0)


CLASSES = 27


def near(index_ref, even_ref, own_ref, odd_ref, table_ref, out_ref, source_ref, picked):
    last = lax.axis_index("wide") % 2
    source_ref[pl.ds(pl.multiple_of(1536 - 1536 * last, 512), 768), :] = even_ref[...]
    source_ref[768:1536, :] = own_ref[...]
    source_ref[pl.ds(pl.multiple_of(1536 * last, 512), 768), :] = odd_ref[...]

    def one(k, carry):
        for b in range(256):
            i = index_ref[k * 256 + b]
            picked[k, pl.ds(b, 1), :] = source_ref[pl.ds(i, 1), :]
        return carry

    lax.fori_loop(0, CLASSES, one, 0)
    total = jnp.zeros((256, 128), F32)
    for k in range(CLASSES):
        gh, gl = split(picked[k])
        re, im = table_ref[k, 0], table_ref[k, 1]
        rows = [jnp.concatenate([re, -im], axis=1), jnp.concatenate([im, re], axis=1)]
        th, tl = split(jnp.concatenate(rows, axis=0))
        total = total + (dot_t(gh, th) + (dot_t(gh, tl) + dot_t(gl, th)))
    out_ref[...] = total.T


def call(kernel, outs, args, kinds, scratch=(), copies=0, flops=0, bytes_accessed=0, name=None, out_kind="v", room=40):
    spaces = {"s": pltpu.SMEM, "v": VMEM, "h": pltpu.HBM}
    single = not isinstance(outs, (tuple, list))
    out_spec = pl.BlockSpec(memory_space=spaces[out_kind])
    scratch = list(scratch) + ([pltpu.SemaphoreType.DMA((copies,))] if copies else [])
    return pl.pallas_call(
        kernel,
        out_shape=outs,
        in_specs=[pl.BlockSpec(memory_space=spaces[k]) for k in kinds],
        out_specs=out_spec if single else tuple(out_spec for _ in outs),
        scratch_shapes=scratch,
        compiler_params=pltpu.CompilerParams(vmem_limit_bytes=room << 20),
        cost_estimate=pl.CostEstimate(flops=flops, bytes_accessed=bytes_accessed, transcendentals=0),
        name=name,
    )(*args)


def swap_pairs(array, axis, size, first):
    pairs = [(i, i + 1) for i in range(first, size - 1, 2)]
    return lax.ppermute(array, axis, pairs + [(j, i) for i, j in pairs])


def per_device(charges, projection, green_hat, near_table, block_site, block_count, near_source):
    forward_z, inverse_z, expand, along = tables()
    fzh, fzl = halves(forward_z)
    izh, izl = halves(inverse_z)
    yh, yl = halves(along)
    expand = expand.astype(jnp.bfloat16)
    site = block_site.reshape(1, 256)
    shape = lambda *s: jax.ShapeDtypeStruct(s, F32)

    cells = charges.reshape(128, 256)
    early = call(turn, shape(256, 128), (block_count, cells), "sv", bytes_accessed=1 << 20, name="turn_early", room=16)
    odd = swap_pairs(early, "narrow", N, 1)
    sent, token = call(
        to_grid, (shape(1024, 128), shape(8, 128)), (block_count, cells, site, projection, np.ascontiguousarray(expand.T), fzh, fzl), "shhhhhh",
        scratch=[VMEM((128, 256), F32), VMEM((1, 256), jnp.int32), VMEM((64, 64), F32), VMEM((2048, 128), BF16)]
        + [VMEM((256, 256), BF16)] * 2,
        copies=6, flops=2 * 10**9, bytes_accessed=2 << 20, name="to_grid", room=63,
    )
    sent, odd = lax.optimization_barrier((sent, odd))
    planes = lax.all_to_all(sent.reshape(256, 4, 128), BOTH, split_axis=0, concat_axis=0, tiled=True)
    masked = call(turn, shape(256, 128), (block_count, cells, token), "svv", bytes_accessed=1 << 20, name="turn", room=16)
    even = swap_pairs(masked, "narrow", N, 0)
    own = call(join, shape(768, 128), (even, masked, odd), "vvv", bytes_accessed=2 << 20, name="join", room=16)
    odd = swap_pairs(own, "wide", W, 1)
    later, planes = lax.optimization_barrier((own, planes))
    even = swap_pairs(later, "wide", W, 0)
    back = call(
        convolve, shape(1024, 128),
        (planes.reshape(1024, 128), yh, yl, green_hat.reshape(2, 512, 512)), "hhhh",
        scratch=[VMEM((1024, 128), F32)] + [VMEM((2, 256, 512), BF16)] * 2 + [VMEM((2, 512, 512), F32)]
        + [VMEM((2, 256, 256), BF16)] * 2 + [VMEM((2, 256, 512), BF16)] * 2
        + [VMEM((2, 512, 512), BF16)] * 2 + [VMEM((2, 256, 512), BF16)] * 2,
        copies=4, flops=5 * 10**9, bytes_accessed=9 << 20, name="convolve", room=63,
    )
    field = lax.all_to_all(back.reshape(256, 4, 128), BOTH, split_axis=0, concat_axis=0, tiled=True)
    index = near_source.reshape(CLASSES * 256)
    beside = call(
        near, shape(128, 256), (index, even, own, odd, near_table), "svvvv",
        scratch=[VMEM((2304, 128), F32), VMEM((CLASSES, 256, 128), F32)],
        flops=10**10, bytes_accessed=40 << 20, name="near", room=16,
    )
    result = call(
        from_grid, shape(128, 256),
        (block_count, site, field.reshape(1024, 128), projection, expand, izh, izl, beside), "svvvvvvv",
        flops=2 * 10**9, bytes_accessed=2 << 20, name="from_grid", room=12,
    )
    return result.reshape(2, 64, 256)


def solution(mesh):
    placed = (
        P(None, None, BOTH),
        P(),
        P(None, BOTH, None, None),
        P(),
        P(BOTH),
        P(BOTH),
        P(None, BOTH),
    )
    return jax.shard_map(
        per_device,
        mesh=mesh,
        in_specs=placed,
        out_specs=P(None, None, BOTH),
        check_vma=False,
    )
```

```python
import numpy as np

import jax
import jax.numpy as jnp
from jax import lax
from jax.experimental import pallas as pl
from jax.experimental.pallas import tpu as pltpu
from jax.sharding import PartitionSpec as P

W = 64
N = 4
F32 = jnp.float32
BF16 = jnp.bfloat16
VMEM = pltpu.VMEM
BOTH = ("wide", "narrow")


def halves(table):
    high = table.astype(jnp.bfloat16)
    low = (table - high.astype(np.float64)).astype(jnp.bfloat16)
    return high, low


def split(value):
    high = value.astype(BF16)
    return high, (value - high.astype(F32)).astype(BF16)


def dot(left, right):
    return lax.dot_general(left, right, (((1,), (0,)), ((), ())), preferred_element_type=F32)


def dot_t(left, right):
    return lax.dot_general(left, right, (((1,), (1,)), ((), ())), preferred_element_type=F32)


def dot3(lh, ll, rh, rl):
    return dot(lh, rh) + (dot(lh, rl) + dot(ll, rh))


def dot_l(left, right):
    return lax.dot_general(left, right, (((0,), (0,)), ((), ())), preferred_element_type=F32)


def tables():
    z = np.arange(128)
    z_of = 4 * (z % 32) + z // 32
    kz = np.arange(256)
    ang = 2 * np.pi * ((kz[:, None] * z_of[None, :]) % 256) / 256
    forward_z = np.concatenate([np.cos(ang), np.sin(ang)], 1)
    inverse_z = np.concatenate([np.cos(ang).T, -np.sin(ang).T], 1) * 2.0**-26
    lane = np.arange(2048)
    group, inner = lane // 128, lane % 128
    ez, ex = group // 4, group % 4
    r, ey = inner // 64, inner // 16 % 2 * 2 + inner // 32 % 2
    row = r * 64 + 16 * ex + 4 * ey + ez
    expand = (np.arange(128)[:, None] == row[None, :]).astype(np.float32)
    k = np.arange(256)
    i = np.arange(256)
    real = (i // 64 % 2 == 0)[:, None]
    along = []
    for p in range(2):
        y = 64 * (i // 128 * 2 + i // 32 % 2) + 4 * (i % 16) + 2 * (i // 16 % 2) + p
        ang = 2 * np.pi * ((y[:, None] * k[None, :]) % 512) / 512
        c, s = np.cos(ang), np.sin(ang)
        along.append(np.concatenate([np.where(real, c, s), np.where(real, -s, c)], 1))
    return forward_z, inverse_z, expand, np.stack(along)


def swap(value):
    lanes = value.shape[1]
    rolled = jnp.concatenate(
        [pltpu.roll(value[:, i : i + 128], 64, 1) for i in range(0, lanes, 128)], axis=1
    )
    sign = jnp.where(lax.broadcasted_iota(jnp.int32, (1, lanes), 1) % 128 < 64, 1.0, -1.0)
    return rolled * sign


def site_masks(count, site):
    rows = lax.broadcasted_iota(jnp.int32, (32, 256), 0)
    line = jnp.where(rows == site % 32, 1.0, 0.0)
    lanes = lax.broadcasted_iota(jnp.int32, (128, 256), 0)
    slots = lax.broadcasted_iota(jnp.int32, (128, 256), 1)
    plane = jnp.where((lanes % 16 == site // 32) & (slots < count), 1.0, 0.0)
    return line, plane.T


def fetch(pairs, sems):
    copies = [pltpu.make_async_copy(s, d, sems.at[i]) for i, (s, d) in enumerate(pairs)]
    for copy in copies:
        copy.start()
    return copies


def to_grid(count_ref, charges_any, site_any, proj_any, expand_any, fh_any, fl_any, out_ref, token_ref,
            charges_ref, site_ref, proj_ref, expand_ref, fh_ref, fl_ref, sems):
    copies = fetch(
        [(charges_any, charges_ref), (proj_any, proj_ref), (site_any, site_ref),
         (expand_any, expand_ref), (fh_any, fh_ref), (fl_any, fl_ref)], sems)
    token_ref[...] = jnp.zeros((8, 128), F32)
    rows = lax.broadcasted_iota(jnp.int32, (128, 256), 0)
    slots = lax.broadcasted_iota(jnp.int32, (128, 256), 1)
    for copy in copies[:3]:
        copy.wait()
    occupied = slots < count_ref[0]
    site = site_ref[...]
    plane = jnp.where((rows % 16 == site // 32) & occupied, 1.0, 0.0).astype(BF16)
    plane = jnp.concatenate([plane] * 4, axis=0)
    masked = jnp.where(occupied, charges_ref[...], 0.0)
    ph, plo = split(proj_ref[...])
    parts = []
    for r in range(2):
        mh, ml = split(masked[64 * r : 64 * r + 64])
        parts.append(dot3(ph, plo, mh, ml))
    both = jnp.concatenate(split(jnp.concatenate(parts, axis=0)), axis=1)
    copies[3].wait()
    grid = jnp.zeros((512, 128), F32)
    for ez in range(4):
        line = jnp.where((rows % 32 == site % 32) & (rows // 32 == ez), 1.0, 0.0).astype(BF16)
        spread = dot(expand_ref[512 * ez : 512 * ez + 512, :], both)
        for h in range(2):
            grid = grid + dot_t(spread[:, 256 * h : 256 * h + 256].astype(BF16) * plane, line)
    turned = []
    for ex in range(4):
        turned += [grid[128 * ex + 64 : 128 * ex + 128], -grid[128 * ex : 128 * ex + 64]]
    gh, gl = split(jnp.concatenate([grid, jnp.concatenate(turned, axis=0)], axis=1))
    copies[4].wait()
    copies[5].wait()
    fh, fl = fh_ref[...], fl_ref[...]
    for e in range(2):
        c = slice(256 * e, 256 * e + 256)
        planes = dot_t(fh, gh[c]) + (dot_t(fh, gl[c]) + dot_t(fl, gh[c]))
        out_ref[pl.ds(2 * e, 256, stride=4), :] = planes[:, :128]
        out_ref[pl.ds(2 * e + 1, 256, stride=4), :] = planes[:, 128:]


def turn(count_ref, charges_ref, *refs):
    out_ref = refs[-1]
    slots = lax.broadcasted_iota(jnp.int32, (128, 256), 1)
    out_ref[...] = jnp.where(slots < count_ref[0], charges_ref[...], 0.0).T


def join(even_ref, own_ref, odd_ref, out_ref):
    last = lax.axis_index("narrow") % 2
    out_ref[pl.ds(pl.multiple_of(512 - 512 * last, 512), 256), :] = even_ref[...]
    out_ref[256:512, :] = own_ref[...]
    out_ref[pl.ds(pl.multiple_of(512 * last, 512), 256), :] = odd_ref[...]


def convolve(in_any, th_any, tl_any, green_any, out_ref,
             in_ref, th, tl, green_ref, ah, al, sh, sl, qh, ql, bh, bl, sems):
    arrived, *copies = fetch([(in_any, in_ref), (th_any, th), (tl_any, tl), (green_any, green_ref)], sems)
    arrived.wait()
    first = lax.broadcasted_iota(jnp.int32, (64, 128), 1) % 64 < 32
    for ex in range(4):
        base = ex % 2 * 128 + ex // 2 * 16
        for m in range(2):
            c = slice(128 * m, 128 * m + 128)
            d0 = in_ref[pl.ds(8 * m + ex, 64, stride=16), :]
            d1 = in_ref[pl.ds(8 * m + 4 + ex, 64, stride=16), :]
            pieces = split(jnp.where(first, d0, pltpu.roll(d1, 32, 1))), split(jnp.where(first, pltpu.roll(d0, 96, 1), d1))
            for p, (h, l) in enumerate(pieces):
                for w in range(4):
                    a = slice(base + 32 * w, base + 32 * w + 16)
                    ah[p, a, c], al[p, a, c] = h[16 * w : 16 * w + 16], l[16 * w : 16 * w + 16]
    copies[0].wait()
    copies[1].wait()
    for r in range(2):
        c = slice(256 * r, 256 * r + 256)
        even = dot3(ah[0], al[0], th[0, :, c], tl[0, :, c])
        odd = dot3(ah[1], al[1], th[1, :, c], tl[1, :, c])
        for half, (h, l) in enumerate((split(even + odd), split(even - odd))):
            k = slice(256 * half, 256 * half + 256)
            for xp in range(2):
                for m in range(2):
                    o, a = slice(128 * m + 64 * r, 128 * m + 64 * r + 64), slice(128 * xp + 64 * m, 128 * xp + 64 * m + 64)
                    sh[xp, o, k], sl[xp, o, k] = h[a], l[a]
    copies[2].wait()
    for j in range(2):
        c = slice(256 * j, 256 * j + 256)
        part = []
        for xp in range(2):
            h, l = sh[xp, :, c], sl[xp, :, c]
            part.append(dot_l(th[xp], h) + (dot_l(th[xp], l) + dot_l(tl[xp], h)))
        sums, diffs = part[0] + part[1], part[0] - part[1]
        gr, gi = green_ref[0, 0:256, c], green_ref[1, 0:256, c]
        p_re, p_im = gr * sums[:256] - gi * sums[256:], gr * sums[256:] + gi * sums[:256]
        gr, gi = green_ref[0, 256:512, c], green_ref[1, 256:512, c]
        q_re, q_im = gr * diffs[:256] - gi * diffs[256:], gr * diffs[256:] + gi * diffs[:256]
        qh[0, 0:256, c], ql[0, 0:256, c] = split(p_re + q_re)
        qh[1, 0:256, c], ql[1, 0:256, c] = split(p_re - q_re)
        qh[0, 256:512, c], ql[0, 256:512, c] = split(p_im + q_im)
        qh[1, 256:512, c], ql[1, 256:512, c] = split(p_im - q_im)
    for xp in range(2):
        u0, u1 = [dot3(th[xp], tl[xp], qh[xp, :, c], ql[xp, :, c]) for c in (slice(0, 256), slice(256, 512))]
        for p, (h, l) in enumerate((split(u0 + u1), split(u0 - u1))):
            for r in range(2):
                for m in range(2):
                    o, a = slice(128 * m + 64 * r, 128 * m + 64 * r + 64), slice(128 * xp + 64 * m, 128 * xp + 64 * m + 64)
                    k = slice(256 * r, 256 * r + 256)
                    bh[p, a, k], bl[p, a, k] = h[o], l[o]
    even, odd = [dot_t(bh[p], th[p]) + (dot_t(bh[p], tl[p]) + dot_t(bl[p], th[p])) for p in range(2)]
    first = first[:16]
    for ex in range(4):
        base = ex % 2 * 128 + ex // 2 * 16
        for w in range(4):
            rows = slice(base + 32 * w, base + 32 * w + 16)
            for m in range(2):
                c = slice(128 * m, 128 * m + 128)
                ve, vo = even[rows, c], odd[rows, c]
                place = 256 * w + 8 * m + ex
                out_ref[pl.ds(place, 16, stride=16), :] = jnp.where(first, ve, pltpu.roll(vo, 32, 1))
                out_ref[pl.ds(place + 4, 16, stride=16), :] = jnp.where(first, pltpu.roll(ve, 96, 1), vo)


def from_grid(count_ref, site_ref, in_ref, proj_ref, expand_ref, fh_ref, fl_ref, near_ref, out_ref):
    count = count_ref[0]
    line, plane = site_masks(count, site_ref[...])
    field = jnp.concatenate([in_ref[pl.ds(ex, 256, stride=4), :] for ex in range(4)], axis=1)
    vh, vl = split(jnp.concatenate([field, swap(field)], axis=0))
    points = dot3(fh_ref[...], fl_ref[...], vh, vl)
    bh, bl = split(points)
    pick = line.T.astype(BF16)
    total = jnp.zeros((256, 128), F32)
    for ez in range(4):
        rows = slice(32 * ez, 32 * ez + 32)
        for ex in range(4):
            c = slice(128 * ex, 128 * ex + 128)
            high = (dot(pick, bh[rows, c]) * plane).astype(BF16)
            low = (dot(pick, bl[rows, c]) * plane).astype(BF16)
            lo = (ez * 4 + ex) * 128
            e = expand_ref[:, lo : lo + 128]
            total = total + (dot_t(high, e) + dot_t(low, e))
    th, tl = split(total)
    ph, plo = split(proj_ref[...])
    parts = []
    for r in range(2):
        c = slice(64 * r, 64 * r + 64)
        parts.append(dot3(th[:, c], tl[:, c], ph, plo))
    far = jnp.concatenate(parts, axis=1).T
    slots = lax.broadcasted_iota(jnp.int32, (128, 256), 1)
    out_ref[...] = far + jnp.where(slots < count, near_ref[...], 0.0)


CLASSES = 27


def near(index_ref, even_ref, own_ref, odd_ref, table_ref, out_ref, source_ref, picked):
    last = lax.axis_index("wide") % 2
    source_ref[pl.ds(pl.multiple_of(1536 - 1536 * last, 512), 768), :] = even_ref[...]
    source_ref[768:1536, :] = own_ref[...]
    source_ref[pl.ds(pl.multiple_of(1536 * last, 512), 768), :] = odd_ref[...]

    def one(k, carry):
        for b in range(256):
            i = index_ref[k * 256 + b]
            picked[k, pl.ds(b, 1), :] = source_ref[pl.ds(i, 1), :]
        return carry

    lax.fori_loop(0, CLASSES, one, 0)
    total = jnp.zeros((256, 128), F32)
    for k in range(CLASSES):
        gh, gl = split(picked[k])
        re, im = table_ref[k, 0], table_ref[k, 1]
        rows = [jnp.concatenate([re, -im], axis=1), jnp.concatenate([im, re], axis=1)]
        th, tl = split(jnp.concatenate(rows, axis=0))
        total = total + (dot_t(gh, th) + (dot_t(gh, tl) + dot_t(gl, th)))
    out_ref[...] = total.T


def call(kernel, outs, args, kinds, scratch=(), copies=0, flops=0, bytes_accessed=0, name=None, out_kind="v", room=40):
    spaces = {"s": pltpu.SMEM, "v": VMEM, "h": pltpu.HBM}
    single = not isinstance(outs, (tuple, list))
    out_spec = pl.BlockSpec(memory_space=spaces[out_kind])
    scratch = list(scratch) + ([pltpu.SemaphoreType.DMA((copies,))] if copies else [])
    return pl.pallas_call(
        kernel,
        out_shape=outs,
        in_specs=[pl.BlockSpec(memory_space=spaces[k]) for k in kinds],
        out_specs=out_spec if single else tuple(out_spec for _ in outs),
        scratch_shapes=scratch,
        compiler_params=pltpu.CompilerParams(vmem_limit_bytes=room << 20),
        cost_estimate=pl.CostEstimate(flops=flops, bytes_accessed=bytes_accessed, transcendentals=0),
        name=name,
    )(*args)


def swap_pairs(array, axis, size, first):
    pairs = [(i, i + 1) for i in range(first, size - 1, 2)]
    return lax.ppermute(array, axis, pairs + [(j, i) for i, j in pairs])


def per_device(charges, projection, green_hat, near_table, block_site, block_count, near_source):
    forward_z, inverse_z, expand, along = tables()
    fzh, fzl = halves(forward_z)
    izh, izl = halves(inverse_z)
    yh, yl = halves(along)
    expand = expand.astype(jnp.bfloat16)
    site = block_site.reshape(1, 256)
    shape = lambda *s: jax.ShapeDtypeStruct(s, F32)

    cells = charges.reshape(128, 256)
    early = call(turn, shape(256, 128), (block_count, cells), "sv", bytes_accessed=1 << 20, name="turn_early", room=16)
    odd = swap_pairs(early, "narrow", N, 1)
    sent, token = call(
        to_grid, (shape(1024, 128), shape(8, 128)), (block_count, cells, site, projection, np.ascontiguousarray(expand.T), fzh, fzl), "shhhhhh",
        scratch=[VMEM((128, 256), F32), VMEM((1, 256), jnp.int32), VMEM((64, 64), F32), VMEM((2048, 128), BF16)]
        + [VMEM((256, 256), BF16)] * 2,
        copies=6, flops=2 * 10**9, bytes_accessed=2 << 20, name="to_grid", room=63,
    )
    sent, odd = lax.optimization_barrier((sent, odd))
    planes = lax.all_to_all(sent.reshape(256, 4, 128), BOTH, split_axis=0, concat_axis=0, tiled=True)
    masked = call(turn, shape(256, 128), (block_count, cells, token), "svv", bytes_accessed=1 << 20, name="turn", room=16)
    even = swap_pairs(masked, "narrow", N, 0)
    own = call(join, shape(768, 128), (even, masked, odd), "vvv", bytes_accessed=2 << 20, name="join", room=16)
    odd = swap_pairs(own, "wide", W, 1)
    even = swap_pairs(own, "wide", W, 0)
    back = call(
        convolve, shape(1024, 128),
        (planes.reshape(1024, 128), yh, yl, green_hat.reshape(2, 512, 512)), "hhhh",
        scratch=[VMEM((1024, 128), F32)] + [VMEM((2, 256, 512), BF16)] * 2 + [VMEM((2, 512, 512), F32)]
        + [VMEM((2, 256, 256), BF16)] * 2 + [VMEM((2, 256, 512), BF16)] * 2
        + [VMEM((2, 512, 512), BF16)] * 2 + [VMEM((2, 256, 512), BF16)] * 2,
        copies=4, flops=5 * 10**9, bytes_accessed=9 << 20, name="convolve", room=63,
    )
    field = lax.all_to_all(back.reshape(256, 4, 128), BOTH, split_axis=0, concat_axis=0, tiled=True)
    index = near_source.reshape(CLASSES * 256)
    beside = call(
        near, shape(128, 256), (index, even, own, odd, near_table), "svvvv",
        scratch=[VMEM((2304, 128), F32), VMEM((CLASSES, 256, 128), F32)],
        flops=10**10, bytes_accessed=40 << 20, name="near", room=16,
    )
    result = call(
        from_grid, shape(128, 256),
        (block_count, site, field.reshape(1024, 128), projection, expand, izh, izl, beside), "svvvvvvv",
        flops=2 * 10**9, bytes_accessed=2 << 20, name="from_grid", room=12,
    )
    return result.reshape(2, 64, 256)


def solution(mesh):
    placed = (
        P(None, None, BOTH),
        P(),
        P(None, BOTH, None, None),
        P(),
        P(BOTH),
        P(BOTH),
        P(None, BOTH),
    )
    return jax.shard_map(
        per_device,
        mesh=mesh,
        in_specs=placed,
        out_specs=P(None, None, BOTH),
        check_vma=False,
    )
```

```python
import numpy as np

import jax
import jax.numpy as jnp
from jax import lax
from jax.experimental import pallas as pl
from jax.experimental.pallas import tpu as pltpu
from jax.sharding import PartitionSpec as P

W = 64
N = 4
F32 = jnp.float32
BF16 = jnp.bfloat16
VMEM = pltpu.VMEM
BOTH = ("wide", "narrow")


def halves(table):
    high = table.astype(jnp.bfloat16)
    low = (table - high.astype(np.float64)).astype(jnp.bfloat16)
    return high, low


def split(value):
    high = value.astype(BF16)
    return high, (value - high.astype(F32)).astype(BF16)


def dot(left, right):
    return lax.dot_general(left, right, (((1,), (0,)), ((), ())), preferred_element_type=F32)


def dot_t(left, right):
    return lax.dot_general(left, right, (((1,), (1,)), ((), ())), preferred_element_type=F32)


def dot3(lh, ll, rh, rl):
    return dot(lh, rh) + (dot(lh, rl) + dot(ll, rh))


def dot_l(left, right):
    return lax.dot_general(left, right, (((0,), (0,)), ((), ())), preferred_element_type=F32)


def tables():
    z = np.arange(128)
    z_of = 4 * (z % 32) + z // 32
    kz = np.arange(256)
    ang = 2 * np.pi * ((kz[:, None] * z_of[None, :]) % 256) / 256
    forward_z = np.concatenate([np.cos(ang), np.sin(ang)], 1)
    inverse_z = np.concatenate([np.cos(ang).T, -np.sin(ang).T], 1) * 2.0**-26
    lane = np.arange(2048)
    group, inner = lane // 128, lane % 128
    ez, ex = group // 4, group % 4
    r, ey = inner // 64, inner // 16 % 2 * 2 + inner // 32 % 2
    row = r * 64 + 16 * ex + 4 * ey + ez
    expand = (np.arange(128)[:, None] == row[None, :]).astype(np.float32)
    k = np.arange(256)
    i = np.arange(256)
    real = (i // 64 % 2 == 0)[:, None]
    along = []
    for p in range(2):
        y = 64 * (i // 128 * 2 + i // 32 % 2) + 4 * (i % 16) + 2 * (i // 16 % 2) + p
        ang = 2 * np.pi * ((y[:, None] * k[None, :]) % 512) / 512
        c, s = np.cos(ang), np.sin(ang)
        along.append(np.concatenate([np.where(real, c, s), np.where(real, -s, c)], 1))
    return forward_z, inverse_z, expand, np.stack(along)


def swap(value):
    lanes = value.shape[1]
    rolled = jnp.concatenate(
        [pltpu.roll(value[:, i : i + 128], 64, 1) for i in range(0, lanes, 128)], axis=1
    )
    sign = jnp.where(lax.broadcasted_iota(jnp.int32, (1, lanes), 1) % 128 < 64, 1.0, -1.0)
    return rolled * sign


def site_masks(count, site):
    rows = lax.broadcasted_iota(jnp.int32, (32, 256), 0)
    line = jnp.where(rows == site % 32, 1.0, 0.0)
    lanes = lax.broadcasted_iota(jnp.int32, (128, 256), 0)
    slots = lax.broadcasted_iota(jnp.int32, (128, 256), 1)
    plane = jnp.where((lanes % 16 == site // 32) & (slots < count), 1.0, 0.0)
    return line, plane.T


def fetch(pairs, sems):
    copies = [pltpu.make_async_copy(s, d, sems.at[i]) for i, (s, d) in enumerate(pairs)]
    for copy in copies:
        copy.start()
    return copies


def to_grid(count_ref, charges_any, site_any, proj_any, expand_any, fh_any, fl_any, out_ref, token_ref,
            charges_ref, site_ref, proj_ref, expand_ref, fh_ref, fl_ref, sems):
    copies = fetch(
        [(charges_any, charges_ref), (proj_any, proj_ref), (site_any, site_ref),
         (expand_any, expand_ref), (fh_any, fh_ref), (fl_any, fl_ref)], sems)
    token_ref[...] = jnp.zeros((8, 128), F32)
    rows = lax.broadcasted_iota(jnp.int32, (128, 256), 0)
    slots = lax.broadcasted_iota(jnp.int32, (128, 256), 1)
    for copy in copies[:3]:
        copy.wait()
    occupied = slots < count_ref[0]
    site = site_ref[...]
    plane = jnp.where((rows % 16 == site // 32) & occupied, 1.0, 0.0).astype(BF16)
    plane = jnp.concatenate([plane] * 4, axis=0)
    masked = jnp.where(occupied, charges_ref[...], 0.0)
    ph, plo = split(proj_ref[...])
    parts = []
    for r in range(2):
        mh, ml = split(masked[64 * r : 64 * r + 64])
        parts.append(dot3(ph, plo, mh, ml))
    both = jnp.concatenate(split(jnp.concatenate(parts, axis=0)), axis=1)
    copies[3].wait()
    grid = jnp.zeros((512, 128), F32)
    for ez in range(4):
        line = jnp.where((rows % 32 == site % 32) & (rows // 32 == ez), 1.0, 0.0).astype(BF16)
        spread = dot(expand_ref[512 * ez : 512 * ez + 512, :], both)
        for h in range(2):
            grid = grid + dot_t(spread[:, 256 * h : 256 * h + 256].astype(BF16) * plane, line)
    turned = []
    for ex in range(4):
        turned += [grid[128 * ex + 64 : 128 * ex + 128], -grid[128 * ex : 128 * ex + 64]]
    gh, gl = split(jnp.concatenate([grid, jnp.concatenate(turned, axis=0)], axis=1))
    copies[4].wait()
    copies[5].wait()
    fh, fl = fh_ref[...], fl_ref[...]
    for e in range(2):
        c = slice(256 * e, 256 * e + 256)
        planes = dot_t(fh, gh[c]) + (dot_t(fh, gl[c]) + dot_t(fl, gh[c]))
        out_ref[pl.ds(2 * e, 256, stride=4), :] = planes[:, :128]
        out_ref[pl.ds(2 * e + 1, 256, stride=4), :] = planes[:, 128:]


def turn(count_ref, charges_ref, *refs):
    out_ref = refs[-1]
    slots = lax.broadcasted_iota(jnp.int32, (128, 256), 1)
    out_ref[...] = jnp.where(slots < count_ref[0], charges_ref[...], 0.0).T


def join(even_ref, own_ref, odd_ref, out_ref):
    last = lax.axis_index("narrow") % 2
    out_ref[pl.ds(pl.multiple_of(512 - 512 * last, 512), 256), :] = even_ref[...]
    out_ref[256:512, :] = own_ref[...]
    out_ref[pl.ds(pl.multiple_of(512 * last, 512), 256), :] = odd_ref[...]


def convolve(in_ref, th_any, tl_any, green_any, out_ref,
             th, tl, green_ref, ah, al, sh, sl, qh, ql, bh, bl, sems):
    copies = fetch([(th_any, th), (tl_any, tl), (green_any, green_ref)], sems)
    first = lax.broadcasted_iota(jnp.int32, (64, 128), 1) % 64 < 32
    for ex in range(4):
        base = ex % 2 * 128 + ex // 2 * 16
        for m in range(2):
            c = slice(128 * m, 128 * m + 128)
            d0 = in_ref[pl.ds(8 * m + ex, 64, stride=16), :]
            d1 = in_ref[pl.ds(8 * m + 4 + ex, 64, stride=16), :]
            pieces = split(jnp.where(first, d0, pltpu.roll(d1, 32, 1))), split(jnp.where(first, pltpu.roll(d0, 96, 1), d1))
            for p, (h, l) in enumerate(pieces):
                for w in range(4):
                    a = slice(base + 32 * w, base + 32 * w + 16)
                    ah[p, a, c], al[p, a, c] = h[16 * w : 16 * w + 16], l[16 * w : 16 * w + 16]
    copies[0].wait()
    copies[1].wait()
    for r in range(2):
        c = slice(256 * r, 256 * r + 256)
        even = dot3(ah[0], al[0], th[0, :, c], tl[0, :, c])
        odd = dot3(ah[1], al[1], th[1, :, c], tl[1, :, c])
        for half, (h, l) in enumerate((split(even + odd), split(even - odd))):
            k = slice(256 * half, 256 * half + 256)
            for xp in range(2):
                for m in range(2):
                    o, a = slice(128 * m + 64 * r, 128 * m + 64 * r + 64), slice(128 * xp + 64 * m, 128 * xp + 64 * m + 64)
                    sh[xp, o, k], sl[xp, o, k] = h[a], l[a]
    copies[2].wait()
    for j in range(2):
        c = slice(256 * j, 256 * j + 256)
        part = []
        for xp in range(2):
            h, l = sh[xp, :, c], sl[xp, :, c]
            part.append(dot_l(th[xp], h) + (dot_l(th[xp], l) + dot_l(tl[xp], h)))
        sums, diffs = part[0] + part[1], part[0] - part[1]
        gr, gi = green_ref[0, 0:256, c], green_ref[1, 0:256, c]
        p_re, p_im = gr * sums[:256] - gi * sums[256:], gr * sums[256:] + gi * sums[:256]
        gr, gi = green_ref[0, 256:512, c], green_ref[1, 256:512, c]
        q_re, q_im = gr * diffs[:256] - gi * diffs[256:], gr * diffs[256:] + gi * diffs[:256]
        qh[0, 0:256, c], ql[0, 0:256, c] = split(p_re + q_re)
        qh[1, 0:256, c], ql[1, 0:256, c] = split(p_re - q_re)
        qh[0, 256:512, c], ql[0, 256:512, c] = split(p_im + q_im)
        qh[1, 256:512, c], ql[1, 256:512, c] = split(p_im - q_im)
    for xp in range(2):
        u0, u1 = [dot3(th[xp], tl[xp], qh[xp, :, c], ql[xp, :, c]) for c in (slice(0, 256), slice(256, 512))]
        for p, (h, l) in enumerate((split(u0 + u1), split(u0 - u1))):
            for r in range(2):
                for m in range(2):
                    o, a = slice(128 * m + 64 * r, 128 * m + 64 * r + 64), slice(128 * xp + 64 * m, 128 * xp + 64 * m + 64)
                    k = slice(256 * r, 256 * r + 256)
                    bh[p, a, k], bl[p, a, k] = h[o], l[o]
    even, odd = [dot_t(bh[p], th[p]) + (dot_t(bh[p], tl[p]) + dot_t(bl[p], th[p])) for p in range(2)]
    first = first[:16]
    for ex in range(4):
        base = ex % 2 * 128 + ex // 2 * 16
        for w in range(4):
            rows = slice(base + 32 * w, base + 32 * w + 16)
            for m in range(2):
                c = slice(128 * m, 128 * m + 128)
                ve, vo = even[rows, c], odd[rows, c]
                place = 256 * w + 8 * m + ex
                out_ref[pl.ds(place, 16, stride=16), :] = jnp.where(first, ve, pltpu.roll(vo, 32, 1))
                out_ref[pl.ds(place + 4, 16, stride=16), :] = jnp.where(first, pltpu.roll(ve, 96, 1), vo)


def from_grid(count_ref, site_ref, in_ref, proj_ref, expand_ref, fh_ref, fl_ref, near_ref, out_ref):
    count = count_ref[0]
    line, plane = site_masks(count, site_ref[...])
    field = jnp.concatenate([in_ref[pl.ds(ex, 256, stride=4), :] for ex in range(4)], axis=1)
    vh, vl = split(jnp.concatenate([field, swap(field)], axis=0))
    points = dot3(fh_ref[...], fl_ref[...], vh, vl)
    bh, bl = split(points)
    pick = line.T.astype(BF16)
    total = jnp.zeros((256, 128), F32)
    for ez in range(4):
        rows = slice(32 * ez, 32 * ez + 32)
        for ex in range(4):
            c = slice(128 * ex, 128 * ex + 128)
            high = (dot(pick, bh[rows, c]) * plane).astype(BF16)
            low = (dot(pick, bl[rows, c]) * plane).astype(BF16)
            lo = (ez * 4 + ex) * 128
            e = expand_ref[:, lo : lo + 128]
            total = total + (dot_t(high, e) + dot_t(low, e))
    th, tl = split(total)
    ph, plo = split(proj_ref[...])
    parts = []
    for r in range(2):
        c = slice(64 * r, 64 * r + 64)
        parts.append(dot3(th[:, c], tl[:, c], ph, plo))
    far = jnp.concatenate(parts, axis=1).T
    slots = lax.broadcasted_iota(jnp.int32, (128, 256), 1)
    out_ref[...] = far + jnp.where(slots < count, near_ref[...], 0.0)


CLASSES = 27


def near(index_ref, even_ref, own_ref, odd_ref, table_ref, out_ref, source_ref, picked):
    last = lax.axis_index("wide") % 2
    source_ref[pl.ds(pl.multiple_of(1536 - 1536 * last, 512), 768), :] = even_ref[...]
    source_ref[768:1536, :] = own_ref[...]
    source_ref[pl.ds(pl.multiple_of(1536 * last, 512), 768), :] = odd_ref[...]

    def one(k, carry):
        for b in range(256):
            i = index_ref[k * 256 + b]
            picked[k, pl.ds(b, 1), :] = source_ref[pl.ds(i, 1), :]
        return carry

    lax.fori_loop(0, CLASSES, one, 0)
    total = jnp.zeros((256, 128), F32)
    for k in range(CLASSES):
        gh, gl = split(picked[k])
        re, im = table_ref[k, 0], table_ref[k, 1]
        rows = [jnp.concatenate([re, -im], axis=1), jnp.concatenate([im, re], axis=1)]
        th, tl = split(jnp.concatenate(rows, axis=0))
        total = total + (dot_t(gh, th) + (dot_t(gh, tl) + dot_t(gl, th)))
    out_ref[...] = total.T


def call(kernel, outs, args, kinds, scratch=(), copies=0, flops=0, bytes_accessed=0, name=None, out_kind="v", room=40):
    spaces = {"s": pltpu.SMEM, "v": VMEM, "h": pltpu.HBM}
    single = not isinstance(outs, (tuple, list))
    out_spec = pl.BlockSpec(memory_space=spaces[out_kind])
    scratch = list(scratch) + ([pltpu.SemaphoreType.DMA((copies,))] if copies else [])
    return pl.pallas_call(
        kernel,
        out_shape=outs,
        in_specs=[pl.BlockSpec(memory_space=spaces[k]) for k in kinds],
        out_specs=out_spec if single else tuple(out_spec for _ in outs),
        scratch_shapes=scratch,
        compiler_params=pltpu.CompilerParams(vmem_limit_bytes=int(room * 2**20)),
        cost_estimate=pl.CostEstimate(flops=flops, bytes_accessed=bytes_accessed, transcendentals=0),
        name=name,
    )(*args)


def swap_pairs(array, axis, size, first):
    pairs = [(i, i + 1) for i in range(first, size - 1, 2)]
    return lax.ppermute(array, axis, pairs + [(j, i) for i, j in pairs])


def per_device(charges, projection, green_hat, near_table, block_site, block_count, near_source):
    forward_z, inverse_z, expand, along = tables()
    fzh, fzl = halves(forward_z)
    izh, izl = halves(inverse_z)
    yh, yl = halves(along)
    expand = expand.astype(jnp.bfloat16)
    site = block_site.reshape(1, 256)
    shape = lambda *s: jax.ShapeDtypeStruct(s, F32)

    cells = charges.reshape(128, 256)
    early = call(turn, shape(256, 128), (block_count, cells), "sv", bytes_accessed=1 << 20, name="turn_early", room=16)
    odd = swap_pairs(early, "narrow", N, 1)
    sent, token = call(
        to_grid, (shape(1024, 128), shape(8, 128)), (block_count, cells, site, projection, np.ascontiguousarray(expand.T), fzh, fzl), "shhhhhh",
        scratch=[VMEM((128, 256), F32), VMEM((1, 256), jnp.int32), VMEM((64, 64), F32), VMEM((2048, 128), BF16)]
        + [VMEM((256, 256), BF16)] * 2,
        copies=6, flops=2 * 10**9, bytes_accessed=2 << 20, name="to_grid", room=63,
    )
    sent, odd = lax.optimization_barrier((sent, odd))
    planes = lax.all_to_all(sent.reshape(256, 4, 128), BOTH, split_axis=0, concat_axis=0, tiled=True)
    masked = call(turn, shape(256, 128), (block_count, cells, token), "svv", bytes_accessed=1 << 20, name="turn", room=16)
    even = swap_pairs(masked, "narrow", N, 0)
    own = call(join, shape(768, 128), (even, masked, odd), "vvv", bytes_accessed=2 << 20, name="join", room=16)
    odd = swap_pairs(own, "wide", W, 1)
    even = swap_pairs(own, "wide", W, 0)
    back = call(
        convolve, shape(1024, 128),
        (planes.reshape(1024, 128), yh, yl, green_hat.reshape(2, 512, 512)), "vhhh",
        scratch=[VMEM((2, 256, 512), BF16)] * 2 + [VMEM((2, 512, 512), F32)]
        + [VMEM((2, 256, 256), BF16)] * 2 + [VMEM((2, 256, 512), BF16)] * 2
        + [VMEM((2, 512, 512), BF16)] * 2 + [VMEM((2, 256, 512), BF16)] * 2,
        copies=3, flops=5 * 10**9, bytes_accessed=9 << 20, name="convolve", room=52.5,
    )
    field = lax.all_to_all(back.reshape(256, 4, 128), BOTH, split_axis=0, concat_axis=0, tiled=True)
    index = near_source.reshape(CLASSES * 256)
    beside = call(
        near, shape(128, 256), (index, even, own, odd, near_table), "svvvv",
        scratch=[VMEM((2304, 128), F32), VMEM((CLASSES, 256, 128), F32)],
        flops=10**10, bytes_accessed=40 << 20, name="near", room=52.5,
    )
    result = call(
        from_grid, shape(128, 256),
        (block_count, site, field.reshape(1024, 128), projection, expand, izh, izl, beside), "svvvvvvv",
        flops=2 * 10**9, bytes_accessed=2 << 20, name="from_grid", room=52.5,
    )
    return result.reshape(2, 64, 256)


def solution(mesh):
    placed = (
        P(None, None, BOTH),
        P(),
        P(None, BOTH, None, None),
        P(),
        P(BOTH),
        P(BOTH),
        P(None, BOTH),
    )
    return jax.shard_map(
        per_device,
        mesh=mesh,
        in_specs=placed,
        out_specs=P(None, None, BOTH),
        check_vma=False,
    )
```
